128 devices in a mesh: dp: 16 (over y, x_hi, core), tensor: 8 (over x_lo, z).
Axes of the slice: x: 4 (x_hi: 2, x_lo: 2; x = x_hi * 2 + x_lo), y: 4, z: 4, core: 2. Of those that a mesh axis runs over, the one named last changes fastest.
Arguments:
- tokens: bfloat16 [16384, 2048], P(('dp', 'tensor')), may hold values from -6 to 6
- lengths: int32 [16, 8], P('dp'), may hold values from 1 to 512, 1024 in all within a row
- attn_gain: float32 [2048], replicated, may hold values from 0.5 to 1.5
- query_weight: bfloat16 [2048, 2048], P('dp', 'tensor'), may hold values from -0.125 to 0.125
- key_weight: bfloat16 [2048, 2048], P('dp', 'tensor'), may hold values from -0.125 to 0.125
- value_weight: bfloat16 [2048, 2048], P('dp', 'tensor'), may hold values from -0.125 to 0.125
- out_weight: bfloat16 [2048, 2048], P('dp', 'tensor'), may hold values from -1 to 1
- mlp_gain: float32 [2048], replicated, may hold values from 0.5 to 1.5
- gate_weight: bfloat16 [2048, 5504], P('dp', 'tensor'), may hold values from -0.125 to 0.125
- up_weight: bfloat16 [2048, 5504], P('dp', 'tensor'), may hold values from -0.125 to 0.125
- down_weight: bfloat16 [2048, 5504], P('dp', 'tensor'), may hold values from -0.078125 to 0.078125
- cotangent: bfloat16 [16384, 2048], P(('dp', 'tensor')), may hold values from -6 to 6
Outputs:
- mixed: bfloat16 [16384, 2048], P(('dp', 'tensor'))
- tokens_grad: float32 [16384, 2048], P(('dp', 'tensor'))
- attn_gain_grad: float32 [2048], replicated
- query_weight_grad: float32 [2048, 2048], P('dp', 'tensor')
- key_weight_grad: float32 [2048, 2048], P('dp', 'tensor')
- value_weight_grad: float32 [2048, 2048], P('dp', 'tensor')
- out_weight_grad: float32 [2048, 2048], P('dp', 'tensor')
- mlp_gain_grad: float32 [2048], replicated
- gate_weight_grad: float32 [2048, 5504], P('dp', 'tensor')
- up_weight_grad: float32 [2048, 5504], P('dp', 'tensor')
- down_weight_grad: float32 [2048, 5504], P('dp', 'tensor')
The draws below stay inside these ranges and needn't reach their ends.
Inputs may be any that keep to these rules, and one draw needn't show every extreme that they name: Each row holds the lengths of 8 sequences that fill one dp index's 1024 tokens in order; they sum to 1024 and the longest is exactly 512.
All inputs are finite; a program needn't handle non-finite values.
Results may differ from the reference program's by a relative error of at most 0.02.
Values may be sent and summed in bfloat16 or wider, within the bound.
A program may use at most 128 MiB of HBM per device.

```python
import math
import jax
import jax.numpy as jnp
import numpy as np
from jax import lax

D = 2048
HEADS = 16
HEAD_DIM = 128
FF = 5504
GROUP = 1024
TOKENS = 16384
SLOTS = 8
MAXLEN = 512
N_DP = 16


def level_of(stream_key, extent, shards, smallest, high):
    loudness, own = 1.0, jax.random.fold_in(stream_key, 6)
    for axis_at, blocks in shards:
        heights = jnp.exp(jax.random.uniform(jax.random.fold_in(own, axis_at), (blocks,), jnp.float32, smallest / len(shards), high / len(shards)))
        loudness = loudness * jnp.repeat(heights, extent[axis_at] // blocks).reshape([-1 if axis == axis_at else 1 for axis in range(len(extent))])
    return loudness


def split_up(number_of, total, reach, skew):
    loads = [(1 << 20) // math.isqrt(standing ** skew) + 1 for standing in range(2, number_of + 1)]
    rest, counts = total - reach - (number_of - 1), [1] * (number_of - 1)
    while rest > 0:
        movable = [i for i in range(number_of - 1) if counts[i] < reach]
        pool, budget = sum([loads[i] for i in movable]), rest
        for i in movable:
            extra = min(reach - counts[i], max(1, budget * loads[i] // pool), rest)
            counts[i] = counts[i] + extra
            rest = rest - extra
    return np.array([reach] + counts)


def uneven(stream_key, count, total, limit, lean):
    if count == 2:
        one = jax.random.randint(stream_key, (), max(1, total - limit), min(limit, total - 1) + 1)
        return jnp.stack([one, total - one])
    sizes = jnp.asarray(split_up(count, total, limit, lean), jnp.int32)
    couples = (count - 1) // 2
    giver, taker = sizes[1:1 + 2 * couples:2], sizes[2:2 + 2 * couples:2]
    margin = jnp.minimum(giver - 1, limit - taker)
    moved = jax.random.randint(jax.random.fold_in(stream_key, 1), (couples,), 0, 1 << 20) % (margin + 1)
    sizes = sizes.at[1:1 + 2 * couples:2].set(giver - moved).at[2:2 + 2 * couples:2].set(taker + moved)
    return sizes[jax.random.permutation(jax.random.fold_in(stream_key, 2), count)]


def bell_draw(stream_key, dims, deviation, limit, split=(), kind=jnp.bfloat16):
    values = deviation * jax.random.normal(stream_key, dims, jnp.float32)
    if split:
        values = values * level_of(stream_key, dims, split, -0.22, 0.18)
    return jnp.clip(values, -limit, limit).astype(kind)


def setup_inputs(seed: int = 0) -> dict:
    seeds = jax.random.split(jax.random.key(seed), 13)
    return {
        "tokens": bell_draw(seeds[0], (TOKENS, D), 1.0, 6.0, ((0, 128),)),
        "lengths": jax.vmap(lambda own: uneven(own, SLOTS, GROUP, MAXLEN, 2))(jax.random.split(seeds[1], N_DP)).reshape((N_DP, SLOTS)).astype(jnp.int32),
        "attn_gain": jnp.clip(1.0 + 0.1 * jax.random.normal(seeds[2], (D,), jnp.float32), 0.5, 1.5),
        "query_weight": bell_draw(seeds[3], (D, D), D ** -0.5, 0.125, ((0, 16), (1, 8))),
        "key_weight": bell_draw(seeds[4], (D, D), D ** -0.5, 0.125, ((0, 16), (1, 8))),
        "value_weight": bell_draw(seeds[5], (D, D), D ** -0.5, 0.125, ((0, 16), (1, 8))),
        "out_weight": bell_draw(seeds[6], (D, D), (D // 64) ** -0.5, 1.0, ((0, 16), (1, 8))),
        "mlp_gain": jnp.clip(1.0 + 0.1 * jax.random.normal(seeds[7], (D,), jnp.float32), 0.5, 1.5),
        "gate_weight": bell_draw(seeds[8], (D, FF), D ** -0.5, 0.125, ((0, 16), (1, 8))),
        "up_weight": bell_draw(seeds[9], (D, FF), D ** -0.5, 0.125, ((0, 16), (1, 8))),
        "down_weight": bell_draw(seeds[10], (D, FF), FF ** -0.5, 0.078125, ((0, 16), (1, 8))),
        "cotangent": bell_draw(seeds[11], (TOKENS, D), 1.0, 6.0, ((0, 128),)),
    }


EPS = 1e-05
THETA = 10000.0
HIGH = lax.Precision.HIGHEST

@jax.custom_vjp
def low(v):
    return lax.optimization_barrier(v.astype(jnp.bfloat16)).astype(jnp.float32)

@jax.custom_vjp
def low_back(v):
    return v

def low_keep(v):
    return (low(v), None)

def low_pass(kept, grad):
    return (grad,)

def back_keep(v):
    return (v, None)

def back_low(kept, grad):
    return (low(grad),)
low.defvjp(low_keep, low_pass)
low_back.defvjp(back_keep, back_low)

def places(lengths_row, group_rows):
    seq_ends = jnp.cumsum(lengths_row).astype(jnp.int32)
    indices = jnp.arange(group_rows, dtype=jnp.int32)
    passed = indices[:, None] >= seq_ends[None, :]
    segment = lax.optimization_barrier(jnp.sum(passed.astype(jnp.int32), axis=1)).astype(jnp.int32)
    seq_start = lax.optimization_barrier(jnp.sum(jnp.where(passed, lengths_row[None, :], 0), axis=1)).astype(jnp.int32)
    return (segment, (indices - seq_start).astype(jnp.int32))

def rotary(position, head_width):
    half_width = head_width // 2
    rates = THETA ** (-(jnp.arange(half_width, dtype=jnp.float32) * 2.0 / head_width))
    angles = position.astype(jnp.float32)[:, None] * rates[None, :]
    rot_cos = jnp.cos(angles)
    rot_sin = jnp.sin(angles)
    return (jnp.concatenate([rot_cos, rot_cos], 1), jnp.concatenate([rot_sin, rot_sin], 1))

def rotate(vector, rot_cos, rot_sin):
    half_width = vector.shape[-1] // 2
    turned = jnp.concatenate([-vector[..., half_width:], vector[..., :half_width]], -1)
    return vector * rot_cos[:, None, :] + turned * rot_sin[:, None, :]

def rms_norm(vector, gain_row):
    return vector * lax.rsqrt(lax.optimization_barrier(jnp.mean(vector * vector, axis=-1, keepdims=True)) + EPS) * gain_row

def matmul(left, right):
    return jnp.dot(left, right, precision=HIGH, preferred_element_type=jnp.float32)

def attend(packed):
    queries, key_rows, value_rows, segment = packed
    group_rows = queries.shape[0]
    scores = jnp.einsum('qhd,khd->hqk', queries, key_rows, precision=HIGH) * HEAD_DIM ** (-0.5)
    scores = low_back(scores)
    indices = jnp.arange(group_rows)
    allowed = (segment[:, None] == segment[None, :]) & (indices[None, :] <= indices[:, None])
    scores = jnp.where(allowed[None], scores, -1e+30)
    weights = low(jax.nn.softmax(scores, axis=-1))
    return jnp.einsum('hqk,khd->qhd', weights, value_rows, precision=HIGH)

def block_layer(stream, gain_one, w_query, w_key, w_value, w_out, gain_two, w_gate, w_up, w_down, rot_cos, rot_sin, segment):
    total_rows = stream.shape[0]
    shape_heads = (total_rows, HEADS, HEAD_DIM)
    normed = low(rms_norm(stream, gain_one))
    query_pre = low_back(matmul(normed, w_query)).reshape(shape_heads)
    key_pre = low_back(matmul(normed, w_key)).reshape(shape_heads)
    value_rows = low(low_back(matmul(normed, w_value))).reshape(shape_heads)
    queries = low(rotate(query_pre, rot_cos, rot_sin))
    key_rows = low(rotate(key_pre, rot_cos, rot_sin))
    batches = total_rows // GROUP
    grouped = (GROUP, HEADS, HEAD_DIM)
    attended = lax.map(jax.checkpoint(attend), (queries.reshape((batches,) + grouped), key_rows.reshape((batches,) + grouped), value_rows.reshape((batches,) + grouped), segment.reshape(batches, GROUP)))
    attn_out = low(low_back(attended.reshape(total_rows, D)))
    branch = low_back(jnp.dot(attn_out, w_out.T, precision=HIGH, preferred_element_type=jnp.float32))
    hidden_res = stream + branch
    normed_two = low(rms_norm(hidden_res, gain_two))
    gate = low_back(matmul(normed_two, w_gate))
    up_part = low_back(matmul(normed_two, w_up))
    inner = low(jax.nn.silu(gate) * up_part)
    mlp_out = low_back(jnp.dot(inner, w_down.T, precision=HIGH, preferred_element_type=jnp.float32))
    return hidden_res + mlp_out

def reference(tokens, lengths, attn_gain, query_weight, key_weight, value_weight, out_weight, mlp_gain, gate_weight, up_weight, down_weight, cotangent):
    segment, position = jax.vmap(lambda lengths_row: places(lengths_row, GROUP))(lengths)
    segment = segment.reshape(-1)
    rot_cos, rot_sin = rotary(position.reshape(-1), HEAD_DIM)
    floats = [arr.astype(jnp.float32) for arr in (tokens, attn_gain, query_weight, key_weight, value_weight, out_weight, mlp_gain, gate_weight, up_weight, down_weight)]

    def forward(stream, gain_one, w_query, w_key, w_value, w_out, gain_two, w_gate, w_up, w_down):
        return block_layer(stream, gain_one, w_query, w_key, w_value, w_out, gain_two, w_gate, w_up, w_down, rot_cos, rot_sin, segment)
    result, pullback = jax.vjp(forward, *floats)
    grads = pullback(cotangent.astype(jnp.float32))
    return (result.astype(jnp.bfloat16), grads[0], grads[1], grads[2], grads[3], grads[4], grads[5], grads[6], grads[7], grads[8], grads[9])
```

```python
import functools

import jax
import jax.numpy as jnp
from jax import lax
from jax.experimental import pallas as pl
from jax.experimental.pallas import tpu as pltpu
from jax.sharding import PartitionSpec as P

HEAD_DIM = 128
QBLOCK = 512
EPS = 1e-05
THETA = 10000.0
D = 2048
ROWS = 128
GROUP = 1024
FFB = 688
CUT = 352
MESH = pl.DeviceIdType.MESH
ANY = pl.BlockSpec(memory_space=pl.ANY)
VMEM = pl.BlockSpec(memory_space=pltpu.VMEM)


class Net:
    def __init__(self, send_sems, recv_sems):
        dp, t = lax.axis_index("dp"), lax.axis_index("tensor")
        self.y, self.c = lax.div(dp, 4), lax.rem(dp, 2)
        self.xl, self.z = lax.div(t, 4), lax.rem(t, 4)
        self.x = lax.rem(lax.div(dp, 2), 2) * 2 + self.xl
        self.dp, self.t = dp, t
        self.send_sems, self.recv_sems = send_sems, recv_sems
        self.used = 0
        self.sent = []

    def device(self, dx=0, dy=0, dz=0, dc=0):
        x, y = lax.rem(self.x + dx + 4, 4), lax.rem(self.y + dy + 4, 4)
        z, c = lax.rem(self.z + dz + 4, 4), lax.rem(self.c + dc, 2)
        return (y * 4 + lax.div(x, 2) * 2 + c, lax.rem(x, 2) * 4 + z)

    @property
    def beside(self):
        return (self.dp, (1 - self.xl) * 4 + self.z)

    @property
    def across(self):
        return self.device(dx=2)

    def along(self, first):
        on_x = self.c == (0 if first else 1)
        both = []
        for step in (1, -1):
            by_x, by_y = self.device(dx=step), self.device(dy=step)
            both.append(tuple(jnp.where(on_x, u, v) for u, v in zip(by_x, by_y)))
        return both

    def send(self, src, dst, to):
        k = self.used
        self.used += 1
        copy = pltpu.make_async_remote_copy(
            src_ref=src,
            dst_ref=dst,
            send_sem=self.send_sems.at[k],
            recv_sem=self.recv_sems.at[k],
            device_id=to,
            device_id_type=MESH,
        )
        copy.start()
        self.sent.append(copy)
        return copy

    def finish(self):
        for copy in self.sent:
            copy.wait_send()

    def greet(self, devices):
        barrier = pltpu.get_barrier_semaphore()
        for device in devices:
            pl.semaphore_signal(barrier, inc=1, device_id=device, device_id_type=MESH)
        pl.semaphore_wait(barrier, len(devices))


def take_turns(chains, order):
    for name in order:
        next(chains[name], None)
    for chain in chains.values():
        for _ in chain:
            pass


def block(z):
    return pl.ds(pl.multiple_of(lax.rem(z + 8, 4) * ROWS, ROWS), ROWS)


def half(z, k):
    return pl.ds(pl.multiple_of(lax.rem(z + 8, 4) * ROWS + k * 64, 64), 64)


def block8(xl, z):
    return pl.ds(pl.multiple_of((xl * 4 + lax.rem(z + 8, 4)) * ROWS, ROWS), ROWS)


def half8(xl, z, k):
    return pl.ds(pl.multiple_of((xl * 4 + lax.rem(z + 8, 4)) * ROWS + k * 64, 64), 64)


def add_rows(rows, dst, *terms):
    def step(i, _):
        at = pl.ds(pl.multiple_of(i * 16, 16), 16)
        total = terms[0][at, :].astype(jnp.float32)
        for term in terms[1:]:
            total = total + term[at, :].astype(jnp.float32)
        dst[at, :] = total.astype(dst.dtype)
        return 0

    lax.fori_loop(0, rows // 16, step, 0)


def gather_z(net, own, dst):
    up, down = net.device(dz=1), net.device(dz=-1)
    z = net.z
    a0 = net.send(own, dst.at[block(z), :], up)
    a1 = net.send(own, dst.at[block(z), :], down)
    yield
    a0.wait_recv()
    b0 = net.send(dst.at[half(z - 1, 0), :], dst.at[half(z - 1, 0), :], up)
    a1.wait_recv()
    b1 = net.send(dst.at[half(z + 1, 1), :], dst.at[half(z + 1, 1), :], down)
    yield
    b0.wait_recv()
    b1.wait_recv()


def gather_8(net, own, dst):
    up, down, beside = net.device(dz=1), net.device(dz=-1), net.beside
    xl, z = net.xl, net.z
    place = dst.at[block8(xl, z), :]
    s0 = net.send(own, place, up)
    s1 = net.send(own, place, down)
    s2 = net.send(own, place, beside)
    yield
    s0.wait_recv()
    ref = dst.at[half8(xl, z - 1, 0), :]
    s5 = net.send(ref, ref, up)
    s1.wait_recv()
    ref = dst.at[half8(xl, z + 1, 1), :]
    s6 = net.send(ref, ref, down)
    s2.wait_recv()
    ref = dst.at[block8(1 - xl, z), :]
    s3 = net.send(ref, ref, up)
    s4 = net.send(ref, ref, down)
    yield
    s5.wait_recv()
    s6.wait_recv()
    ref = dst.at[block8(xl, z + 2), :]
    s7 = net.send(ref, ref, beside)
    yield
    s3.wait_recv()
    s4.wait_recv()
    s7.wait_recv()


def reduce_z(net, part, sums, got, out):
    up, down = net.device(dz=1), net.device(dz=-1)
    z = net.z
    c0 = net.send(part.at[half(z + 2, 0), :], got.at[0], up)
    c1 = net.send(part.at[half(z + 2, 1), :], got.at[1], down)
    d1 = net.send(part.at[half(z + 1, 1), :], got.at[3], up)
    d2 = net.send(part.at[half(z - 1, 0), :], got.at[4], down)
    yield
    c0.wait_recv()
    add_rows(64, sums.at[0], part.at[half(z + 1, 0), :], got.at[0])
    d0 = net.send(sums.at[0], got.at[2], up)
    c1.wait_recv()
    add_rows(64, sums.at[1], part.at[half(z - 1, 1), :], got.at[1])
    d3 = net.send(sums.at[1], got.at[5], down)
    yield
    for copy in (d0, d1, d2, d3):
        copy.wait_recv()
    out.append(lambda at, k: part[pl.ds(pl.multiple_of(net.z * ROWS + at, 16), 16), :].astype(jnp.float32)
               + got[2 + k, pl.ds(pl.multiple_of(at - 64 * k, 16), 16), :].astype(jnp.float32)
               + got[4 + k, pl.ds(pl.multiple_of(at - 64 * k, 16), 16), :].astype(jnp.float32))


def reduce_8(net, part, sums, got, sums_half, got_half, out):
    up, down, beside = net.device(dz=1), net.device(dz=-1), net.beside
    xl, z = net.xl, net.z
    a = net.send(part.at[block8(1 - xl, z + 2), :], got.at[0], beside)
    b0 = net.send(part.at[block8(1 - xl, z + 1), :], got.at[1], up)
    b1 = net.send(part.at[block8(1 - xl, z - 1), :], got.at[2], down)
    d1 = net.send(part.at[half8(xl, z + 1, 1), :], got_half.at[3], up)
    d2 = net.send(part.at[half8(xl, z - 1, 0), :], got_half.at[4], down)
    yield
    a.wait_recv()
    add_rows(128, sums.at[0], part.at[block8(xl, z + 2), :], got.at[0])
    c0 = net.send(sums.at[0, pl.ds(0, 64), :], got_half.at[0], up)
    c1 = net.send(sums.at[0, pl.ds(64, 64), :], got_half.at[1], down)
    yield
    b0.wait_recv()
    b1.wait_recv()
    add_rows(128, sums.at[1], part.at[block8(1 - xl, z), :], got.at[1], got.at[2])
    e = net.send(sums.at[1], got.at[3], beside)
    yield
    c0.wait_recv()
    add_rows(64, sums_half.at[0], part.at[half8(xl, z + 1, 0), :], got_half.at[0])
    d0 = net.send(sums_half.at[0], got_half.at[2], up)
    c1.wait_recv()
    add_rows(64, sums_half.at[1], part.at[half8(xl, z - 1, 1), :], got_half.at[1])
    d3 = net.send(sums_half.at[1], got_half.at[5], down)
    yield
    for copy in (e, d0, d1, d2, d3):
        copy.wait_recv()

    def rows(at, k):
        here = pl.ds(pl.multiple_of(at - 64 * k, 16), 16)
        total = part[pl.ds(pl.multiple_of(net.t * ROWS + at, 16), 16), :].astype(jnp.float32)
        total = total + got[3, pl.ds(pl.multiple_of(at, 16), 16), :].astype(jnp.float32)
        return total + got_half[2 + k, here, :].astype(jnp.float32) + got_half[4 + k, here, :].astype(jnp.float32)

    out.append(rows)


def each_half(step):
    for k in (0, 1):
        def body(i, _, k=k):
            step(pl.multiple_of(k * 64 + i * 16, 16), k)
            return 0

        lax.fori_loop(0, 4, body, 0)


def gather_plane(net, slab, cut, first, second):
    low, high = cut
    sib = net.device(dc=1)
    second_up, second_down = second

    def share(i, j):
        ref = slab(i, j)
        return net.send(ref, ref, sib)

    def go(i):
        ref = slab(i, 0)
        return net.send(ref, ref, second_up), net.send(ref, ref, second_down)

    shared = []
    own = slab(0, 0)
    ring = len(first) == 2
    if ring:
        a0, a1 = net.send(own, own, first[0]), net.send(own, own, first[1])
    else:
        a0 = net.send(own, own, first[0])
    sent = {0: go(0)}
    shared.append(share(0, 0))
    yield
    if ring:
        a0.wait_recv()
        ref = low(slab(-1, 0))
        f0 = net.send(ref, ref, first[0])
        a1.wait_recv()
        ref = high(slab(1, 0))
        f1 = net.send(ref, ref, first[1])
        for i in (-1, 1):
            sent[i] = go(i)
            shared.append(share(i, 0))
        yield
        f0.wait_recv()
        f1.wait_recv()
        sent[2] = go(2)
        shared.append(share(2, 0))
    else:
        a0.wait_recv()
        sent[1] = go(1)
        shared.append(share(1, 0))
    halves = {}
    for i in sent:
        yield
        sent[i][0].wait_recv()
        ref = low(slab(i, -1))
        h0 = net.send(ref, ref, second_up)
        shared.append(share(i, -1))
        sent[i][1].wait_recv()
        ref = high(slab(i, 1))
        h1 = net.send(ref, ref, second_down)
        shared.append(share(i, 1))
        halves[i] = (h0, h1)
    for i in sent:
        yield
        halves[i][0].wait_recv()
        halves[i][1].wait_recv()
        shared.append(share(i, 2))
    yield
    for copy in shared:
        copy.wait_recv()


def reduce_plane(net, mine, other, from_sib, got_half, got_up, got_down, last_bufs, cut, add, first, second):
    low, high = cut
    sib = net.device(dc=1)
    up, down = second
    ring = len(first) == 2
    steps = (0, 1, 3, 2) if ring else (0, 1)
    shared = {}
    for j in (2, 1, 3, 0):
        for i in steps:
            shared[i, j] = net.send(other(i, j), from_sib(i, j), sib)
    yield
    halves, full = {}, {}
    for i in steps:
        shared[i, 2].wait_recv()
        add(None, mine(i, 2), from_sib(i, 2))
        halves[i] = (
            net.send(low(mine(i, 2)), low(got_half(i)), up),
            net.send(high(mine(i, 2)), high(got_half(i)), down),
        )
        yield
    for i in steps:
        for j in (1, 3):
            shared[i, j].wait_recv()
            add(None, mine(i, j), from_sib(i, j))
        halves[i][0].wait_recv()
        add(0, mine(i, 1), got_half(i))
        u = net.send(mine(i, 1), got_up(i), up)
        halves[i][1].wait_recv()
        add(1, mine(i, 3), got_half(i))
        full[i] = (u, net.send(mine(i, 3), got_down(i), down))
        yield
    last = {}
    for i in reversed(steps):
        shared[i, 0].wait_recv()
        full[i][0].wait_recv()
        full[i][1].wait_recv()
        add(None, mine(i, 0), from_sib(i, 0), got_up(i), got_down(i))
        if ring and i == 2:
            ref, to = mine(2, 0), last_bufs(2)
            last[2] = (net.send(low(ref), low(to), first[0]), net.send(high(ref), high(to), first[1]))
        if ring and i == 3:
            last[2][1].wait_recv()
            add(1, mine(3, 0), last_bufs(2))
            last[3] = net.send(mine(3, 0), last_bufs(1), first[1])
        if ring and i == 1:
            last[2][0].wait_recv()
            add(0, mine(1, 0), last_bufs(2))
        if i == 1:
            last[1] = net.send(mine(1, 0), last_bufs(0), first[0])
        yield
    last[1].wait_recv()
    if ring:
        last[3].wait_recv()
        add(None, mine(0, 0), last_bufs(0), last_bufs(1))
    else:
        add(None, mine(0, 0), last_bufs(0))


PIECES = {None: ((0, 176), (176, 176), (352, 176), (528, 160)), 0: ((0, 176), (176, 176)), 1: ((352, 176), (528, 160))}


def add_slab(part, dst, *terms):
    def step(m, _):
        for at, n in PIECES[part]:
            total = dst[m, at : at + n, :].astype(jnp.float32)
            for term in terms:
                total = total + term[m, at : at + n, :].astype(jnp.float32)
            dst[m, at : at + n, :] = total.astype(dst.dtype)
        return 0

    lax.fori_loop(0, 3, step, 0)


FF_CUT = (lambda ref: ref.at[:, pl.ds(0, CUT), :], lambda ref: ref.at[:, pl.ds(CUT, FFB - CUT), :])


def ff_slab(net, ref, kind, i, j):
    x = lax.rem(net.x + jnp.where(kind == 0, i, j) + 4, 4)
    y = lax.rem(net.y + jnp.where(kind == 0, j, i) + 4, 4)
    at = pl.ds(pl.multiple_of((y * 4 + lax.div(x, 2) * 2 + kind) * 128, 128), 128)
    return ref.at[:, lax.rem(x, 2), :, at]


def mlp_in_kernel(a_part, tok, gain, wg, wu, wd, w_all, n2_all, h1, n2, sums, got, sums_half, got_half, send_sems, recv_sems, sems):
    net = Net(send_sems, recv_sems)
    xy = [net.device(dx=1), net.device(dx=-1), net.device(dy=1), net.device(dy=-1)]
    own = ff_slab(net, w_all, net.c, 0, 0)
    copies = [pltpu.make_async_copy(w, own.at[k], sems.at[k]) for k, w in enumerate((wg, wu, wd))]
    for copy in copies:
        copy.start()
    net.greet(xy + [net.device(dz=1), net.device(dz=-1), net.device(dc=1)])

    def tokens():
        out = []
        yield from reduce_8(net, a_part, sums, got, sums_half, got_half, out)

        def step(at, k):
            here = pl.ds(at, 16)
            h = tok[here, :].astype(jnp.float32) + out[0](at, k)
            h1[here, :] = h
            r = lax.rsqrt(jnp.mean(h * h, axis=-1, keepdims=True) + EPS)
            n2[here, :] = (h * r * gain[...]).astype(jnp.bfloat16)

        each_half(step)
        place = pltpu.make_async_copy(n2, n2_all.at[block(net.z), :], sems.at[3])
        place.start()
        yield from gather_z(net, n2, n2_all)
        place.wait()

    def weights():
        for copy in copies:
            copy.wait()
        slab = functools.partial(ff_slab, net, w_all, net.c)
        yield from gather_plane(net, slab, FF_CUT, net.along(True), net.along(False))

    take_turns({"t": tokens(), "w": weights()}, "twwttwtwtwwtwwww")
    net.finish()


def mlp_in(a_part, tok, gain, wg, wu, wd):
    return pl.pallas_call(
        mlp_in_kernel,
        name="mlp_in",
        out_shape=(
            jax.ShapeDtypeStruct((3, 2, FFB, D), jnp.bfloat16),
            jax.ShapeDtypeStruct((4 * ROWS, D), jnp.bfloat16),
            jax.ShapeDtypeStruct((ROWS, D), jnp.float32),
        ),
        in_specs=[VMEM, VMEM, VMEM, ANY, ANY, ANY],
        out_specs=(ANY, ANY, VMEM),
        scratch_shapes=[
            pltpu.VMEM((ROWS, D), jnp.bfloat16),
            pltpu.VMEM((2, ROWS, D), jnp.bfloat16),
            pltpu.VMEM((4, ROWS, D), jnp.bfloat16),
            pltpu.VMEM((2, 64, D), jnp.bfloat16),
            pltpu.VMEM((6, 64, D), jnp.bfloat16),
            pltpu.SemaphoreType.DMA((64,)),
            pltpu.SemaphoreType.DMA((64,)),
            pltpu.SemaphoreType.DMA((4,)),
        ],
        compiler_params=pltpu.CompilerParams(collective_id=1, has_side_effects=True, vmem_limit_bytes=56 << 20),
    )(a_part, tok, gain, wg, wu, wd)


NT = (((1,), (1,)), ((), ()))
TILES = ((0, 256), (256, 256), (512, 176))


def mlp_kernel(w_all, n2_all, g_all, m_out, dn_out, grads, w, n2, g, hid, dgate, dup, turned, stage, sems, out_sems):
    copies = [
        pltpu.make_async_copy(n2_all, n2, sems.at[0]),
        pltpu.make_async_copy(g_all, g, sems.at[1]),
    ]
    loads = [pltpu.make_async_copy(w_all.at[m, b], w.at[m, b], sems.at[2 + m * 2 + b]) for m in range(3) for b in range(2)]
    for copy in copies + loads:
        copy.start()
    for copy in copies + loads:
        copy.wait()

    def ahead(b, _):
        for at, n in TILES:
            gate = lax.dot_general(n2[...], w[0, b, at : at + n, :], NT, preferred_element_type=jnp.float32)
            up = lax.dot_general(n2[...], w[1, b, at : at + n, :], NT, preferred_element_type=jnp.float32)
            dh = lax.dot_general(g[...], w[2, b, at : at + n, :], NT, preferred_element_type=jnp.float32)
            sig = jax.nn.sigmoid(gate)
            act = gate * sig
            for k, (dst, value) in enumerate(
                ((dgate, dh * up * sig * (1.0 + gate * (1.0 - sig))), (dup, dh * act), (hid, act * up))
            ):
                value = value.astype(jnp.bfloat16)
                dst[b, :, at : at + n] = value
                turned[k, b, at : at + n, :] = value.T
        return 0

    lax.fori_loop(0, 2, ahead, 0)

    def back(i, _):
        at = pl.ds(pl.multiple_of(i * 256, 256), 256)
        m = jnp.dot(hid[0], w[2, 0, :, at], preferred_element_type=jnp.float32)
        m = m + jnp.dot(hid[1], w[2, 1, :, at], preferred_element_type=jnp.float32)
        m_out[:, at] = m.astype(jnp.bfloat16)
        d = jnp.dot(dgate[0], w[0, 0, :, at], preferred_element_type=jnp.float32)
        d = d + jnp.dot(dgate[1], w[0, 1, :, at], preferred_element_type=jnp.float32)
        d = d + jnp.dot(dup[0], w[1, 0, :, at], preferred_element_type=jnp.float32)
        d = d + jnp.dot(dup[1], w[1, 1, :, at], preferred_element_type=jnp.float32)
        dn_out[:, at] = d.astype(jnp.bfloat16)
        return 0

    lax.fori_loop(0, 8, back, 0)

    def put(i, m, b, slot):
        at = pl.ds(pl.multiple_of(i * 256, 256), 256)
        return pltpu.make_async_copy(stage.at[slot], grads.at[m, b, :, at], out_sems.at[slot])

    def outer(i, _):
        at = pl.ds(pl.multiple_of(i * 256, 256), 256)
        for m in range(3):
            right = (n2, n2, g)[m][:, at]
            for b in range(2):
                slot = m * 2 + b
                pl.when(i > 0)(lambda: put(i - 1, m, b, slot).wait())
                stage[slot] = jnp.dot(turned[m, b], right, preferred_element_type=jnp.float32).astype(jnp.bfloat16)
                put(i, m, b, slot).start()
        return 0

    lax.fori_loop(0, 8, outer, 0)
    for m in range(3):
        for b in range(2):
            put(7, m, b, m * 2 + b).wait()


def mlp(w_all, n2_all, g_all):
    bf = jnp.bfloat16
    return pl.pallas_call(
        mlp_kernel,
        name="mlp",
        out_shape=(
            jax.ShapeDtypeStruct((512, D), bf),
            jax.ShapeDtypeStruct((512, D), bf),
            jax.ShapeDtypeStruct((3, 2, FFB, D), bf),
        ),
        in_specs=[ANY] * 3,
        out_specs=(VMEM, VMEM, ANY),
        scratch_shapes=[
            pltpu.VMEM((3, 2, FFB, D), bf),
            pltpu.VMEM((512, D), bf),
            pltpu.VMEM((512, D), bf),
            pltpu.VMEM((2, 512, FFB), bf),
            pltpu.VMEM((2, 512, FFB), bf),
            pltpu.VMEM((2, 512, FFB), bf),
            pltpu.VMEM((3, 2, FFB, 512), bf),
            pltpu.VMEM((6, FFB, 256), bf),
            pltpu.SemaphoreType.DMA((8,)),
            pltpu.SemaphoreType.DMA((6,)),
        ],
        compiler_params=pltpu.CompilerParams(vmem_limit_bytes=58 << 20),
        cost_estimate=pl.CostEstimate(flops=26 * 10**9, bytes_accessed=40 << 20, transcendentals=704512),
    )(w_all, n2_all, g_all)


def mlp_out_kernel(m_part, dn_part, grads, h1, gain, cot, mixed, dh1, da_all, gain_part, wg, wu, wd,
                   da, sums_m, got_m, sums_d, got_d, mine, sib, got_half, got_up, got_down, last, send_sems, recv_sems, sems):
    net = Net(send_sems, recv_sems)
    xy = [net.device(dx=1), net.device(dx=-1), net.device(dy=1), net.device(dy=-1)]
    order = [(i, j) for j in (2, 1, 3, 0) for i in (0, 1, 3, 2)]
    loads = {}
    for k, (i, j) in enumerate(order):
        loads[i, j] = pltpu.make_async_copy(ff_slab(net, grads, net.c, i, j), mine.at[i, j], sems.at[k])
        loads[i, j].start()
    net.greet(xy + [net.device(dz=1), net.device(dz=-1), net.device(dc=1)])

    def tokens():
        out = []
        yield from reduce_z(net, dn_part, sums_d, got_d, out)

        def step(at, k, total):
            here = pl.ds(at, 16)
            h = h1[here, :]
            r = lax.rsqrt(jnp.mean(h * h, axis=-1, keepdims=True) + EPS)
            d = out[0](at, k)
            inner = d * gain[...]
            grad = r * inner - h * (r * r * r) * jnp.mean(h * inner, axis=-1, keepdims=True)
            grad = cot[here, :].astype(jnp.float32) + grad
            dh1[here, :] = grad
            da[here, :] = grad.astype(jnp.bfloat16)
            gain_part[...] += jnp.sum(d * h * r, axis=0, keepdims=True)

        gain_part[...] = jnp.zeros_like(gain_part)
        each_half(lambda at, k: step(at, k, None))
        place = pltpu.make_async_copy(da, da_all.at[block8(net.xl, net.z), :], sems.at[16])
        place.start()
        yield from gather_8(net, da, da_all)
        place.wait()

    def forward():
        out = []
        yield from reduce_z(net, m_part, sums_m, got_m, out)

        def step(at, k):
            here = pl.ds(at, 16)
            mixed[here, :] = (h1[here, :] + out[0](at, k)).astype(jnp.bfloat16)

        each_half(step)

    def weights():
        waited = set()

        def add(part, dst, *terms):
            add_slab(part, dst, *terms)

        def slot(ref):
            return lambda i, j: ref.at[i, j]

        sib_kind = 1 - net.c
        for copy in loads.values():
            copy.wait()
        yield from reduce_plane(
            net, slot(mine), functools.partial(ff_slab, net, grads, sib_kind), slot(sib),
            lambda i: got_half.at[i], lambda i: got_up.at[i], lambda i: got_down.at[i], lambda i: last.at[i],
            FF_CUT, add, net.along(True), net.along(False),
        )
        for k, dst in enumerate((wg, wu, wd)):
            for at, n in PIECES[None]:
                dst[at : at + n, :] = mine[0, 0, k, at : at + n, :].astype(jnp.float32)

    take_turns({"t": tokens(), "m": forward(), "w": weights()}, "twwwwtwmwwtwwtwwtwww")
    net.finish()


def mlp_out(m_part, dn_part, grads, h1, gain, cot):
    bf, f32 = jnp.bfloat16, jnp.float32
    slab = (3, FFB, 128)
    return pl.pallas_call(
        mlp_out_kernel,
        name="mlp_out",
        out_shape=(
            jax.ShapeDtypeStruct((ROWS, D), bf),
            jax.ShapeDtypeStruct((ROWS, D), f32),
            jax.ShapeDtypeStruct((GROUP, D), bf),
            jax.ShapeDtypeStruct((1, D), f32),
        ) + (jax.ShapeDtypeStruct((FFB, 128), f32),) * 3,
        in_specs=[VMEM, VMEM, ANY, VMEM, VMEM, VMEM],
        out_specs=(VMEM, VMEM, ANY, VMEM, VMEM, VMEM, VMEM),
        scratch_shapes=[
            pltpu.VMEM((ROWS, D), bf),
            pltpu.VMEM((2, 64, D), bf),
            pltpu.VMEM((6, 64, D), bf),
            pltpu.VMEM((2, 64, D), bf),
            pltpu.VMEM((6, 64, D), bf),
            pltpu.VMEM((4, 4) + slab, bf),
            pltpu.VMEM((4, 4) + slab, bf),
            pltpu.VMEM((4,) + slab, bf),
            pltpu.VMEM((4,) + slab, bf),
            pltpu.VMEM((4,) + slab, bf),
            pltpu.VMEM((3,) + slab, bf),
            pltpu.SemaphoreType.DMA((64,)),
            pltpu.SemaphoreType.DMA((64,)),
            pltpu.SemaphoreType.DMA((17,)),
        ],
        compiler_params=pltpu.CompilerParams(collective_id=2, has_side_effects=True, vmem_limit_bytes=56 << 20),
    )(m_part, dn_part, grads, h1, gain, cot)


def places(lengths_row, group_rows):
    seq_ends = jnp.cumsum(lengths_row)
    indices = jnp.arange(group_rows, dtype=jnp.int32)
    passed = indices[:, None] >= seq_ends[None, :]
    segment = jnp.sum(passed.astype(jnp.int32), axis=1)
    seq_start = jnp.sum(jnp.where(passed, lengths_row[None, :], 0), axis=1)
    return (segment, indices - seq_start)


def rotary(position, head_width):
    half_width = head_width // 2
    rates = THETA ** (-(jnp.arange(half_width, dtype=jnp.float32) * 2.0 / head_width))
    angles = position.astype(jnp.float32)[:, None] * rates[None, :]
    rot_cos = jnp.cos(angles)
    rot_sin = jnp.sin(angles)
    return (jnp.concatenate([rot_cos, rot_cos], 1), jnp.concatenate([rot_sin, rot_sin], 1))


def rotate(vector, rot_cos, rot_sin):
    half_width = vector.shape[-1] // 2
    turned = jnp.concatenate([-vector[..., half_width:], vector[..., :half_width]], -1)
    return vector * rot_cos[:, None, :] + turned * rot_sin[:, None, :]


def rotate_back(grad_rows, rot_cos, rot_sin):
    half_width = grad_rows.shape[-1] // 2
    moved = grad_rows * rot_sin[:, None, :]
    turned = jnp.concatenate([-moved[..., half_width:], moved[..., :half_width]], -1)
    return grad_rows * rot_cos[:, None, :] - turned


def scaled_norm(vector, gain_row):
    factor = lax.rsqrt(jnp.mean(vector * vector, axis=-1, keepdims=True) + EPS)
    return (vector * factor * gain_row, factor)


def norm_back(vector, factor, gain_row, grad_rows):
    inner = grad_rows * gain_row
    return factor * inner - vector * (factor * factor * factor) * jnp.mean(
        vector * inner, axis=-1, keepdims=True
    )


def contract(left, right):
    return lax.dot_general(
        left, right, (((1,), (1,)), ((), ())), preferred_element_type=jnp.float32
    )


def outer_sum(left, right):
    return lax.dot_general(
        left, right, (((0,), (0,)), ((), ())), preferred_element_type=jnp.float32
    )


def allowed_mask(segment, offset, block):
    group_rows = segment.shape[0]
    indices = jnp.arange(group_rows, dtype=jnp.int32)
    query_at = offset + jnp.arange(block, dtype=jnp.int32)
    seg_block = lax.dynamic_slice_in_dim(segment, offset, block, 0)
    return (seg_block[:, None] == segment[None, :]) & (indices[None, :] <= query_at[:, None])


def attention_forward(queries, key_rows, value_rows, segment, block):
    group_rows, head_count, head_width = queries.shape
    score_scale = head_width ** (-0.5)

    def one_block(offset):
        query_block = lax.dynamic_slice_in_dim(queries, offset, block, 0)
        allowed = allowed_mask(segment, offset, block)
        scores = (
            jnp.einsum("qhd,khd->hqk", query_block, key_rows, preferred_element_type=jnp.float32)
            * score_scale
        )
        scores = jnp.where(allowed[None], scores, -1e30)
        row_max = jnp.max(scores, axis=-1, keepdims=True)
        raised = jnp.exp(scores - row_max)
        totals = jnp.sum(raised, axis=-1, keepdims=True)
        weights = (raised / totals).astype(jnp.bfloat16)
        mixed_out = jnp.einsum(
            "hqk,khd->qhd", weights, value_rows, preferred_element_type=jnp.float32
        )
        return (mixed_out.astype(jnp.bfloat16), (row_max + jnp.log(totals))[..., 0])

    offsets = jnp.arange(group_rows // block, dtype=jnp.int32) * block
    mixed_out, log_totals = lax.map(one_block, offsets)
    return (mixed_out.reshape(group_rows, head_count * head_width), log_totals)


def attention_backward(queries, key_rows, value_rows, segment, log_totals, out_grad, block):
    group_rows, head_count, head_width = queries.shape
    score_scale = head_width ** (-0.5)

    def back_step(carried, block_in):
        key_grad, value_grad = carried
        offset, lse_block = block_in
        query_block = lax.dynamic_slice_in_dim(queries, offset, block, 0)
        grad_block = lax.dynamic_slice_in_dim(out_grad, offset, block, 0)
        allowed = allowed_mask(segment, offset, block)
        scores = (
            jnp.einsum("qhd,khd->hqk", query_block, key_rows, preferred_element_type=jnp.float32)
            * score_scale
        )
        scores = jnp.where(allowed[None], scores, -1e30)
        probs = jnp.exp(scores - lse_block[..., None])
        weights = probs.astype(jnp.bfloat16)
        value_grad = value_grad + jnp.einsum(
            "hqk,qhd->khd", weights, grad_block, preferred_element_type=jnp.float32
        )
        prob_grad = jnp.einsum(
            "qhd,khd->hqk", grad_block, value_rows, preferred_element_type=jnp.float32
        )
        centre = jnp.sum(probs * prob_grad, axis=-1, keepdims=True)
        score_grad = (probs * (prob_grad - centre)).astype(jnp.bfloat16)
        query_grad = (
            jnp.einsum("hqk,khd->qhd", score_grad, key_rows, preferred_element_type=jnp.float32)
            * score_scale
        )
        key_grad = (
            key_grad
            + jnp.einsum(
                "hqk,qhd->khd", score_grad, query_block, preferred_element_type=jnp.float32
            )
            * score_scale
        )
        return ((key_grad, value_grad), query_grad)

    offsets = jnp.arange(group_rows // block, dtype=jnp.int32) * block
    zeros_rows = jnp.zeros((group_rows, head_count, head_width), jnp.float32)
    (key_grad, value_grad), query_grad = lax.scan(
        back_step, (zeros_rows, zeros_rows), (offsets, log_totals)
    )
    return (query_grad.reshape(group_rows, head_count, head_width), key_grad, value_grad)


def shards(
    tokens,
    lengths,
    attn_gain,
    query_weight,
    key_weight,
    value_weight,
    out_weight,
    mlp_gain,
    gate_weight,
    up_weight,
    down_weight,
    cotangent,
):
    local_rows = tokens.shape[0]
    group_rows = local_rows * lax.axis_size("tensor")
    heads_here = query_weight.shape[1] // HEAD_DIM
    block = min(QBLOCK, group_rows)
    segment, position = places(lengths[0], group_rows)
    rot_cos, rot_sin = rotary(position, HEAD_DIM)
    shape_heads = (group_rows, heads_here, HEAD_DIM)
    residual = tokens.astype(jnp.float32)
    normed, factor_attn = scaled_norm(residual, attn_gain)
    normed_all = lax.all_gather(normed.astype(jnp.bfloat16), "tensor", axis=0, tiled=True)
    wq_full, wk_full, wv_full, wo_full = (
        lax.all_gather(query_weight, "dp", axis=0, tiled=True),
        lax.all_gather(key_weight, "dp", axis=0, tiled=True),
        lax.all_gather(value_weight, "dp", axis=0, tiled=True),
        lax.all_gather(out_weight, "dp", axis=0, tiled=True),
    )
    query_pre = jnp.dot(normed_all, wq_full, preferred_element_type=jnp.float32).reshape(
        shape_heads
    )
    key_pre = jnp.dot(normed_all, wk_full, preferred_element_type=jnp.float32).reshape(shape_heads)
    value_rows = (
        jnp.dot(normed_all, wv_full, preferred_element_type=jnp.float32)
        .astype(jnp.bfloat16)
        .reshape(shape_heads)
    )
    queries = rotate(query_pre, rot_cos, rot_sin).astype(jnp.bfloat16)
    key_rows = rotate(key_pre, rot_cos, rot_sin).astype(jnp.bfloat16)
    attended, log_totals = attention_forward(queries, key_rows, value_rows, segment, block)
    a_part = contract(attended, wo_full).astype(jnp.bfloat16)
    groups = [[0, 1, 2, 3], [4, 5, 6, 7]]
    cotangent_all = lax.all_gather(cotangent, "tensor", axis=0, tiled=True, axis_index_groups=groups)
    w_all, n2_all, hidden_res = mlp_in(a_part, tokens, mlp_gain[None], gate_weight.T, up_weight.T, down_weight.T)
    m_part, dn_part, grads = mlp(w_all, n2_all, cotangent_all)
    output, hidden_grad, branch_all, mlp_gain_part, gate_wg, up_wg, down_wg = mlp_out(
        m_part, dn_part, grads, hidden_res, mlp_gain[None], cotangent
    )
    mlp_gain_part = mlp_gain_part[0]
    wq_back, wk_back, wv_back, wo_back = (
        lax.all_gather(query_weight, "dp", axis=0, tiled=True),
        lax.all_gather(key_weight, "dp", axis=0, tiled=True),
        lax.all_gather(value_weight, "dp", axis=0, tiled=True),
        lax.all_gather(out_weight, "dp", axis=0, tiled=True),
    )
    attended_grad = (
        jnp.dot(branch_all, wo_back, preferred_element_type=jnp.float32)
        .astype(jnp.bfloat16)
        .reshape(shape_heads)
    )
    query_grad_rot, key_grad_rot, value_grad = attention_backward(
        queries, key_rows, value_rows, segment, log_totals, attended_grad, block
    )
    query_grad = (
        rotate_back(query_grad_rot, rot_cos, rot_sin).astype(jnp.bfloat16).reshape(group_rows, -1)
    )
    key_grad = (
        rotate_back(key_grad_rot, rot_cos, rot_sin).astype(jnp.bfloat16).reshape(group_rows, -1)
    )
    value_grad = value_grad.astype(jnp.bfloat16).reshape(group_rows, -1)
    out_wgrad = outer_sum(branch_all, attended)
    query_wgrad = outer_sum(normed_all, query_grad)
    key_wgrad = outer_sum(normed_all, key_grad)
    value_wgrad = outer_sum(normed_all, value_grad)
    normed_part = (
        contract(query_grad, wq_back) + contract(key_grad, wk_back) + contract(value_grad, wv_back)
    )
    normed_grad = lax.psum_scatter(
        normed_part.astype(jnp.bfloat16), "tensor", scatter_dimension=0, tiled=True
    ).astype(jnp.float32)
    tokens_grad = hidden_grad + norm_back(residual, factor_attn, attn_gain, normed_grad)
    attn_gain_part = jnp.sum(normed_grad * residual * factor_attn, axis=0)
    summed = (
        lax.psum_scatter(
            query_wgrad.astype(jnp.bfloat16), "dp", scatter_dimension=0, tiled=True
        ).astype(jnp.float32),
        lax.psum_scatter(
            key_wgrad.astype(jnp.bfloat16), "dp", scatter_dimension=0, tiled=True
        ).astype(jnp.float32),
        lax.psum_scatter(
            value_wgrad.astype(jnp.bfloat16), "dp", scatter_dimension=0, tiled=True
        ).astype(jnp.float32),
        lax.psum_scatter(
            out_wgrad.astype(jnp.bfloat16), "dp", scatter_dimension=0, tiled=True
        ).astype(jnp.float32),
        gate_wg.T,
        up_wg.T,
        down_wg.T,
    )
    gain_sums = lax.psum((attn_gain_part, mlp_gain_part), ("dp", "tensor"))
    return (
        output,
        tokens_grad,
        gain_sums[0],
        summed[0],
        summed[1],
        summed[2],
        summed[3],
        gain_sums[1],
        summed[4],
        summed[5],
        summed[6],
    )


def solution(mesh):
    return jax.shard_map(
        shards,
        mesh=mesh,
        in_specs=(
            P(("dp", "tensor"), None),
            P("dp", None),
            P(),
            P("dp", "tensor"),
            P("dp", "tensor"),
            P("dp", "tensor"),
            P("dp", "tensor"),
            P(),
            P("dp", "tensor"),
            P("dp", "tensor"),
            P("dp", "tensor"),
            P(("dp", "tensor"), None),
        ),
        out_specs=(
            P(("dp", "tensor"), None),
            P(("dp", "tensor"), None),
            P(),
            P("dp", "tensor"),
            P("dp", "tensor"),
            P("dp", "tensor"),
            P("dp", "tensor"),
            P(),
            P("dp", "tensor"),
            P("dp", "tensor"),
            P("dp", "tensor"),
        ),
        check_vma=False,
    )
```

```python
import functools

import jax
import jax.numpy as jnp
import numpy as np
from jax import lax
from jax.experimental import pallas as pl
from jax.experimental.pallas import tpu as pltpu
from jax.sharding import PartitionSpec as P

HEAD_DIM = 128
EPS = 1e-05
THETA = 10000.0
D = 2048
ROWS = 128
GROUP = 1024
FFB = 688
CUT = 352
MESH = pl.DeviceIdType.MESH
ANY = pl.BlockSpec(memory_space=pl.ANY)
VMEM = pl.BlockSpec(memory_space=pltpu.VMEM)
NT = (((1,), (1,)), ((), ()))
TN = (((0,), (0,)), ((), ()))


class Net:
    def __init__(self, send_sems, recv_sems):
        dp, t = lax.axis_index("dp"), lax.axis_index("tensor")
        self.y, self.c = lax.div(dp, 4), lax.rem(dp, 2)
        self.xl, self.z = lax.div(t, 4), lax.rem(t, 4)
        self.x = lax.rem(lax.div(dp, 2), 2) * 2 + self.xl
        self.dp, self.t = dp, t
        self.send_sems, self.recv_sems = send_sems, recv_sems
        self.used = 0
        self.sent = []

    def device(self, dx=0, dy=0, dz=0, dc=0):
        x, y = lax.rem(self.x + dx + 4, 4), lax.rem(self.y + dy + 4, 4)
        z, c = lax.rem(self.z + dz + 4, 4), lax.rem(self.c + dc, 2)
        return (y * 4 + lax.div(x, 2) * 2 + c, lax.rem(x, 2) * 4 + z)

    @property
    def beside(self):
        return (self.dp, (1 - self.xl) * 4 + self.z)

    @property
    def across(self):
        return self.device(dx=2)

    def along(self, first):
        on_x = self.c == (0 if first else 1)
        both = []
        for step in (1, -1):
            by_x, by_y = self.device(dx=step), self.device(dy=step)
            both.append(tuple(jnp.where(on_x, u, v) for u, v in zip(by_x, by_y)))
        return both

    def send(self, src, dst, to):
        k = self.used
        self.used += 1
        copy = pltpu.make_async_remote_copy(
            src_ref=src,
            dst_ref=dst,
            send_sem=self.send_sems.at[k],
            recv_sem=self.recv_sems.at[k],
            device_id=to,
            device_id_type=MESH,
        )
        copy.start()
        self.sent.append(copy)
        return copy

    def finish(self):
        for copy in self.sent:
            copy.wait_send()

    def greet(self, devices):
        barrier = pltpu.get_barrier_semaphore()
        for device in devices:
            pl.semaphore_signal(barrier, inc=1, device_id=device, device_id_type=MESH)
        pl.semaphore_wait(barrier, len(devices))


def take_turns(chains, order):
    for name in order:
        next(chains[name], None)
    for chain in chains.values():
        for _ in chain:
            pass


def block(z):
    return pl.ds(pl.multiple_of(lax.rem(z + 8, 4) * ROWS, ROWS), ROWS)


def half(z, k):
    return pl.ds(pl.multiple_of(lax.rem(z + 8, 4) * ROWS + k * 64, 64), 64)


def block8(xl, z):
    return pl.ds(pl.multiple_of((xl * 4 + lax.rem(z + 8, 4)) * ROWS, ROWS), ROWS)


def half8(xl, z, k):
    return pl.ds(pl.multiple_of((xl * 4 + lax.rem(z + 8, 4)) * ROWS + k * 64, 64), 64)


def add_rows(rows, dst, *terms):
    def step(i, _):
        at = pl.ds(pl.multiple_of(i * 16, 16), 16)
        total = terms[0][at, :].astype(jnp.float32)
        for term in terms[1:]:
            total = total + term[at, :].astype(jnp.float32)
        dst[at, :] = total.astype(dst.dtype)
        return 0

    lax.fori_loop(0, rows // 16, step, 0)


def gather_z(net, own, dst):
    up, down = net.device(dz=1), net.device(dz=-1)
    z = net.z
    a0 = net.send(own, dst.at[block(z), :], up)
    a1 = net.send(own, dst.at[block(z), :], down)
    yield
    a0.wait_recv()
    b0 = net.send(dst.at[half(z - 1, 0), :], dst.at[half(z - 1, 0), :], up)
    a1.wait_recv()
    b1 = net.send(dst.at[half(z + 1, 1), :], dst.at[half(z + 1, 1), :], down)
    yield
    b0.wait_recv()
    b1.wait_recv()


def gather_8(net, own, dst):
    up, down, beside = net.device(dz=1), net.device(dz=-1), net.beside
    xl, z = net.xl, net.z
    place = dst.at[block8(xl, z), :]
    s0 = net.send(own, place, up)
    s1 = net.send(own, place, down)
    s2 = net.send(own, place, beside)
    yield
    s0.wait_recv()
    ref = dst.at[half8(xl, z - 1, 0), :]
    s5 = net.send(ref, ref, up)
    s1.wait_recv()
    ref = dst.at[half8(xl, z + 1, 1), :]
    s6 = net.send(ref, ref, down)
    s2.wait_recv()
    ref = dst.at[block8(1 - xl, z), :]
    s3 = net.send(ref, ref, up)
    s4 = net.send(ref, ref, down)
    yield
    s5.wait_recv()
    s6.wait_recv()
    ref = dst.at[block8(xl, z + 2), :]
    s7 = net.send(ref, ref, beside)
    yield
    s3.wait_recv()
    s4.wait_recv()
    s7.wait_recv()


def reduce_z(net, part, sums, got, out):
    up, down = net.device(dz=1), net.device(dz=-1)
    z = net.z
    c0 = net.send(part.at[half(z + 2, 0), :], got.at[0], up)
    c1 = net.send(part.at[half(z + 2, 1), :], got.at[1], down)
    d1 = net.send(part.at[half(z + 1, 1), :], got.at[3], up)
    d2 = net.send(part.at[half(z - 1, 0), :], got.at[4], down)
    yield
    c0.wait_recv()
    add_rows(64, sums.at[0], part.at[half(z + 1, 0), :], got.at[0])
    d0 = net.send(sums.at[0], got.at[2], up)
    c1.wait_recv()
    add_rows(64, sums.at[1], part.at[half(z - 1, 1), :], got.at[1])
    d3 = net.send(sums.at[1], got.at[5], down)
    yield
    for copy in (d0, d1, d2, d3):
        copy.wait_recv()
    out.append(lambda at, k: part[pl.ds(pl.multiple_of(net.z * ROWS + at, 16), 16), :].astype(jnp.float32)
               + got[2 + k, pl.ds(pl.multiple_of(at - 64 * k, 16), 16), :].astype(jnp.float32)
               + got[4 + k, pl.ds(pl.multiple_of(at - 64 * k, 16), 16), :].astype(jnp.float32))


def reduce_8(net, make, part, sums, got, sums_half, got_half, out):
    up, down, beside = net.device(dz=1), net.device(dz=-1), net.beside
    xl, z = net.xl, net.z
    make(1 - xl, z + 2)
    a = net.send(part.at[block8(1 - xl, z + 2), :], got.at[0], beside)
    make(1 - xl, z + 1)
    b0 = net.send(part.at[block8(1 - xl, z + 1), :], got.at[1], up)
    make(1 - xl, z - 1)
    b1 = net.send(part.at[block8(1 - xl, z - 1), :], got.at[2], down)
    make(xl, z + 2)
    make(xl, z + 1)
    d1 = net.send(part.at[half8(xl, z + 1, 1), :], got_half.at[3], up)
    make(xl, z - 1)
    d2 = net.send(part.at[half8(xl, z - 1, 0), :], got_half.at[4], down)
    make(1 - xl, z)
    make(xl, z)
    yield
    a.wait_recv()
    add_rows(128, sums.at[0], part.at[block8(xl, z + 2), :], got.at[0])
    c0 = net.send(sums.at[0, pl.ds(0, 64), :], got_half.at[0], up)
    c1 = net.send(sums.at[0, pl.ds(64, 64), :], got_half.at[1], down)
    yield
    b0.wait_recv()
    b1.wait_recv()
    add_rows(128, sums.at[1], part.at[block8(1 - xl, z), :], got.at[1], got.at[2])
    e = net.send(sums.at[1], got.at[3], beside)
    yield
    c0.wait_recv()
    add_rows(64, sums_half.at[0], part.at[half8(xl, z + 1, 0), :], got_half.at[0])
    d0 = net.send(sums_half.at[0], got_half.at[2], up)
    c1.wait_recv()
    add_rows(64, sums_half.at[1], part.at[half8(xl, z - 1, 1), :], got_half.at[1])
    d3 = net.send(sums_half.at[1], got_half.at[5], down)
    yield
    for copy in (e, d0, d1, d2, d3):
        copy.wait_recv()

    def rows(at, k):
        here = pl.ds(pl.multiple_of(at - 64 * k, 16), 16)
        total = part[pl.ds(pl.multiple_of(net.t * ROWS + at, 16), 16), :].astype(jnp.float32)
        total = total + got[3, pl.ds(pl.multiple_of(at, 16), 16), :].astype(jnp.float32)
        return total + got_half[2 + k, here, :].astype(jnp.float32) + got_half[4 + k, here, :].astype(jnp.float32)

    out.append(rows)


def each_half(step):
    for k in (0, 1):
        def body(i, _, k=k):
            step(pl.multiple_of(k * 64 + i * 16, 16), k)
            return 0

        lax.fori_loop(0, 4, body, 0)


def gather_plane(net, slab, cut, first, second):
    low, high = cut
    sib = net.device(dc=1)
    second_up, second_down = second

    def share(i, j):
        ref = slab(i, j)
        return net.send(ref, ref, sib)

    def go(i):
        ref = slab(i, 0)
        return net.send(ref, ref, second_up), net.send(ref, ref, second_down)

    shared = []
    own = slab(0, 0)
    ring = len(first) == 2
    if ring:
        a0, a1 = net.send(own, own, first[0]), net.send(own, own, first[1])
    else:
        a0 = net.send(own, own, first[0])
    sent = {0: go(0)}
    shared.append(share(0, 0))
    yield
    if ring:
        a0.wait_recv()
        ref = low(slab(-1, 0))
        f0 = net.send(ref, ref, first[0])
        a1.wait_recv()
        ref = high(slab(1, 0))
        f1 = net.send(ref, ref, first[1])
        for i in (-1, 1):
            sent[i] = go(i)
            shared.append(share(i, 0))
        yield
        f0.wait_recv()
        f1.wait_recv()
        sent[2] = go(2)
        shared.append(share(2, 0))
    else:
        a0.wait_recv()
        sent[1] = go(1)
        shared.append(share(1, 0))
    halves = {}
    for i in sent:
        yield
        sent[i][0].wait_recv()
        ref = low(slab(i, -1))
        h0 = net.send(ref, ref, second_up)
        shared.append(share(i, -1))
        sent[i][1].wait_recv()
        ref = high(slab(i, 1))
        h1 = net.send(ref, ref, second_down)
        shared.append(share(i, 1))
        halves[i] = (h0, h1)
    for i in sent:
        yield
        halves[i][0].wait_recv()
        halves[i][1].wait_recv()
        shared.append(share(i, 2))
    yield
    for copy in shared:
        copy.wait_recv()


def reduce_plane(net, mine, other, from_sib, got_half, got_up, got_down, last_bufs, cut, add, first, second):
    low, high = cut
    sib = net.device(dc=1)
    up, down = second
    ring = len(first) == 2
    steps = (0, 1, 3, 2) if ring else (0, 1)
    shared = {}
    for j in (2, 1, 3, 0):
        for i in steps:
            shared[i, j] = net.send(other(i, j), from_sib(i, j), sib)
    yield
    halves, full = {}, {}
    for i in steps:
        shared[i, 2].wait_recv()
        add(None, mine(i, 2), from_sib(i, 2))
        halves[i] = (
            net.send(low(mine(i, 2)), low(got_half(i)), up),
            net.send(high(mine(i, 2)), high(got_half(i)), down),
        )
        yield
    for i in steps:
        for j in (1, 3):
            shared[i, j].wait_recv()
            add(None, mine(i, j), from_sib(i, j))
        halves[i][0].wait_recv()
        add(0, mine(i, 1), got_half(i))
        u = net.send(mine(i, 1), got_up(i), up)
        halves[i][1].wait_recv()
        add(1, mine(i, 3), got_half(i))
        full[i] = (u, net.send(mine(i, 3), got_down(i), down))
        yield
    last = {}
    for i in reversed(steps):
        shared[i, 0].wait_recv()
        full[i][0].wait_recv()
        full[i][1].wait_recv()
        add(None, mine(i, 0), from_sib(i, 0), got_up(i), got_down(i))
        if ring and i == 2:
            ref, to = mine(2, 0), last_bufs(2)
            last[2] = (net.send(low(ref), low(to), first[0]), net.send(high(ref), high(to), first[1]))
        if ring and i == 3:
            last[2][1].wait_recv()
            add(1, mine(3, 0), last_bufs(2))
            last[3] = net.send(mine(3, 0), last_bufs(1), first[1])
        if ring and i == 1:
            last[2][0].wait_recv()
            add(0, mine(1, 0), last_bufs(2))
        if i == 1:
            last[1] = net.send(mine(1, 0), last_bufs(0), first[0])
        yield
    last[1].wait_recv()
    if ring:
        last[3].wait_recv()
        add(None, mine(0, 0), last_bufs(0), last_bufs(1))
    else:
        add(None, mine(0, 0), last_bufs(0))


PIECES = {None: ((0, 176), (176, 176), (352, 176), (528, 160)), 0: ((0, 176), (176, 176)), 1: ((352, 176), (528, 160))}


def add_slab(part, dst, *terms):
    def step(m, _):
        for at, n in PIECES[part]:
            total = dst[m, at : at + n, :].astype(jnp.float32)
            for term in terms:
                total = total + term[m, at : at + n, :].astype(jnp.float32)
            dst[m, at : at + n, :] = total.astype(dst.dtype)
        return 0

    lax.fori_loop(0, 3, step, 0)


FF_CUT = (lambda ref: ref.at[:, pl.ds(0, CUT), :], lambda ref: ref.at[:, pl.ds(CUT, FFB - CUT), :])


def ff_slab(net, ref, kind, i, j):
    x = lax.rem(net.x + jnp.where(kind == 0, i, j) + 4, 4)
    y = lax.rem(net.y + jnp.where(kind == 0, j, i) + 4, 4)
    at = pl.ds(pl.multiple_of((y * 4 + lax.div(x, 2) * 2 + kind) * 128, 128), 128)
    return ref.at[:, lax.rem(x, 2), :, at]


def mlp_in_kernel(o, wo, tok, gain, wg, wu, wd, w_all, n2_all, h1, a_part, n2, sums, got, sums_half, got_half, send_sems, recv_sems, sems):
    net = Net(send_sems, recv_sems)
    xy = [net.device(dx=1), net.device(dx=-1), net.device(dy=1), net.device(dy=-1)]
    own = ff_slab(net, w_all, net.c, 0, 0)
    copies = [pltpu.make_async_copy(w, own.at[k], sems.at[k]) for k, w in enumerate((wg, wu, wd))]
    for copy in copies:
        copy.start()
    net.greet(xy + [net.device(dz=1), net.device(dz=-1), net.device(dc=1)])

    def tokens():
        out = []

        def make(xl, z):
            here = block8(xl, z)
            a_part[here, :] = lax.dot_general(o[here, :], wo[...], NT, preferred_element_type=jnp.float32).astype(jnp.bfloat16)

        yield from reduce_8(net, make, a_part, sums, got, sums_half, got_half, out)

        def step(at, k):
            here = pl.ds(at, 16)
            h = tok[here, :].astype(jnp.float32) + out[0](at, k)
            h1[here, :] = h
            r = lax.rsqrt(jnp.mean(h * h, axis=-1, keepdims=True) + EPS)
            n2[here, :] = (h * r * gain[...]).astype(jnp.bfloat16)

        each_half(step)
        place = pltpu.make_async_copy(n2, n2_all.at[block(net.z), :], sems.at[3])
        place.start()
        yield from gather_z(net, n2, n2_all)
        place.wait()

    def weights():
        for copy in copies:
            copy.wait()
        slab = functools.partial(ff_slab, net, w_all, net.c)
        yield from gather_plane(net, slab, FF_CUT, net.along(True), net.along(False))

    take_turns({"t": tokens(), "w": weights()}, "twwttwtwtwwtwwww")
    net.finish()


def mlp_in(o, wo, tok, gain, wg, wu, wd):
    return pl.pallas_call(
        mlp_in_kernel,
        name="mlp_in",
        out_shape=(
            jax.ShapeDtypeStruct((3, 2, FFB, D), jnp.bfloat16),
            jax.ShapeDtypeStruct((4 * ROWS, D), jnp.bfloat16),
            jax.ShapeDtypeStruct((ROWS, D), jnp.float32),
        ),
        in_specs=[VMEM, VMEM, VMEM, VMEM, ANY, ANY, ANY],
        out_specs=(ANY, ANY, VMEM),
        scratch_shapes=[
            pltpu.VMEM((GROUP, D), jnp.bfloat16),
            pltpu.VMEM((ROWS, D), jnp.bfloat16),
            pltpu.VMEM((2, ROWS, D), jnp.bfloat16),
            pltpu.VMEM((4, ROWS, D), jnp.bfloat16),
            pltpu.VMEM((2, 64, D), jnp.bfloat16),
            pltpu.VMEM((6, 64, D), jnp.bfloat16),
            pltpu.SemaphoreType.DMA((64,)),
            pltpu.SemaphoreType.DMA((64,)),
            pltpu.SemaphoreType.DMA((4,)),
        ],
        compiler_params=pltpu.CompilerParams(collective_id=1, has_side_effects=True, vmem_limit_bytes=56 << 20),
    )(o, wo, tok, gain, wg, wu, wd)


TILES = ((0, 256), (256, 256), (512, 176))


def mlp_kernel(w_all, n2_all, g_all, m_out, dn_out, grads, w, n2, g, hid, dgate, dup, turned, stage, sems, out_sems):
    copies = [
        pltpu.make_async_copy(n2_all, n2, sems.at[0]),
        pltpu.make_async_copy(g_all, g, sems.at[1]),
    ]
    loads = [pltpu.make_async_copy(w_all.at[m, b], w.at[m, b], sems.at[2 + m * 2 + b]) for m in range(3) for b in range(2)]
    for copy in copies + loads:
        copy.start()
    for copy in copies + loads:
        copy.wait()

    def ahead(b, _):
        for at, n in TILES:
            gate = lax.dot_general(n2[...], w[0, b, at : at + n, :], NT, preferred_element_type=jnp.float32)
            up = lax.dot_general(n2[...], w[1, b, at : at + n, :], NT, preferred_element_type=jnp.float32)
            dh = lax.dot_general(g[...], w[2, b, at : at + n, :], NT, preferred_element_type=jnp.float32)
            sig = jax.nn.sigmoid(gate)
            act = gate * sig
            for k, (dst, value) in enumerate(
                ((dgate, dh * up * sig * (1.0 + gate * (1.0 - sig))), (dup, dh * act), (hid, act * up))
            ):
                value = value.astype(jnp.bfloat16)
                dst[b, :, at : at + n] = value
                turned[k, b, at : at + n, :] = value.T
        return 0

    lax.fori_loop(0, 2, ahead, 0)

    def back(i, _):
        at = pl.ds(pl.multiple_of(i * 256, 256), 256)
        m = jnp.dot(hid[0], w[2, 0, :, at], preferred_element_type=jnp.float32)
        m = m + jnp.dot(hid[1], w[2, 1, :, at], preferred_element_type=jnp.float32)
        m_out[:, at] = m.astype(jnp.bfloat16)
        d = jnp.dot(dgate[0], w[0, 0, :, at], preferred_element_type=jnp.float32)
        d = d + jnp.dot(dgate[1], w[0, 1, :, at], preferred_element_type=jnp.float32)
        d = d + jnp.dot(dup[0], w[1, 0, :, at], preferred_element_type=jnp.float32)
        d = d + jnp.dot(dup[1], w[1, 1, :, at], preferred_element_type=jnp.float32)
        dn_out[:, at] = d.astype(jnp.bfloat16)
        return 0

    lax.fori_loop(0, 8, back, 0)

    def put(i, m, b, slot):
        at = pl.ds(pl.multiple_of(i * 256, 256), 256)
        return pltpu.make_async_copy(stage.at[slot], grads.at[m, b, :, at], out_sems.at[slot])

    def outer(i, _):
        at = pl.ds(pl.multiple_of(i * 256, 256), 256)
        for m in range(3):
            right = (n2, n2, g)[m][:, at]
            for b in range(2):
                slot = m * 2 + b
                pl.when(i > 0)(lambda: put(i - 1, m, b, slot).wait())
                stage[slot] = jnp.dot(turned[m, b], right, preferred_element_type=jnp.float32).astype(jnp.bfloat16)
                put(i, m, b, slot).start()
        return 0

    lax.fori_loop(0, 8, outer, 0)
    for m in range(3):
        for b in range(2):
            put(7, m, b, m * 2 + b).wait()


def mlp(w_all, n2_all, g_all):
    bf = jnp.bfloat16
    return pl.pallas_call(
        mlp_kernel,
        name="mlp",
        out_shape=(
            jax.ShapeDtypeStruct((512, D), bf),
            jax.ShapeDtypeStruct((512, D), bf),
            jax.ShapeDtypeStruct((3, 2, FFB, D), bf),
        ),
        in_specs=[ANY] * 3,
        out_specs=(VMEM, VMEM, ANY),
        scratch_shapes=[
            pltpu.VMEM((3, 2, FFB, D), bf),
            pltpu.VMEM((512, D), bf),
            pltpu.VMEM((512, D), bf),
            pltpu.VMEM((2, 512, FFB), bf),
            pltpu.VMEM((2, 512, FFB), bf),
            pltpu.VMEM((2, 512, FFB), bf),
            pltpu.VMEM((3, 2, FFB, 512), bf),
            pltpu.VMEM((6, FFB, 256), bf),
            pltpu.SemaphoreType.DMA((8,)),
            pltpu.SemaphoreType.DMA((6,)),
        ],
        compiler_params=pltpu.CompilerParams(vmem_limit_bytes=58 << 20),
        cost_estimate=pl.CostEstimate(flops=26 * 10**9, bytes_accessed=40 << 20, transcendentals=704512),
    )(w_all, n2_all, g_all)


def mlp_out_kernel(m_part, dn_part, grads, h1, gain, cot, mixed, dh1, da_all, gain_part, wg, wu, wd,
                   da, sums_m, got_m, sums_d, got_d, mine, sib, got_half, got_up, got_down, last, send_sems, recv_sems, sems):
    net = Net(send_sems, recv_sems)
    xy = [net.device(dx=1), net.device(dx=-1), net.device(dy=1), net.device(dy=-1)]
    order = [(i, j) for j in (2, 1, 3, 0) for i in (0, 1, 3, 2)]
    loads = {}
    for k, (i, j) in enumerate(order):
        loads[i, j] = pltpu.make_async_copy(ff_slab(net, grads, net.c, i, j), mine.at[i, j], sems.at[k])
        loads[i, j].start()
    net.greet(xy + [net.device(dz=1), net.device(dz=-1), net.device(dc=1)])

    def tokens():
        out = []
        yield from reduce_z(net, dn_part, sums_d, got_d, out)

        def step(at, k, total):
            here = pl.ds(at, 16)
            h = h1[here, :]
            r = lax.rsqrt(jnp.mean(h * h, axis=-1, keepdims=True) + EPS)
            d = out[0](at, k)
            inner = d * gain[...]
            grad = r * inner - h * (r * r * r) * jnp.mean(h * inner, axis=-1, keepdims=True)
            grad = cot[here, :].astype(jnp.float32) + grad
            dh1[here, :] = grad
            da[here, :] = grad.astype(jnp.bfloat16)
            gain_part[...] += jnp.sum(d * h * r, axis=0, keepdims=True)

        gain_part[...] = jnp.zeros_like(gain_part)
        each_half(lambda at, k: step(at, k, None))
        place = pltpu.make_async_copy(da, da_all.at[block8(net.xl, net.z), :], sems.at[16])
        place.start()
        yield from gather_8(net, da, da_all)
        place.wait()

    def forward():
        out = []
        yield from reduce_z(net, m_part, sums_m, got_m, out)

        def step(at, k):
            here = pl.ds(at, 16)
            mixed[here, :] = (h1[here, :] + out[0](at, k)).astype(jnp.bfloat16)

        each_half(step)

    def weights():
        waited = set()

        def add(part, dst, *terms):
            add_slab(part, dst, *terms)

        def slot(ref):
            return lambda i, j: ref.at[i, j]

        sib_kind = 1 - net.c
        for copy in loads.values():
            copy.wait()
        yield from reduce_plane(
            net, slot(mine), functools.partial(ff_slab, net, grads, sib_kind), slot(sib),
            lambda i: got_half.at[i], lambda i: got_up.at[i], lambda i: got_down.at[i], lambda i: last.at[i],
            FF_CUT, add, net.along(True), net.along(False),
        )
        for k, dst in enumerate((wg, wu, wd)):
            for at, n in PIECES[None]:
                dst[at : at + n, :] = mine[0, 0, k, at : at + n, :].astype(jnp.float32)

    take_turns({"t": tokens(), "m": forward(), "w": weights()}, "twwwwtwmwwtwwtwwtwww")
    net.finish()


def mlp_out(m_part, dn_part, grads, h1, gain, cot):
    bf, f32 = jnp.bfloat16, jnp.float32
    slab = (3, FFB, 128)
    return pl.pallas_call(
        mlp_out_kernel,
        name="mlp_out",
        out_shape=(
            jax.ShapeDtypeStruct((ROWS, D), bf),
            jax.ShapeDtypeStruct((ROWS, D), f32),
            jax.ShapeDtypeStruct((GROUP, D), bf),
            jax.ShapeDtypeStruct((1, D), f32),
        ) + (jax.ShapeDtypeStruct((FFB, 128), f32),) * 3,
        in_specs=[VMEM, VMEM, ANY, VMEM, VMEM, VMEM],
        out_specs=(VMEM, VMEM, ANY, VMEM, VMEM, VMEM, VMEM),
        scratch_shapes=[
            pltpu.VMEM((ROWS, D), bf),
            pltpu.VMEM((2, 64, D), bf),
            pltpu.VMEM((6, 64, D), bf),
            pltpu.VMEM((2, 64, D), bf),
            pltpu.VMEM((6, 64, D), bf),
            pltpu.VMEM((4, 4) + slab, bf),
            pltpu.VMEM((4, 4) + slab, bf),
            pltpu.VMEM((4,) + slab, bf),
            pltpu.VMEM((4,) + slab, bf),
            pltpu.VMEM((4,) + slab, bf),
            pltpu.VMEM((3,) + slab, bf),
            pltpu.SemaphoreType.DMA((64,)),
            pltpu.SemaphoreType.DMA((64,)),
            pltpu.SemaphoreType.DMA((17,)),
        ],
        compiler_params=pltpu.CompilerParams(collective_id=2, has_side_effects=True, vmem_limit_bytes=56 << 20),
    )(m_part, dn_part, grads, h1, gain, cot)


ATT_CUT = (lambda ref: ref.at[:, pl.ds(0, 64), :], lambda ref: ref.at[:, pl.ds(64, 64), :])
ATT_CUT_T = (lambda ref: ref.at[:, pl.ds(0, 128), :], lambda ref: ref.at[:, pl.ds(128, 128), :])


def att_at(net, kind, i, j):
    x, y = lax.rem(net.x + 2 * i + 4, 4), lax.rem(net.y + j + 4, 4)
    return pl.ds(pl.multiple_of((y * 4 + lax.div(x, 2) * 2 + kind) * 128, 128), 128)


def sequence_starts(lengths, at, rows):
    index = lax.broadcasted_iota(jnp.int32, (rows, 1), 0) + at
    end, start = lengths[0, 0], jnp.zeros((rows, 1), jnp.int32)
    for s in range(8):
        start = jnp.where(index >= end, end, start)
        if s < 7:
            end = end + lengths[0, s + 1]
    return index, start


QROWS = 256


def attn_in_kernel(tok, cot, lengths, gain, rates, wq, wk, wv, wo,
                   g_all, n1_out, w_out, q_out, k_out, v_out, p_out, o_out, table_out,
                   n1, n1_all, w, q, k, v, p, o, table, send_sems, recv_sems, sems):
    net = Net(send_sems, recv_sems)
    own_rows = att_at(net, net.c, 0, 0)
    copies = [pltpu.make_async_copy(u, w.at[m, own_rows, :], sems.at[m]) for m, u in enumerate((wq, wk, wv, wo))]
    for copy in copies:
        copy.start()
    copies.append(pltpu.make_async_copy(cot, g_all.at[block(net.z), :], sems.at[4]))
    copies[4].start()

    def norm(at, _):
        here = pl.ds(at, 16)
        value = tok[here, :].astype(jnp.float32)
        r = lax.rsqrt(jnp.mean(value * value, axis=-1, keepdims=True) + EPS)
        n1[here, :] = (value * r * gain[...]).astype(jnp.bfloat16)

    each_half(norm)
    net.greet([net.device(dy=1), net.device(dy=-1), net.device(dz=1), net.device(dz=-1), net.device(dc=1), net.beside, net.across])
    place = pltpu.make_async_copy(n1, n1_all.at[block8(net.xl, net.z), :], sems.at[5])
    place.start()

    def tokens():
        yield from gather_8(net, n1, n1_all)

    def cotangent():
        yield from gather_z(net, cot, g_all)

    def weights():
        for copy in copies[:4]:
            copy.wait()

        def slab(i, j):
            return w.at[:, att_at(net, net.c, i, j), :]

        yield from gather_plane(net, slab, ATT_CUT, (net.across,), (net.device(dy=1), net.device(dy=-1)))

    chains = {"t": tokens(), "w": weights(), "g": cotangent()}
    for name in "tw":
        next(chains[name])

    def tables(i, _):
        at = pl.multiple_of(i * 128, 128)
        index, start = sequence_starts(lengths, at, 128)
        angle = (index - start).astype(jnp.float32) * rates[...]
        lane = lax.broadcasted_iota(jnp.int32, (128, 128), 1)
        table[0, pl.ds(at, 128), :] = jnp.cos(angle)
        sin = jnp.sin(angle)
        table[1, pl.ds(at, 128), :] = jnp.where(lane < 64, -sin, sin)
        return 0

    lax.fori_loop(0, 8, tables, 0)
    for name in "wttwt":
        next(chains[name], None)
    for name in "tw":
        for _ in chains[name]:
            pass
    place.wait()
    next(chains["g"])
    saves = [
        pltpu.make_async_copy(n1_all, n1_out, sems.at[6]),
        pltpu.make_async_copy(w, w_out, sems.at[7]),
        pltpu.make_async_copy(table, table_out, sems.at[8]),
    ]
    for copy in saves:
        copy.start()

    def project(i, _):
        here = pl.ds(pl.multiple_of(i * QROWS, QROWS), QROWS)
        left = n1_all[here, :]
        cos, sin = table[0, here, :], table[1, here, :]
        for m, dst in ((0, q), (1, k)):
            u = jnp.dot(left, w[m], preferred_element_type=jnp.float32)
            for h in range(2):
                uh = u[:, h * 128 : h * 128 + 128]
                dst[h, here, :] = (uh * cos + pltpu.roll(uh, 64, 1) * sin).astype(jnp.bfloat16)
        u = jnp.dot(left, w[2], preferred_element_type=jnp.float32).astype(jnp.bfloat16)
        for h in range(2):
            v[h, here, :] = u[:, h * 128 : h * 128 + 128]
        return 0

    lax.fori_loop(0, GROUP // QROWS, project, 0)
    next(chains["g"], None)

    for b in range(GROUP // QROWS):
        rows = slice(b * QROWS, b * QROWS + QROWS)
        first, last = max(0, b - 2) * QROWS, (b + 1) * QROWS
        index, start = sequence_starts(lengths, b * QROWS, QROWS)
        key = lax.broadcasted_iota(jnp.int32, (QROWS, last - first), 1) + first
        allowed = (key <= index) & (key >= start)

        for h in range(2):
            s = lax.dot_general(q[h, rows, :], k[h, first:last, :], NT, preferred_element_type=jnp.float32)
            s = jnp.where(allowed, s * HEAD_DIM ** (-0.5), -1e30)
            e = jnp.exp(s - jnp.max(s, axis=-1, keepdims=True))
            weights_b = (e / jnp.sum(e, axis=-1, keepdims=True)).astype(jnp.bfloat16)
            p[h, rows, first:last] = weights_b
            o[rows, h * 128 : h * 128 + 128] = jnp.dot(
                weights_b, v[h, first:last, :], preferred_element_type=jnp.float32
            ).astype(jnp.bfloat16)

    more = [pltpu.make_async_copy(src, dst, sems.at[9 + n]) for n, (src, dst) in enumerate(((q, q_out), (k, k_out), (v, v_out), (p, p_out), (o, o_out)))]
    for copy in more:
        copy.start()
    for _ in chains["g"]:
        pass
    for copy in copies[4:] + saves + more:
        copy.wait()
    net.finish()


def attn_in(tok, cot, lengths, gain, rates, wq, wk, wv, wo):
    bf, f32 = jnp.bfloat16, jnp.float32
    shapes = (
        ((4 * ROWS, D), bf), ((GROUP, D), bf), ((4, D, 256), bf), ((2, GROUP, 128), bf), ((2, GROUP, 128), bf),
        ((2, GROUP, 128), bf), ((2, GROUP, GROUP), bf), ((GROUP, 256), bf), ((2, GROUP, 128), f32),
    )
    return pl.pallas_call(
        attn_in_kernel,
        name="attn_in",
        out_shape=tuple(jax.ShapeDtypeStruct(*s) for s in shapes),
        in_specs=[VMEM, VMEM, pl.BlockSpec(memory_space=pltpu.SMEM), VMEM, VMEM, ANY, ANY, ANY, ANY],
        out_specs=(ANY,) * 9,
        scratch_shapes=[pltpu.VMEM((ROWS, D), bf)] + [pltpu.VMEM(*s) for s in shapes[1:]] + [
            pltpu.SemaphoreType.DMA((48,)),
            pltpu.SemaphoreType.DMA((48,)),
            pltpu.SemaphoreType.DMA((14,)),
        ],
        compiler_params=pltpu.CompilerParams(collective_id=3, has_side_effects=True, vmem_limit_bytes=56 << 20),
    )(tok, cot, lengths, gain, rates, wq, wk, wv, wo)


def add_att(part, dst, *terms):
    def step(m, _):
        for at in {None: (0, 128), 0: (0,), 1: (128,)}[part]:
            total = dst[m, at : at + 128, :].astype(jnp.float32)
            for term in terms:
                total = total + term[m, at : at + 128, :].astype(jnp.float32)
            dst[m, at : at + 128, :] = total.astype(dst.dtype)
        return 0

    lax.fori_loop(0, 4, step, 0)


def attn_out_kernel(da_in, n1_in, w_in, q_in, k_in, v_in, p_in, o_in, table_in, tok, dh1, gain, mlp_gain_part,
                    dx, gains, gq, gk, gv, go,
                    da, n1, w, q, k, v, p, o, table, do, dqkv, dk, dv, part, sums, got, sums_half, got_half,
                    ga, sib, slab_half, slab_up, slab_down, slab_last, sum_z, sum_x, sum_y, sum_c,
                    send_sems, recv_sems, sems):
    net = Net(send_sems, recv_sems)
    bf, f32 = jnp.bfloat16, jnp.float32
    loads = [
        pltpu.make_async_copy(src, dst, sems.at[m])
        for m, (src, dst) in enumerate(((da_in, da), (w_in, w), (v_in, v), (p_in, p), (q_in, q), (k_in, k), (o_in, o), (table_in, table), (n1_in, n1)))
    ]
    for copy in loads:
        copy.start()
    line_x = [net.device(dx=s) for s in (1, 2, 3)]
    line_y = [net.device(dy=s) for s in (1, 2, 3)]
    line_z = [net.device(dz=s) for s in (1, 2, 3)]
    net.greet(line_x + line_y + line_z + [net.device(dc=1)])
    for copy in loads[:2]:
        copy.wait()

    def back(i, _):
        here = pl.ds(pl.multiple_of(i * QROWS, QROWS), QROWS)
        u = jnp.dot(da[here, :], w[3], preferred_element_type=f32).astype(bf)
        for h in range(2):
            do[h, here, :] = u[:, h * 128 : h * 128 + 128]
        return 0

    lax.fori_loop(0, GROUP // QROWS, back, 0)
    for copy in loads[2:]:
        copy.wait()
    for h in range(2):
        for b in range(GROUP // QROWS):
            rows = slice(b * QROWS, b * QROWS + QROWS)
            first, last = max(0, b - 2) * QROWS, (b + 1) * QROWS
            keys = slice(first, last)
            old = slice(first, b * QROWS)
            weights_b = p[h, rows, keys]
            do_b = do[h, rows, :]
            dp = lax.dot_general(do_b, v[h, keys, :], NT, preferred_element_type=f32)
            wide = weights_b.astype(f32)
            centre = jnp.sum(wide * dp, axis=-1, keepdims=True)
            ds = (wide * (dp - centre)).astype(bf)
            dvb = lax.dot_general(weights_b, do_b, TN, preferred_element_type=f32)
            dkb = lax.dot_general(ds, q[h, rows, :], TN, preferred_element_type=f32)
            if b > 0:
                dv[h, old, :] += dvb[: b * QROWS - first]
                dk[h, old, :] += dkb[: b * QROWS - first]
            dv[h, rows, :] = dvb[b * QROWS - first :]
            dk[h, rows, :] = dkb[b * QROWS - first :]
            dqb = jnp.dot(ds, k[h, keys, :], preferred_element_type=f32) * HEAD_DIM ** (-0.5)
            dqb = dqb * table[0, rows, :] - pltpu.roll(dqb, 64, 1) * table[1, rows, :]
            dqkv[rows, h * 128 : h * 128 + 128] = dqb.astype(bf)

    def turn(i, _):
        here = pl.ds(pl.multiple_of(i * QROWS, QROWS), QROWS)
        for h in range(2):
            u = dk[h, here, :] * HEAD_DIM ** (-0.5)
            u = u * table[0, here, :] - pltpu.roll(u, 64, 1) * table[1, here, :]
            dqkv[here, 256 + h * 128 : 384 + h * 128] = u.astype(bf)
            dqkv[here, 512 + h * 128 : 640 + h * 128] = dv[h, here, :].astype(bf)
        return 0

    lax.fori_loop(0, GROUP // QROWS, turn, 0)
    sum_z[net.z, 0:1, :] = jnp.zeros((1, D), f32)
    sum_z[net.z, 1:2, :] = mlp_gain_part[...]

    def make(xl, z):
        here = block8(xl, z)
        left = dqkv[here, :]

        def columns(i, _):
            at = pl.ds(pl.multiple_of(i * 512, 512), 512)
            u = lax.dot_general(left[:, :256], w[0, at, :], NT, preferred_element_type=f32)
            u = u + lax.dot_general(left[:, 256:512], w[1, at, :], NT, preferred_element_type=f32)
            u = u + lax.dot_general(left[:, 512:], w[2, at, :], NT, preferred_element_type=f32)
            part[here, at] = u.astype(bf)
            sum_z[net.z, 0:1, at] += jnp.sum(u * n1[here, at].astype(f32), axis=0, keepdims=True)
            return 0

        lax.fori_loop(0, 4, columns, 0)

    def tokens():
        out = []
        yield from reduce_8(net, make, part, sums, got, sums_half, got_half, out)

        def step(at, k):
            here = pl.ds(at, 16)
            value = tok[here, :].astype(f32)
            r = lax.rsqrt(jnp.mean(value * value, axis=-1, keepdims=True) + EPS)
            inner = out[0](at, k) * gain[...]
            dx[here, :] = dh1[here, :] + r * inner - value * (r * r * r) * jnp.mean(value * inner, axis=-1, keepdims=True)

        each_half(step)

    def weights():
        def outer(i, _):
            at = pl.ds(pl.multiple_of(i * 256, 256), 256)
            u = lax.dot_general(dqkv[...], n1[:, at], TN, preferred_element_type=f32)
            for m in range(3):
                ga[m, :, at] = u[m * 256 : m * 256 + 256].astype(bf)
            ga[3, :, at] = lax.dot_general(o[...], da[:, at], TN, preferred_element_type=f32).astype(bf)
            return 0

        lax.fori_loop(0, 8, outer, 0)

        def slab(kind):
            return lambda i, j: ga.at[:, :, att_at(net, kind, i, j)]

        yield from reduce_plane(
            net, slab(net.c), slab(1 - net.c), lambda i, j: sib.at[i, j], lambda i: slab_half.at[i], lambda i: slab_up.at[i],
            lambda i: slab_down.at[i], lambda i: slab_last.at[i], ATT_CUT_T, add_att, (net.across,), (net.device(dy=1), net.device(dy=-1)),
        )
        mine = ga.at[:, :, att_at(net, net.c, 0, 0)]
        for m, dst in enumerate((gq, gk, gv, go)):
            dst[...] = mine[m].astype(f32).T

    def gain_sums():
        here = net.z
        for ref, line, then, place in ((sum_z, line_z, sum_x, net.x), (sum_x, line_x, sum_y, net.y), (sum_y, line_y, sum_c, net.c), (sum_c, [net.device(dc=1)], None, None)):
            sent = [net.send(ref.at[here], ref.at[here], to) for to in line]
            yield
            for copy in sent:
                copy.wait_recv()
            total = ref[0]
            for n in range(1, len(line) + 1):
                total = total + ref[n]
            if then is None:
                gains[0:1, :] = total[0:1] / gain[...]
                gains[1:2, :] = total[1:2]
            else:
                then[place] = total
                here = place

    take_turns({"t": tokens(), "s": gain_sums(), "w": weights()}, "tswtswtswtwsswww")
    net.finish()


def attn_out(da_all, n1_all, w, q, k, v, p, o, table, tok, dh1, gain, mlp_gain_part):
    bf, f32 = jnp.bfloat16, jnp.float32
    slab = (4, 256, 128)
    scratch = [
        ((GROUP, D), bf), ((GROUP, D), bf), ((4, D, 256), bf), ((2, GROUP, 128), bf), ((2, GROUP, 128), bf), ((2, GROUP, 128), bf),
        ((2, GROUP, GROUP), bf), ((GROUP, 256), bf), ((2, GROUP, 128), f32), ((2, GROUP, 128), bf), ((GROUP, 768), bf),
        ((2, GROUP, 128), f32), ((2, GROUP, 128), f32), ((GROUP, D), bf), ((2, ROWS, D), bf), ((4, ROWS, D), bf),
        ((2, 64, D), bf), ((6, 64, D), bf), ((4, 256, D), bf), ((2, 4) + slab, bf), ((2,) + slab, bf), ((2,) + slab, bf),
        ((2,) + slab, bf), ((2,) + slab, bf), ((4, 2, D), f32), ((4, 2, D), f32), ((4, 2, D), f32), ((2, 2, D), f32),
    ]
    return pl.pallas_call(
        attn_out_kernel,
        name="attn_out",
        out_shape=(
            jax.ShapeDtypeStruct((ROWS, D), f32),
            jax.ShapeDtypeStruct((2, D), f32),
        ) + (jax.ShapeDtypeStruct((ROWS, 256), f32),) * 4,
        in_specs=[ANY] * 9 + [VMEM] * 4,
        out_specs=(VMEM,) * 6,
        scratch_shapes=[pltpu.VMEM(*s) for s in scratch] + [
            pltpu.SemaphoreType.DMA((64,)),
            pltpu.SemaphoreType.DMA((64,)),
            pltpu.SemaphoreType.DMA((9,)),
        ],
        compiler_params=pltpu.CompilerParams(collective_id=4, has_side_effects=True, vmem_limit_bytes=58 << 20),
    )(da_all, n1_all, w, q, k, v, p, o, table, tok, dh1, gain, mlp_gain_part)


def shards(
    tokens,
    lengths,
    attn_gain,
    query_weight,
    key_weight,
    value_weight,
    out_weight,
    mlp_gain,
    gate_weight,
    up_weight,
    down_weight,
    cotangent,
):
    half_rates = THETA ** (-(np.arange(64, dtype=np.float32) * np.float32(2.0 / HEAD_DIM)))
    rates = jnp.asarray(np.concatenate([half_rates, half_rates])[None].astype(np.float32))
    g_all, n1_all, w, q, k, v, p, o, table = attn_in(
        tokens, cotangent, lengths, attn_gain[None], rates, query_weight, key_weight, value_weight, out_weight
    )
    w_all, n2_all, h1 = mlp_in(o, w[3], tokens, mlp_gain[None], gate_weight.T, up_weight.T, down_weight.T)
    m_part, dn_part, grads = mlp(w_all, n2_all, g_all)
    output, dh1, da_all, mlp_gain_part, gate_wg, up_wg, down_wg = mlp_out(m_part, dn_part, grads, h1, mlp_gain[None], cotangent)
    dx, gains, gq, gk, gv, go = attn_out(da_all, n1_all, w, q, k, v, p, o, table, tokens, dh1, attn_gain[None], mlp_gain_part)
    return (output, dx, gains[0], gq, gk, gv, go, gains[1], gate_wg.T, up_wg.T, down_wg.T)


def solution(mesh):
    return jax.shard_map(
        shards,
        mesh=mesh,
        in_specs=(
            P(("dp", "tensor"), None),
            P("dp", None),
            P(),
            P("dp", "tensor"),
            P("dp", "tensor"),
            P("dp", "tensor"),
            P("dp", "tensor"),
            P(),
            P("dp", "tensor"),
            P("dp", "tensor"),
            P("dp", "tensor"),
            P(("dp", "tensor"), None),
        ),
        out_specs=(
            P(("dp", "tensor"), None),
            P(("dp", "tensor"), None),
            P(),
            P("dp", "tensor"),
            P("dp", "tensor"),
            P("dp", "tensor"),
            P("dp", "tensor"),
            P(),
            P("dp", "tensor"),
            P("dp", "tensor"),
            P("dp", "tensor"),
        ),
        check_vma=False,
    )
```

```python
import functools

import jax
import jax.numpy as jnp
import numpy as np
from jax import lax
from jax.experimental import pallas as pl
from jax.experimental.pallas import tpu as pltpu
from jax.sharding import PartitionSpec as P

HEAD_DIM = 128
EPS = 1e-05
THETA = 10000.0
D = 2048
ROWS = 128
GROUP = 1024
FFB = 688
QROWS = 256
MESH = pl.DeviceIdType.MESH
ANY = pl.BlockSpec(memory_space=pl.ANY)
VMEM = pl.BlockSpec(memory_space=pltpu.VMEM)
NT = (((1,), (1,)), ((), ()))
TN = (((0,), (0,)), ((), ()))


class Net:
    def __init__(self, send_sems, recv_sems):
        dp, t = lax.axis_index("dp"), lax.axis_index("tensor")
        self.y, self.c = lax.div(dp, 4), lax.rem(dp, 2)
        self.xl, self.z = lax.div(t, 4), lax.rem(t, 4)
        self.x = lax.rem(lax.div(dp, 2), 2) * 2 + self.xl
        self.dp, self.t = dp, t
        self.send_sems, self.recv_sems = send_sems, recv_sems
        self.used = 0
        self.sent = []

    def device(self, dx=0, dy=0, dz=0, dc=0):
        x, y = lax.rem(self.x + dx + 4, 4), lax.rem(self.y + dy + 4, 4)
        z, c = lax.rem(self.z + dz + 4, 4), lax.rem(self.c + dc, 2)
        return (y * 4 + lax.div(x, 2) * 2 + c, lax.rem(x, 2) * 4 + z)

    @property
    def beside(self):
        return (self.dp, (1 - self.xl) * 4 + self.z)

    @property
    def across(self):
        return self.device(dx=2)

    def along(self, first):
        on_x = self.c == (0 if first else 1)
        both = []
        for step in (1, -1):
            by_x, by_y = self.device(dx=step), self.device(dy=step)
            both.append(tuple(jnp.where(on_x, u, v) for u, v in zip(by_x, by_y)))
        return both

    def send(self, src, dst, to):
        k = self.used
        self.used += 1
        copy = pltpu.make_async_remote_copy(
            src_ref=src,
            dst_ref=dst,
            send_sem=self.send_sems.at[k],
            recv_sem=self.recv_sems.at[k],
            device_id=to,
            device_id_type=MESH,
        )
        copy.start()
        self.sent.append(copy)
        return copy

    def flush(self):
        for copy in self.sent:
            copy.wait_send()
        self.sent = []

    def greet(self, devices):
        barrier = pltpu.get_barrier_semaphore()
        for device in devices:
            pl.semaphore_signal(barrier, inc=1, device_id=device, device_id_type=MESH)
        pl.semaphore_wait(barrier, len(devices))


def block(z):
    return pl.ds(pl.multiple_of(lax.rem(z + 8, 4) * ROWS, ROWS), ROWS)


def half(z, k):
    return pl.ds(pl.multiple_of(lax.rem(z + 8, 4) * ROWS + k * 64, 64), 64)


def block8(xl, z):
    return pl.ds(pl.multiple_of((xl * 4 + lax.rem(z + 8, 4)) * ROWS, ROWS), ROWS)


def half8(xl, z, k):
    return pl.ds(pl.multiple_of((xl * 4 + lax.rem(z + 8, 4)) * ROWS + k * 64, 64), 64)


def add_rows(rows, dst, *terms):
    def step(i, _):
        at = pl.ds(pl.multiple_of(i * 16, 16), 16)
        total = terms[0][at, :].astype(jnp.float32)
        for term in terms[1:]:
            total = total + term[at, :].astype(jnp.float32)
        dst[at, :] = total.astype(dst.dtype)
        return 0

    lax.fori_loop(0, rows // 16, step, 0)


def gather_z(net, own, dst, arrived=None):
    up, down = net.device(dz=1), net.device(dz=-1)
    z = net.z
    here = arrived or (lambda z: None)
    a0 = net.send(own, dst.at[block(z), :], up)
    a1 = net.send(own, dst.at[block(z), :], down)
    here(z)
    yield
    a0.wait_recv()
    b0 = net.send(dst.at[half(z - 1, 0), :], dst.at[half(z - 1, 0), :], up)
    a1.wait_recv()
    b1 = net.send(dst.at[half(z + 1, 1), :], dst.at[half(z + 1, 1), :], down)
    here(z - 1)
    here(z + 1)
    yield
    b0.wait_recv()
    b1.wait_recv()
    here(z + 2)


def reduce_z(net, part, sums, got, cols=pl.ds(0, D)):
    up, down = net.device(dz=1), net.device(dz=-1)
    z = net.z
    c0 = net.send(part.at[half(z + 2, 0), cols], got.at[0, :, cols], up)
    c1 = net.send(part.at[half(z + 2, 1), cols], got.at[1, :, cols], down)
    d1 = net.send(part.at[half(z + 1, 1), cols], got.at[3, :, cols], up)
    d2 = net.send(part.at[half(z - 1, 0), cols], got.at[4, :, cols], down)
    yield
    c0.wait_recv()
    add_rows(64, sums.at[0, :, cols], part.at[half(z + 1, 0), cols], got.at[0, :, cols])
    d0 = net.send(sums.at[0, :, cols], got.at[2, :, cols], up)
    c1.wait_recv()
    add_rows(64, sums.at[1, :, cols], part.at[half(z - 1, 1), cols], got.at[1, :, cols])
    d3 = net.send(sums.at[1, :, cols], got.at[5, :, cols], down)
    yield
    for copy in (d0, d1, d2, d3):
        copy.wait_recv()


def reduced(net, part, got, at, k):
    here = pl.ds(pl.multiple_of(at - 64 * k, 16), 16)
    total = part[pl.ds(pl.multiple_of(net.z * ROWS + at, 16), 16), :].astype(jnp.float32)
    return total + got[2 + k, here, :].astype(jnp.float32) + got[4 + k, here, :].astype(jnp.float32)


def gather_8(net, own, dst):
    up, down, beside = net.device(dz=1), net.device(dz=-1), net.beside
    xl, z = net.xl, net.z
    place = dst.at[block8(xl, z), :]
    s0 = net.send(own, place, up)
    s1 = net.send(own, place, down)
    s2 = net.send(own, place, beside)
    yield
    s0.wait_recv()
    ref = dst.at[half8(xl, z - 1, 0), :]
    s5 = net.send(ref, ref, up)
    s1.wait_recv()
    ref = dst.at[half8(xl, z + 1, 1), :]
    s6 = net.send(ref, ref, down)
    s2.wait_recv()
    ref = dst.at[block8(1 - xl, z), :]
    s3 = net.send(ref, ref, up)
    s4 = net.send(ref, ref, down)
    yield
    s5.wait_recv()
    s6.wait_recv()
    ref = dst.at[block8(xl, z + 2), :]
    s7 = net.send(ref, ref, beside)
    yield
    s3.wait_recv()
    s4.wait_recv()
    s7.wait_recv()


def reduce_8(net, make, part, sums, got, sums_half, got_half, out):
    up, down, beside = net.device(dz=1), net.device(dz=-1), net.beside
    xl, z = net.xl, net.z
    make(1 - xl, z + 2)
    a = net.send(part.at[block8(1 - xl, z + 2), :], got.at[0], beside)
    make(1 - xl, z + 1)
    b0 = net.send(part.at[block8(1 - xl, z + 1), :], got.at[1], up)
    make(1 - xl, z - 1)
    b1 = net.send(part.at[block8(1 - xl, z - 1), :], got.at[2], down)
    make(xl, z + 2)
    make(xl, z + 1)
    d1 = net.send(part.at[half8(xl, z + 1, 1), :], got_half.at[3], up)
    make(xl, z - 1)
    d2 = net.send(part.at[half8(xl, z - 1, 0), :], got_half.at[4], down)
    make(1 - xl, z)
    make(xl, z)
    yield
    a.wait_recv()
    add_rows(128, sums.at[0], part.at[block8(xl, z + 2), :], got.at[0])
    c0 = net.send(sums.at[0, pl.ds(0, 64), :], got_half.at[0], up)
    c1 = net.send(sums.at[0, pl.ds(64, 64), :], got_half.at[1], down)
    yield
    b0.wait_recv()
    b1.wait_recv()
    add_rows(128, sums.at[1], part.at[block8(1 - xl, z), :], got.at[1], got.at[2])
    e = net.send(sums.at[1], got.at[3], beside)
    yield
    c0.wait_recv()
    add_rows(64, sums_half.at[0], part.at[half8(xl, z + 1, 0), :], got_half.at[0])
    d0 = net.send(sums_half.at[0], got_half.at[2], up)
    c1.wait_recv()
    add_rows(64, sums_half.at[1], part.at[half8(xl, z - 1, 1), :], got_half.at[1])
    d3 = net.send(sums_half.at[1], got_half.at[5], down)
    yield
    for copy in (e, d0, d1, d2, d3):
        copy.wait_recv()

    def rows(at, k):
        here = pl.ds(pl.multiple_of(at - 64 * k, 16), 16)
        total = part[pl.ds(pl.multiple_of(net.t * ROWS + at, 16), 16), :].astype(jnp.float32)
        total = total + got[3, pl.ds(pl.multiple_of(at, 16), 16), :].astype(jnp.float32)
        return total + got_half[2 + k, here, :].astype(jnp.float32) + got_half[4 + k, here, :].astype(jnp.float32)

    out.append(rows)


def each_half(step):
    for k in (0, 1):
        def body(i, _, k=k):
            step(pl.multiple_of(k * 64 + i * 16, 16), k)
            return 0

        lax.fori_loop(0, 4, body, 0)


def gather_plane(net, slab, cut, first, second):
    low, high = cut
    sib = net.device(dc=1)
    second_up, second_down = second

    def share(i, j):
        ref = slab(i, j)
        return net.send(ref, ref, sib)

    def go(i):
        ref = slab(i, 0)
        return net.send(ref, ref, second_up), net.send(ref, ref, second_down)

    shared, halves = [], {}
    own = slab(0, 0)
    ring = len(first) == 2
    round_ = [net.send(own, own, to) for to in first]
    sent = {0: go(0)}
    shared.append(share(0, 0))

    def on(i):
        sent[i][0].wait_recv()
        ref = low(slab(i, -1))
        h0 = net.send(ref, ref, second_up)
        sent[i][1].wait_recv()
        ref = high(slab(i, 1))
        halves[i] = (h0, net.send(ref, ref, second_down))
        shared.append(share(i, -1))
        shared.append(share(i, 1))

    yield
    if ring:
        round_[0].wait_recv()
        ref = low(slab(-1, 0))
        f0 = net.send(ref, ref, first[0])
        round_[1].wait_recv()
        ref = high(slab(1, 0))
        f1 = net.send(ref, ref, first[1])
        for i in (-1, 1):
            sent[i] = go(i)
            shared.append(share(i, 0))
        yield
        on(0)
        yield
        f0.wait_recv()
        f1.wait_recv()
        sent[2] = go(2)
        shared.append(share(2, 0))
    else:
        round_[0].wait_recv()
        sent[1] = go(1)
        shared.append(share(1, 0))
        yield
        on(0)
    for i in list(sent)[1:]:
        yield
        on(i)
    for i in sent:
        yield
        halves[i][0].wait_recv()
        halves[i][1].wait_recv()
        shared.append(share(i, 2))
    yield
    for copy in shared:
        copy.wait_recv()


def reduce_plane(net, mine, other, from_sib, got_half, got_up, got_down, last_bufs, cut, add, first, second):
    low, high = cut
    sib = net.device(dc=1)
    up, down = second
    ring = len(first) == 2
    steps = (0, 1, 3, 2) if ring else (0, 1)
    shared = {}
    for j in (2, 1, 3, 0):
        for i in steps:
            shared[i, j] = net.send(other(i, j), from_sib(i, j), sib)
    yield
    halves, full = {}, {}
    for i in steps:
        shared[i, 2].wait_recv()
        add(None, mine(i, 2), from_sib(i, 2))
        halves[i] = (
            net.send(low(mine(i, 2)), low(got_half(i)), up),
            net.send(high(mine(i, 2)), high(got_half(i)), down),
        )
        yield
    for i in steps:
        for j in (1, 3):
            shared[i, j].wait_recv()
            add(None, mine(i, j), from_sib(i, j))
        halves[i][0].wait_recv()
        add(0, mine(i, 1), got_half(i))
        u = net.send(mine(i, 1), got_up(i), up)
        halves[i][1].wait_recv()
        add(1, mine(i, 3), got_half(i))
        full[i] = (u, net.send(mine(i, 3), got_down(i), down))
        yield
    last = {}
    for i in reversed(steps):
        shared[i, 0].wait_recv()
        full[i][0].wait_recv()
        full[i][1].wait_recv()
        add(None, mine(i, 0), from_sib(i, 0), got_up(i), got_down(i))
        if ring and i == 2:
            ref, to = mine(2, 0), last_bufs(2)
            last[2] = (net.send(low(ref), low(to), first[0]), net.send(high(ref), high(to), first[1]))
        if ring and i == 3:
            last[2][1].wait_recv()
            add(1, mine(3, 0), last_bufs(2))
            last[3] = net.send(mine(3, 0), last_bufs(1), first[1])
        if ring and i == 1:
            last[2][0].wait_recv()
            add(0, mine(1, 0), last_bufs(2))
        if i == 1:
            last[1] = net.send(mine(1, 0), last_bufs(0), first[0])
        yield
    last[1].wait_recv()
    if ring:
        last[3].wait_recv()
        add(None, mine(0, 0), last_bufs(0), last_bufs(1))
    else:
        add(None, mine(0, 0), last_bufs(0))


ATT_CUT = (lambda ref: ref.at[:, pl.ds(0, 64), :], lambda ref: ref.at[:, pl.ds(64, 64), :])


def add_in(cut, total):
    def add(part, dst, *terms):
        begin, n = {None: (0, total), 0: (0, cut), 1: (cut, total - cut)}[part]

        def piece(at, size):
            here = pl.ds(at, size)
            value = dst[here, :].astype(jnp.float32)
            for term in terms:
                value = value + term[here, :].astype(jnp.float32)
            dst[here, :] = value.astype(dst.dtype)

        def step(i, _):
            piece(pl.multiple_of(begin + i * 160, 16), 160)
            return 0

        lax.fori_loop(0, n // 160, step, 0)
        if n % 160:
            piece(begin + n // 160 * 160, n % 160)

    return add


def cut_at(cut, total):
    return (lambda ref: ref.at[pl.ds(0, cut), :], lambda ref: ref.at[pl.ds(cut, total - cut), :])


OD, OD_CUT = 944, 480
GU, GU_CUT = 1376, 688
QKV, QKV_CUT = 768, 384


def plane_slab(net, ref, kind, i, j):
    x = lax.rem(net.x + jnp.where(kind == 0, i, j) + 4, 4)
    y = lax.rem(net.y + jnp.where(kind == 0, j, i) + 4, 4)
    at = pl.ds(pl.multiple_of((y * 4 + lax.div(x, 2) * 2 + kind) * 128, 128), 128)
    return ref.at[lax.rem(x, 2), :, at]


def att_at(net, kind, i, j):
    x, y = lax.rem(net.x + 2 * i + 4, 4), lax.rem(net.y + j + 4, 4)
    return pl.ds(pl.multiple_of((y * 4 + lax.div(x, 2) * 2 + kind) * 128, 128), 128)


def forward(chain, times=1):
    for _ in range(times):
        next(chain, None)


def end(*chains):
    for chain in chains:
        for _ in chain:
            pass


def start(copies):
    for copy in copies:
        copy.start()
    return copies


def sequence_starts(lengths, at, rows):
    index = lax.broadcasted_iota(jnp.int32, (rows, 1), 0) + at
    limit, first = lengths[0, 0], jnp.zeros((rows, 1), jnp.int32)
    for s in range(8):
        first = jnp.where(index >= limit, limit, first)
        if s < 7:
            limit = limit + lengths[0, s + 1]
    return index, first


def params(collective, mib=58):
    return pltpu.CompilerParams(collective_id=collective, has_side_effects=True, vmem_limit_bytes=mib << 20)


def sems(n, local):
    return [pltpu.SemaphoreType.DMA((n,)), pltpu.SemaphoreType.DMA((n,)), pltpu.SemaphoreType.DMA((local,))]


def attn_in_kernel(tok, cot, lengths, gain, rates, wq, wk, wv, wo, wd,
                   g_all, n1_out, w_out, q_out, k_out, v_out, p_out, table_out, o_out, od_out,
                   n1, wo_turned, n1_all, w, q, k, v, p, table, o, send_sems, recv_sems, local):
    net = Net(send_sems, recv_sems)
    own_rows = att_at(net, net.c, 0, 0)
    own_od = plane_slab(net, od_out, net.c, 0, 0)
    wo_turned[...] = wo[...].T
    copies = start(
        [pltpu.make_async_copy(u, w.at[m, own_rows, :], local.at[m]) for m, u in enumerate((wq, wk, wv))]
        + [
            pltpu.make_async_copy(wo_turned, own_od.at[pl.ds(0, 256), :], local.at[3]),
            pltpu.make_async_copy(wd, own_od.at[pl.ds(256, FFB), :], local.at[4]),
        ]
    )
    saves = start([pltpu.make_async_copy(cot, g_all.at[block(net.z), :], local.at[5])])

    def norm(at, _):
        here = pl.ds(at, 16)
        value = tok[here, :].astype(jnp.float32)
        r = lax.rsqrt(jnp.mean(value * value, axis=-1, keepdims=True) + EPS)
        n1[here, :] = (value * r * gain[...]).astype(jnp.bfloat16)

    each_half(norm)
    net.greet([net.device(dx=s) for s in (1, 2, 3)] + [net.device(dy=1), net.device(dy=-1), net.device(dz=1), net.device(dz=-1), net.device(dc=1)])
    place = pltpu.make_async_copy(n1, n1_all.at[block8(net.xl, net.z), :], local.at[6])
    place.start()
    tokens = gather_8(net, n1, n1_all)
    cotangent = gather_z(net, cot, g_all)
    weights = gather_plane(net, lambda i, j: w.at[:, att_at(net, net.c, i, j), :], ATT_CUT, (net.across,), (net.device(dy=1), net.device(dy=-1)))
    later = gather_plane(net, lambda i, j: plane_slab(net, od_out, net.c, i, j), cut_at(OD_CUT, OD), net.along(True), net.along(False))
    forward(tokens)
    for copy in copies:
        copy.wait()
    forward(weights)
    forward(later)

    def tables(i, _):
        at = pl.multiple_of(i * 128, 128)
        index, first = sequence_starts(lengths, at, 128)
        angle = (index - first).astype(jnp.float32) * rates[...]
        lane = lax.broadcasted_iota(jnp.int32, (128, 128), 1)
        table[0, pl.ds(at, 128), :] = jnp.cos(angle)
        sin = jnp.sin(angle)
        table[1, pl.ds(at, 128), :] = jnp.where(lane < 64, -sin, sin)
        return 0

    lax.fori_loop(0, 8, tables, 0)
    forward(tokens)
    forward(weights)
    forward(tokens)
    forward(weights, 2)
    forward(later)
    end(tokens)
    place.wait()
    forward(cotangent)
    end(weights)
    saves += start(
        [
            pltpu.make_async_copy(n1_all, n1_out, local.at[7]),
            pltpu.make_async_copy(w, w_out, local.at[8]),
            pltpu.make_async_copy(table, table_out, local.at[9]),
        ]
    )

    def project(i, _):
        here = pl.ds(pl.multiple_of(i * QROWS, QROWS), QROWS)
        left = n1_all[here, :]
        cos, sin = table[0, here, :], table[1, here, :]
        for m, dst in ((0, q), (1, k)):
            u = jnp.dot(left, w[m], preferred_element_type=jnp.float32)
            for h in range(2):
                uh = u[:, h * 128 : h * 128 + 128]
                dst[h, here, :] = (uh * cos + pltpu.roll(uh, 64, 1) * sin).astype(jnp.bfloat16)
        u = jnp.dot(left, w[2], preferred_element_type=jnp.float32).astype(jnp.bfloat16)
        for h in range(2):
            v[h, here, :] = u[:, h * 128 : h * 128 + 128]
        return 0

    lax.fori_loop(0, GROUP // QROWS, project, 0)
    saves += start([pltpu.make_async_copy(src, dst, local.at[10 + n]) for n, (src, dst) in enumerate(((q, q_out), (k, k_out), (v, v_out)))])
    forward(later)
    forward(cotangent)

    def attend(b):
        rows = slice(b * QROWS, b * QROWS + QROWS)
        first, last = max(0, b - 2) * QROWS, (b + 1) * QROWS
        index, begin = sequence_starts(lengths, b * QROWS, QROWS)
        key = lax.broadcasted_iota(jnp.int32, (QROWS, last - first), 1) + first
        allowed = (key <= index) & (key >= begin)
        for h in range(2):
            s = lax.dot_general(q[h, rows, :], k[h, first:last, :], NT, preferred_element_type=jnp.float32)
            s = jnp.where(allowed, s * HEAD_DIM ** (-0.5), -1e30)
            e = jnp.exp(s - jnp.max(s, axis=-1, keepdims=True))
            weights_b = (e / jnp.sum(e, axis=-1, keepdims=True)).astype(jnp.bfloat16)
            p[h, rows, first:last] = weights_b
            o[rows, h * 128 : h * 128 + 128] = jnp.dot(
                weights_b, v[h, first:last, :], preferred_element_type=jnp.float32
            ).astype(jnp.bfloat16)
        at = (slice(None), pl.ds(b * QROWS, QROWS), pl.ds(first, last - first))
        saves.extend(start([pltpu.make_async_copy(p.at[at], p_out.at[at], local.at[13 + b])]))

    def exchange(n):
        src = o.at[pl.ds(pl.multiple_of((1 - net.xl) * 512 + n * QROWS, QROWS), QROWS), :]
        return net.send(src, o_out.at[net.xl, pl.ds(n * QROWS, QROWS), :], net.beside)

    attend(0)
    forward(later)
    attend(2)
    turn = [exchange(0)]
    forward(later)
    attend(1)
    forward(later)
    attend(3)
    turn.append(exchange(1))
    kept = o.at[pl.ds(pl.multiple_of(net.xl * 512, 512), 512), :]
    saves += start([pltpu.make_async_copy(kept, o_out.at[net.xl], local.at[17])])
    end(later, cotangent)
    for copy in turn:
        copy.wait_recv()
    for copy in saves:
        copy.wait()
    net.flush()


def attn_in(tok, cot, lengths, gain, rates, wq, wk, wv, wo, wd):
    bf, f32 = jnp.bfloat16, jnp.float32
    shapes = (
        ((4 * ROWS, D), bf), ((GROUP, D), bf), ((3, D, 256), bf), ((2, GROUP, 128), bf), ((2, GROUP, 128), bf),
        ((2, GROUP, 128), bf), ((2, GROUP, GROUP), bf), ((2, GROUP, 128), f32), ((2, 512, 256), bf), ((2, OD, D), bf),
    )
    return pl.pallas_call(
        attn_in_kernel,
        name="attn_in",
        out_shape=tuple(jax.ShapeDtypeStruct(*s) for s in shapes),
        in_specs=[VMEM, VMEM, pl.BlockSpec(memory_space=pltpu.SMEM), VMEM, VMEM, ANY, ANY, ANY, VMEM, ANY],
        out_specs=(ANY,) * 10,
        scratch_shapes=[pltpu.VMEM((ROWS, D), bf), pltpu.VMEM((256, 128), bf)] + [pltpu.VMEM(*s) for s in shapes[1:8]] + [pltpu.VMEM((GROUP, 256), bf)] + sems(80, 18),
        compiler_params=params(3),
    )(tok, cot, lengths, gain, rates, wq, wk, wv, wo, wd)


def mlp_kernel(o_in, od_in, wg, wu, tok, cot, g_in, gain,
               h1, dh1, do_out, m_out, od_grad, gain_part, gu_grad,
               w1, w2, o, n2, g, part, m_part, hid, dgate, dup, turned, da, do, sums_a, got_a, sums_d, got_d,
               sib, got_half, got_up, got_down, last, send_sems, recv_sems, local):
    net = Net(send_sems, recv_sems)
    bf, f32 = jnp.bfloat16, jnp.float32
    own = plane_slab(net, w2, net.c, 0, 0)
    early = start(
        [pltpu.make_async_copy(o_in, o, local.at[0]), pltpu.make_async_copy(od_in.at[:, pl.ds(0, 256), :], w1.at[:, pl.ds(0, 256), :], local.at[1])]
    )
    copies = start([pltpu.make_async_copy(u, own.at[pl.ds(n * FFB, FFB), :], local.at[2 + n]) for n, u in enumerate((wg, wu))])
    late = start(
        [pltpu.make_async_copy(g_in, g, local.at[4]), pltpu.make_async_copy(od_in.at[:, pl.ds(256, FFB), :], w1.at[:, pl.ds(256, FFB), :], local.at[5])]
    )
    net.greet([net.device(dx=1), net.device(dx=-1), net.device(dy=1), net.device(dy=-1), net.device(dz=1), net.device(dz=-1), net.device(dc=1)])
    for copy in early:
        copy.wait()

    def branch(z):
        here = block(z)
        u = jnp.dot(o[0, here, :], w1[0, :256, :], preferred_element_type=f32)
        u = u + jnp.dot(o[1, here, :], w1[1, :256, :], preferred_element_type=f32)
        part[here, :] = u.astype(bf)

    for step in (2, 1, -1, 0):
        branch(net.z + step)
    summed = reduce_z(net, part, sums_a, got_a)
    forward(summed)
    for copy in copies:
        copy.wait()
    weights = gather_plane(net, lambda i, j: plane_slab(net, w2, net.c, i, j), cut_at(GU_CUT, GU), net.along(True), net.along(False))
    forward(weights)
    for copy in late:
        copy.wait()

    def hidden_grad(b):
        for at, n in TILES:
            u = lax.dot_general(g[...], w1[b, 256 + at : 256 + at + n, :], NT, preferred_element_type=f32)
            dgate[b, :, at : at + n] = u.astype(bf)

    hidden_grad(0)
    forward(summed)
    forward(weights)
    hidden_grad(1)
    forward(weights)
    end(summed)

    def norm(at, k):
        here = pl.ds(at, 16)
        h = tok[here, :].astype(f32) + reduced(net, part, got_a, at, k)
        h1[here, :] = h
        r = lax.rsqrt(jnp.mean(h * h, axis=-1, keepdims=True) + EPS)
        n2[pl.ds(pl.multiple_of(net.z * ROWS + at, 16), 16), :] = (h * r * gain[...]).astype(bf)

    each_half(norm)
    normed = gather_z(net, n2.at[block(net.z), :], n2)
    forward(normed)
    forward(weights, 2)
    forward(normed)
    forward(weights, 3)
    end(normed)
    end(weights)
    net.flush()

    def ahead(b, _):
        for at, n in TILES:
            gate = lax.dot_general(n2[...], w2[b, at : at + n, :], NT, preferred_element_type=f32)
            up = lax.dot_general(n2[...], w2[b, FFB + at : FFB + at + n, :], NT, preferred_element_type=f32)
            dh = dgate[b, :, at : at + n].astype(f32)
            sig = jax.nn.sigmoid(gate)
            act = gate * sig
            for k, (dst, value) in enumerate(
                ((dgate, dh * up * sig * (1.0 + gate * (1.0 - sig))), (dup, dh * act), (hid, act * up))
            ):
                value = value.astype(bf)
                dst[b, :, at : at + n] = value
                turned[k, b, at : at + n, :] = value.T
        return 0

    lax.fori_loop(0, 2, ahead, 0)

    def back(i, _):
        at = pl.ds(pl.multiple_of(i * 256, 256), 256)
        d = jnp.dot(dgate[0], w2[0, :FFB, at], preferred_element_type=f32)
        d = d + jnp.dot(dgate[1], w2[1, :FFB, at], preferred_element_type=f32)
        d = d + jnp.dot(dup[0], w2[0, FFB:, at], preferred_element_type=f32)
        d = d + jnp.dot(dup[1], w2[1, FFB:, at], preferred_element_type=f32)
        part[:, at] = d.astype(bf)
        return 0

    lax.fori_loop(0, 4, back, 0)
    back_a = reduce_z(net, part, sums_d, got_d, pl.ds(0, D // 2))
    forward(back_a)
    lax.fori_loop(4, 8, back, 0)
    back_b = reduce_z(net, part, sums_d, got_d, pl.ds(D // 2, D // 2))
    forward(back_b)

    def outer(i, _):
        at = pl.ds(pl.multiple_of(i * 512, 512), 512)
        right = n2[:, at]
        for m in range(2):
            for b in range(2):
                w2[b, m * FFB : m * FFB + FFB, at] = jnp.dot(turned[m, b], right, preferred_element_type=f32).astype(bf)
        return 0

    lax.fori_loop(0, 4, outer, 0)
    grads = reduce_plane(
        net, lambda i, j: plane_slab(net, w2, net.c, i, j), lambda i, j: plane_slab(net, w2, 1 - net.c, i, j), lambda i, j: sib.at[i, j],
        lambda i: got_half.at[i], lambda i: got_up.at[i], lambda i: got_down.at[i], lambda i: last.at[i],
        cut_at(GU_CUT, GU), add_in(GU_CUT, GU), net.along(True), net.along(False),
    )
    forward(grads)
    forward(back_a)

    def mixed_part(i, _):
        at = pl.ds(pl.multiple_of(i * 256, 256), 256)
        u = jnp.dot(hid[0], w1[0, 256:, at], preferred_element_type=f32)
        u = u + jnp.dot(hid[1], w1[1, 256:, at], preferred_element_type=f32)
        m_part[:, at] = u.astype(bf)
        return 0

    lax.fori_loop(0, 8, mixed_part, 0)
    saves = start([pltpu.make_async_copy(m_part, m_out, local.at[6])])
    forward(back_b)
    forward(grads, 2)

    def outer_down(i, _):
        at = pl.ds(pl.multiple_of(i * 512, 512), 512)
        for b in range(2):
            w1[b, 256:, at] = jnp.dot(turned[2, b], g[:, at], preferred_element_type=f32).astype(bf)
        return 0

    lax.fori_loop(0, 4, outer_down, 0)
    saves += start([pltpu.make_async_copy(w1.at[:, pl.ds(256, FFB), :], od_grad.at[:, pl.ds(256, FFB), :], local.at[7])])
    forward(grads, 2)
    end(back_a, back_b)
    gain_part[...] = jnp.zeros_like(gain_part)

    def norm_back(at, k):
        here = pl.ds(at, 16)
        h = h1[here, :]
        r = lax.rsqrt(jnp.mean(h * h, axis=-1, keepdims=True) + EPS)
        d = reduced(net, part, got_d, at, k)
        inner = d * gain[...]
        grad = r * inner - h * (r * r * r) * jnp.mean(h * inner, axis=-1, keepdims=True)
        grad = cot[here, :].astype(f32) + grad
        dh1[here, :] = grad
        da[pl.ds(pl.multiple_of(net.z * ROWS + at, 16), 16), :] = grad.astype(bf)
        gain_part[...] += jnp.sum(d * h * r, axis=0, keepdims=True)

    each_half(norm_back)
    turn = []

    def back_out(z):
        here = block(z)
        for b in range(2):
            do[b, here, :] = lax.dot_general(da[here, :], w1[b, :256, :], NT, preferred_element_type=f32).astype(bf)
        rows = pl.ds(pl.multiple_of(net.xl * 512 + lax.rem(z + 8, 4) * ROWS, ROWS), ROWS)
        turn.append(net.send(do.at[1 - net.xl, here, :], do_out.at[rows, :], net.beside))
        saves.extend(start([pltpu.make_async_copy(do.at[net.xl, here, :], do_out.at[rows, :], local.at[8 + len(turn)])]))

    branch_grad = gather_z(net, da.at[block(net.z), :], da, back_out)
    forward(branch_grad)
    forward(grads, 2)
    forward(branch_grad)
    forward(grads, 2)
    end(branch_grad)

    def outer_out(i, _):
        at = pl.ds(pl.multiple_of(i * 512, 512), 512)
        for b in range(2):
            w1[b, :256, at] = lax.dot_general(o[b], da[:, at], TN, preferred_element_type=f32).astype(bf)
        return 0

    lax.fori_loop(0, 4, outer_out, 0)
    saves += start([pltpu.make_async_copy(w1.at[:, pl.ds(0, 256), :], od_grad.at[:, pl.ds(0, 256), :], local.at[8])])
    end(grads)
    gu_grad[...] = plane_slab(net, w2, net.c, 0, 0)[...]
    for copy in turn:
        copy.wait_recv()
    for copy in saves:
        copy.wait()
    net.flush()


TILES = ((0, 256), (256, 256), (512, 176))


def mlp(o, od, wg, wu, tok, cot, g_all, gain):
    bf, f32 = jnp.bfloat16, jnp.float32
    slab = (GU, 128)
    scratch = [
        ((2, OD, D), bf), ((2, GU, D), bf), ((2, 512, 256), bf), ((512, D), bf), ((512, D), bf), ((512, D), bf), ((512, D), bf),
        ((2, 512, FFB), bf), ((2, 512, FFB), bf), ((2, 512, FFB), bf), ((3, 2, FFB, 512), bf), ((512, D), bf), ((2, 512, 256), bf),
        ((2, 64, D), bf), ((6, 64, D), bf), ((2, 64, D), bf), ((6, 64, D), bf),
        ((4, 4) + slab, bf), ((4,) + slab, bf), ((4,) + slab, bf), ((4,) + slab, bf), ((3,) + slab, bf),
    ]
    outs = (((ROWS, D), f32), ((ROWS, D), f32), ((GROUP, 256), bf), ((512, D), bf), ((2, OD, D), bf), ((1, D), f32), (slab, bf))
    return pl.pallas_call(
        mlp_kernel,
        name="mlp",
        out_shape=tuple(jax.ShapeDtypeStruct(*s) for s in outs),
        in_specs=[ANY, ANY, ANY, ANY, VMEM, VMEM, ANY, VMEM],
        out_specs=(VMEM, VMEM, ANY, ANY, ANY, VMEM, VMEM),
        scratch_shapes=[pltpu.VMEM(*s) for s in scratch] + sems(112, 13),
        compiler_params=params(1, 62),
    )(o, od, wg, wu, tok, cot, g_all, gain)


def attn_out_kernel(do_in, n1_in, w_in, q_in, k_in, v_in, p_in, table_in, m_in, od_in, tok, h1, dh1, gain, mlp_gain_part,
                    mixed, dx, gains, qkv_grad, od_grad,
                    do, n1, w, q, k, v, p, table, dqkv, dk, dv, part, sums, got, sums_half, got_half,
                    ga, sib, slab_half, slab_up, slab_down, slab_last, sum_z, sum_x, sum_y, sum_c,
                    m_part, sums_m, got_m, od, od_sib, od_half, od_up, od_down, od_last,
                    send_sems, recv_sems, local):
    net = Net(send_sems, recv_sems)
    bf, f32 = jnp.bfloat16, jnp.float32
    loads = start(
        [
            pltpu.make_async_copy(src, dst, local.at[m])
            for m, (src, dst) in enumerate(((do_in, do), (v_in, v), (p_in, p), (q_in, q), (k_in, k), (table_in, table), (m_in, m_part), (w_in, w), (n1_in, n1)))
        ]
    )
    slabs = start(
        [
            pltpu.make_async_copy(plane_slab(net, od_in, net.c, i, j), od.at[i, j], local.at[9 + n])
            for n, (i, j) in enumerate((i, j) for j in (2, 1, 3, 0) for i in (0, 1, 3, 2))
        ]
    )
    line_x = [net.device(dx=s) for s in (1, 2, 3)]
    line_y = [net.device(dy=s) for s in (1, 2, 3)]
    line_z = [net.device(dz=s) for s in (1, 2, 3)]
    net.greet(line_x + line_y + line_z + [net.device(dc=1)])
    early = reduce_plane(
        net, lambda i, j: od.at[i, j], lambda i, j: plane_slab(net, od_in, 1 - net.c, i, j), lambda i, j: od_sib.at[i, j],
        lambda i: od_half.at[i], lambda i: od_up.at[i], lambda i: od_down.at[i], lambda i: od_last.at[i],
        cut_at(OD_CUT, OD), add_in(OD_CUT, OD), net.along(True), net.along(False),
    )
    forward(early)
    for copy in loads[:7]:
        copy.wait()
    mixing = reduce_z(net, m_part, sums_m, got_m)
    forward(mixing)
    for copy in slabs:
        copy.wait()
    forward(early, 2)

    def attend_back(h, b):
        rows = slice(b * QROWS, b * QROWS + QROWS)
        first, last = max(0, b - 2) * QROWS, (b + 1) * QROWS
        keys, old = slice(first, last), slice(first, b * QROWS)
        weights_b = p[h, rows, keys]
        do_b = do[rows, h * 128 : h * 128 + 128]
        dp = lax.dot_general(do_b, v[h, keys, :], NT, preferred_element_type=f32)
        wide = weights_b.astype(f32)
        centre = jnp.sum(wide * dp, axis=-1, keepdims=True)
        ds = (wide * (dp - centre)).astype(bf)
        dvb = lax.dot_general(weights_b, do_b, TN, preferred_element_type=f32)
        dkb = lax.dot_general(ds, q[h, rows, :], TN, preferred_element_type=f32)
        if b > 0:
            dv[h, old, :] += dvb[: b * QROWS - first]
            dk[h, old, :] += dkb[: b * QROWS - first]
        dv[h, rows, :] = dvb[b * QROWS - first :]
        dk[h, rows, :] = dkb[b * QROWS - first :]
        dqb = jnp.dot(ds, k[h, keys, :], preferred_element_type=f32) * HEAD_DIM ** (-0.5)
        dqb = dqb * table[0, rows, :] - pltpu.roll(dqb, 64, 1) * table[1, rows, :]
        dqkv[rows, h * 128 : h * 128 + 128] = dqb.astype(bf)

    for b in range(GROUP // QROWS):
        for h in range(2):
            attend_back(h, b)
        forward(early)
        if b == 1:
            forward(mixing)

    def turn(i, _):
        here = pl.ds(pl.multiple_of(i * QROWS, QROWS), QROWS)
        for h in range(2):
            u = dk[h, here, :] * HEAD_DIM ** (-0.5)
            u = u * table[0, here, :] - pltpu.roll(u, 64, 1) * table[1, here, :]
            dqkv[here, 256 + h * 128 : 384 + h * 128] = u.astype(bf)
            dqkv[here, 512 + h * 128 : 640 + h * 128] = dv[h, here, :].astype(bf)
        return 0

    lax.fori_loop(0, GROUP // QROWS, turn, 0)
    for copy in loads[7:]:
        copy.wait()
    sum_z[net.z, 0:1, :] = jnp.zeros((1, D), f32)
    sum_z[net.z, 1:2, :] = mlp_gain_part[...]

    def make(xl, z):
        here = block8(xl, z)
        left = dqkv[here, :]

        def columns(i, _):
            at = pl.ds(pl.multiple_of(i * 512, 512), 512)
            u = lax.dot_general(left[:, :256], w[0, at, :], NT, preferred_element_type=f32)
            u = u + lax.dot_general(left[:, 256:512], w[1, at, :], NT, preferred_element_type=f32)
            u = u + lax.dot_general(left[:, 512:], w[2, at, :], NT, preferred_element_type=f32)
            part[here, at] = u.astype(bf)
            sum_z[net.z, 0:1, at] += jnp.sum(u * n1[here, at].astype(f32), axis=0, keepdims=True)
            return 0

        lax.fori_loop(0, 4, columns, 0)

    out = []
    tokens = reduce_8(net, make, part, sums, got, sums_half, got_half, out)
    forward(tokens)

    def outer(i, _):
        at = pl.ds(pl.multiple_of(i * 256, 256), 256)
        ga[:, at] = lax.dot_general(dqkv[...], n1[:, at], TN, preferred_element_type=f32).astype(bf)
        return 0

    lax.fori_loop(0, 8, outer, 0)

    def slab(kind):
        return lambda i, j: ga.at[:, att_at(net, kind, i, j)]

    weights = reduce_plane(
        net, slab(net.c), slab(1 - net.c), lambda i, j: sib.at[i, j], lambda i: slab_half.at[i], lambda i: slab_up.at[i],
        lambda i: slab_down.at[i], lambda i: slab_last.at[i], cut_at(QKV_CUT, QKV), add_in(QKV_CUT, QKV), (net.across,), (net.device(dy=1), net.device(dy=-1)),
    )

    def gain_sums():
        here = net.z
        for ref, line, then, place in ((sum_z, line_z, sum_x, net.x), (sum_x, line_x, sum_y, net.y), (sum_y, line_y, sum_c, net.c), (sum_c, [net.device(dc=1)], None, None)):
            sent = [net.send(ref.at[here], ref.at[here], to) for to in line]
            yield
            for copy in sent:
                copy.wait_recv()
            total = ref[0]
            for n in range(1, len(line) + 1):
                total = total + ref[n]
            if then is None:
                gains[0:1, :] = total[0:1] / gain[...]
                gains[1:2, :] = total[1:2]
            else:
                then[place] = total
                here = place

    sums_of_gains = gain_sums()
    forward(tokens)
    forward(weights)
    forward(sums_of_gains)
    forward(early)
    forward(tokens)
    forward(weights)
    forward(early)
    forward(sums_of_gains)
    forward(tokens)
    forward(weights)
    end(mixing)

    def mix(at, k):
        here = pl.ds(at, 16)
        mixed[here, :] = (h1[here, :] + reduced(net, m_part, got_m, at, k)).astype(bf)

    each_half(mix)
    forward(sums_of_gains)
    forward(weights)
    end(early)
    od_grad[...] = od[0, 0]
    forward(sums_of_gains)
    end(tokens)

    def step(at, k):
        here = pl.ds(at, 16)
        value = tok[here, :].astype(f32)
        r = lax.rsqrt(jnp.mean(value * value, axis=-1, keepdims=True) + EPS)
        inner = out[0](at, k) * gain[...]
        dx[here, :] = dh1[here, :] + r * inner - value * (r * r * r) * jnp.mean(value * inner, axis=-1, keepdims=True)

    each_half(step)
    end(weights, sums_of_gains)
    qkv_grad[...] = slab(net.c)(0, 0)[...]
    net.flush()


def attn_out(do, n1, w, q, k, v, p, table, m, od, tok, h1, dh1, gain, mlp_gain_part):
    bf, f32 = jnp.bfloat16, jnp.float32
    slab, slab_od = (QKV, 128), (OD, 128)
    scratch = [
        ((GROUP, 256), bf), ((GROUP, D), bf), ((3, D, 256), bf), ((2, GROUP, 128), bf), ((2, GROUP, 128), bf), ((2, GROUP, 128), bf),
        ((2, GROUP, GROUP), bf), ((2, GROUP, 128), f32), ((GROUP, QKV), bf),
        ((2, GROUP, 128), f32), ((2, GROUP, 128), f32), ((GROUP, D), bf), ((2, ROWS, D), bf), ((4, ROWS, D), bf),
        ((2, 64, D), bf), ((6, 64, D), bf), ((QKV, D), bf), ((2, 4) + slab, bf), ((2,) + slab, bf), ((2,) + slab, bf),
        ((2,) + slab, bf), ((1,) + slab, bf), ((4, 2, D), f32), ((4, 2, D), f32), ((4, 2, D), f32), ((2, 2, D), f32),
        ((512, D), bf), ((2, 64, D), bf), ((6, 64, D), bf), ((4, 4) + slab_od, bf), ((4, 4) + slab_od, bf),
        ((4,) + slab_od, bf), ((4,) + slab_od, bf), ((4,) + slab_od, bf), ((3,) + slab_od, bf),
    ]
    outs = (((ROWS, D), bf), ((ROWS, D), f32), ((2, D), f32), (slab, bf), (slab_od, bf))
    return pl.pallas_call(
        attn_out_kernel,
        name="attn_out",
        out_shape=tuple(jax.ShapeDtypeStruct(*s) for s in outs),
        in_specs=[ANY] * 10 + [VMEM] * 5,
        out_specs=(VMEM,) * 5,
        scratch_shapes=[pltpu.VMEM(*s) for s in scratch] + sems(112, 25),
        compiler_params=params(4),
    )(do, n1, w, q, k, v, p, table, m, od, tok, h1, dh1, gain, mlp_gain_part)


def finish_kernel(mixed_in, dx_in, gains, qkv, od, gu, mixed, dx, ag, gq, gk, gv, go, mg, gg, gu_out, gd):
    f32 = jnp.float32
    mixed[...] = mixed_in[...]
    dx[...] = dx_in[...]
    ag[...] = gains[0:1, :]
    mg[...] = gains[1:2, :]
    for n, dst in enumerate((gq, gk, gv)):
        dst[...] = qkv[n * 256 : n * 256 + 256, :].astype(f32).T
    go[...] = od[:256, :].astype(f32).T
    gd[...] = od[256:, :].astype(f32)
    gg[...] = gu[:FFB, :].astype(f32)
    gu_out[...] = gu[FFB:, :].astype(f32)


def finish(mixed, dx, gains, qkv, od, gu):
    f32 = jnp.float32
    outs = (
        ((ROWS, D), jnp.bfloat16), ((ROWS, D), f32), ((1, D), f32), ((ROWS, 256), f32), ((ROWS, 256), f32), ((ROWS, 256), f32),
        ((ROWS, 256), f32), ((1, D), f32), ((FFB, 128), f32), ((FFB, 128), f32), ((FFB, 128), f32),
    )
    return pl.pallas_call(
        finish_kernel,
        name="finish",
        out_shape=tuple(jax.ShapeDtypeStruct(*s) for s in outs),
        in_specs=[VMEM] * 6,
        out_specs=(VMEM,) * 11,
        compiler_params=pltpu.CompilerParams(vmem_limit_bytes=32 << 20),
    )(mixed, dx, gains, qkv, od, gu)


def shards(
    tokens,
    lengths,
    attn_gain,
    query_weight,
    key_weight,
    value_weight,
    out_weight,
    mlp_gain,
    gate_weight,
    up_weight,
    down_weight,
    cotangent,
):
    half_rates = THETA ** (-(np.arange(64, dtype=np.float32) * np.float32(2.0 / HEAD_DIM)))
    rates = jnp.asarray(np.concatenate([half_rates, half_rates])[None].astype(np.float32))
    g_all, n1_all, w, q, k, v, p, table, o, od = attn_in(
        tokens, cotangent, lengths, attn_gain[None], rates, query_weight, key_weight, value_weight, out_weight, down_weight.T
    )
    h1, dh1, do, m, od_part, gain_part, gu = mlp(o, od, gate_weight.T, up_weight.T, tokens, cotangent, g_all, mlp_gain[None])
    mixed, dx, gains, qkv, od_grad = attn_out(do, n1_all, w, q, k, v, p, table, m, od_part, tokens, h1, dh1, attn_gain[None], gain_part)
    mixed, dx, ag, gq, gk, gv, go, mg, gg, gu, gd = finish(mixed, dx, gains, qkv, od_grad, gu)
    return (mixed, dx, ag[0], gq, gk, gv, go, mg[0], gg.T, gu.T, gd.T)


def solution(mesh):
    return jax.shard_map(
        shards,
        mesh=mesh,
        in_specs=(
            P(("dp", "tensor"), None),
            P("dp", None),
            P(),
            P("dp", "tensor"),
            P("dp", "tensor"),
            P("dp", "tensor"),
            P("dp", "tensor"),
            P(),
            P("dp", "tensor"),
            P("dp", "tensor"),
            P("dp", "tensor"),
            P(("dp", "tensor"), None),
        ),
        out_specs=(
            P(("dp", "tensor"), None),
            P(("dp", "tensor"), None),
            P(),
            P("dp", "tensor"),
            P("dp", "tensor"),
            P("dp", "tensor"),
            P("dp", "tensor"),
            P(),
            P("dp", "tensor"),
            P("dp", "tensor"),
            P("dp", "tensor"),
        ),
        check_vma=False,
    )
```

```python
import copy
import functools

import jax
import jax.numpy as jnp
import numpy as np
from jax import lax
from jax.experimental import pallas as pl
from jax.experimental.pallas import tpu as pltpu
from jax.sharding import PartitionSpec as P

HEAD_DIM = 128
EPS = 1e-05
THETA = 10000.0
D = 2048
ROWS = 128
GROUP = 1024
FFB = 688
QROWS = 256
MESH = pl.DeviceIdType.MESH
ANY = pl.BlockSpec(memory_space=pl.ANY)
VMEM = pl.BlockSpec(memory_space=pltpu.VMEM)
NT = (((1,), (1,)), ((), ()))
TN = (((0,), (0,)), ((), ()))


class Net:
    def __init__(self, send_sems, recv_sems):
        dp, t = lax.axis_index("dp"), lax.axis_index("tensor")
        self.y, self.c = lax.div(dp, 4), lax.rem(dp, 2)
        self.xl, self.z = lax.div(t, 4), lax.rem(t, 4)
        self.x = lax.rem(lax.div(dp, 2), 2) * 2 + self.xl
        self.dp, self.t = dp, t
        self.send_sems, self.recv_sems = send_sems, recv_sems
        self.used = [0]
        self.sent = []
        self.lanes = [self]

    def lane(self):
        other = copy.copy(self)
        other.sent = []
        self.lanes.append(other)
        return other

    def device(self, dx=0, dy=0, dz=0, dc=0):
        x, y = lax.rem(self.x + dx + 4, 4), lax.rem(self.y + dy + 4, 4)
        z, c = lax.rem(self.z + dz + 4, 4), lax.rem(self.c + dc, 2)
        return (y * 4 + lax.div(x, 2) * 2 + c, lax.rem(x, 2) * 4 + z)

    @property
    def beside(self):
        return (self.dp, (1 - self.xl) * 4 + self.z)

    @property
    def across(self):
        return self.device(dx=2)

    def along(self, first):
        on_x = self.c == (0 if first else 1)
        both = []
        for step in (1, -1):
            by_x, by_y = self.device(dx=step), self.device(dy=step)
            both.append(tuple(jnp.where(on_x, u, v) for u, v in zip(by_x, by_y)))
        return both

    def send(self, src, dst, to):
        k = self.used[0]
        self.used[0] += 1
        sent = pltpu.make_async_remote_copy(
            src_ref=src,
            dst_ref=dst,
            send_sem=self.send_sems.at[k],
            recv_sem=self.recv_sems.at[k],
            device_id=to,
            device_id_type=MESH,
        )
        sent.start()
        self.sent.append(sent)
        return sent

    def flush(self):
        for sent in self.sent:
            sent.wait_send()
        self.sent.clear()

    def finish(self):
        for lane in self.lanes:
            lane.flush()

    def greet(self, devices):
        barrier = pltpu.get_barrier_semaphore()
        for device in devices:
            pl.semaphore_signal(barrier, inc=1, device_id=device, device_id_type=MESH)
        pl.semaphore_wait(barrier, len(devices))


def block(z):
    return pl.ds(pl.multiple_of(lax.rem(z + 8, 4) * ROWS, ROWS), ROWS)


def half(z, k):
    return pl.ds(pl.multiple_of(lax.rem(z + 8, 4) * ROWS + k * 64, 64), 64)


def block8(xl, z):
    return pl.ds(pl.multiple_of((xl * 4 + lax.rem(z + 8, 4)) * ROWS, ROWS), ROWS)


def half8(xl, z, k):
    return pl.ds(pl.multiple_of((xl * 4 + lax.rem(z + 8, 4)) * ROWS + k * 64, 64), 64)


def add_rows(rows, dst, *terms):
    def step(i, _):
        at = pl.ds(pl.multiple_of(i * 16, 16), 16)
        total = terms[0][at, :].astype(jnp.float32)
        for term in terms[1:]:
            total = total + term[at, :].astype(jnp.float32)
        dst[at, :] = total.astype(dst.dtype)
        return 0

    lax.fori_loop(0, rows // 16, step, 0)


def gather_z(net, own, dst, arrived=lambda z: None):
    up, down = net.device(dz=1), net.device(dz=-1)
    z = net.z
    a0 = net.send(own, dst.at[block(z), :], up)
    a1 = net.send(own, dst.at[block(z), :], down)
    arrived(z)
    yield
    a0.wait_recv()
    b0 = net.send(dst.at[half(z - 1, 0), :], dst.at[half(z - 1, 0), :], up)
    arrived(z - 1)
    yield
    a1.wait_recv()
    b1 = net.send(dst.at[half(z + 1, 1), :], dst.at[half(z + 1, 1), :], down)
    arrived(z + 1)
    yield
    b0.wait_recv()
    b1.wait_recv()
    arrived(z + 2)


def reduce_z(net, part, sums, got, cols=pl.ds(0, D), make=None):
    up, down = net.device(dz=1), net.device(dz=-1)
    z = net.z
    if make:
        make(z + 2)
    c0 = net.send(part.at[half(z + 2, 0), cols], got.at[0, :, cols], up)
    c1 = net.send(part.at[half(z + 2, 1), cols], got.at[1, :, cols], down)
    if make:
        yield
        make(z + 1)
    d1 = net.send(part.at[half(z + 1, 1), cols], got.at[3, :, cols], up)
    if make:
        yield
        make(z - 1)
    d2 = net.send(part.at[half(z - 1, 0), cols], got.at[4, :, cols], down)
    if make:
        yield
        make(z)
    yield
    c0.wait_recv()
    add_rows(64, sums.at[0, :, cols], part.at[half(z + 1, 0), cols], got.at[0, :, cols])
    d0 = net.send(sums.at[0, :, cols], got.at[2, :, cols], up)
    yield
    c1.wait_recv()
    add_rows(64, sums.at[1, :, cols], part.at[half(z - 1, 1), cols], got.at[1, :, cols])
    d3 = net.send(sums.at[1, :, cols], got.at[5, :, cols], down)
    yield
    for sent in (d0, d1, d2, d3):
        sent.wait_recv()


def reduced(net, part, got, at, k):
    here = pl.ds(pl.multiple_of(at - 64 * k, 16), 16)
    total = part[pl.ds(pl.multiple_of(net.z * ROWS + at, 16), 16), :].astype(jnp.float32)
    return total + got[2 + k, here, :].astype(jnp.float32) + got[4 + k, here, :].astype(jnp.float32)


def gather_8(net, own, dst):
    up, down, beside = net.device(dz=1), net.device(dz=-1), net.beside
    xl, z = net.xl, net.z
    place = dst.at[block8(xl, z), :]
    s0 = net.send(own, place, up)
    s1 = net.send(own, place, down)
    s2 = net.send(own, place, beside)
    yield
    s0.wait_recv()
    ref = dst.at[half8(xl, z - 1, 0), :]
    s5 = net.send(ref, ref, up)
    yield
    s1.wait_recv()
    ref = dst.at[half8(xl, z + 1, 1), :]
    s6 = net.send(ref, ref, down)
    yield
    s2.wait_recv()
    ref = dst.at[block8(1 - xl, z), :]
    s3 = net.send(ref, ref, up)
    s4 = net.send(ref, ref, down)
    yield
    s5.wait_recv()
    s6.wait_recv()
    ref = dst.at[block8(xl, z + 2), :]
    s7 = net.send(ref, ref, beside)
    yield
    s3.wait_recv()
    s4.wait_recv()
    s7.wait_recv()


def reduce_8(net, make, part, sums, got, sums_half, got_half, out):
    up, down, beside = net.device(dz=1), net.device(dz=-1), net.beside
    xl, z = net.xl, net.z
    make(1 - xl, z + 2)
    a = net.send(part.at[block8(1 - xl, z + 2), :], got.at[0], beside)
    yield
    make(1 - xl, z + 1)
    b0 = net.send(part.at[block8(1 - xl, z + 1), :], got.at[1], up)
    yield
    make(1 - xl, z - 1)
    b1 = net.send(part.at[block8(1 - xl, z - 1), :], got.at[2], down)
    yield
    make(xl, z + 2)
    make(xl, z + 1)
    d1 = net.send(part.at[half8(xl, z + 1, 1), :], got_half.at[3], up)
    make(xl, z - 1)
    d2 = net.send(part.at[half8(xl, z - 1, 0), :], got_half.at[4], down)
    yield
    make(1 - xl, z)
    make(xl, z)
    yield
    a.wait_recv()
    add_rows(128, sums.at[0], part.at[block8(xl, z + 2), :], got.at[0])
    c0 = net.send(sums.at[0, pl.ds(0, 64), :], got_half.at[0], up)
    c1 = net.send(sums.at[0, pl.ds(64, 64), :], got_half.at[1], down)
    yield
    b0.wait_recv()
    b1.wait_recv()
    add_rows(128, sums.at[1], part.at[block8(1 - xl, z), :], got.at[1], got.at[2])
    e = net.send(sums.at[1], got.at[3], beside)
    yield
    c0.wait_recv()
    add_rows(64, sums_half.at[0], part.at[half8(xl, z + 1, 0), :], got_half.at[0])
    d0 = net.send(sums_half.at[0], got_half.at[2], up)
    yield
    c1.wait_recv()
    add_rows(64, sums_half.at[1], part.at[half8(xl, z - 1, 1), :], got_half.at[1])
    d3 = net.send(sums_half.at[1], got_half.at[5], down)
    yield
    for sent in (e, d0, d1, d2, d3):
        sent.wait_recv()

    def rows(at, k):
        here = pl.ds(pl.multiple_of(at - 64 * k, 16), 16)
        total = part[pl.ds(pl.multiple_of(net.t * ROWS + at, 16), 16), :].astype(jnp.float32)
        total = total + got[3, pl.ds(pl.multiple_of(at, 16), 16), :].astype(jnp.float32)
        return total + got_half[2 + k, here, :].astype(jnp.float32) + got_half[4 + k, here, :].astype(jnp.float32)

    out.append(rows)


def each_half(step):
    for k in (0, 1):
        def body(i, _, k=k):
            step(pl.multiple_of(k * 64 + i * 16, 16), k)
            return 0

        lax.fori_loop(0, 4, body, 0)


def gather_plane(net, slab, cut, first, second):
    low, high = cut
    sib = net.device(dc=1)
    second_up, second_down = second
    shared, halves, sent = [], {}, {}

    def share(i, j):
        ref = slab(i, j)
        shared.append(net.send(ref, ref, sib))

    def go(i):
        ref = slab(i, 0)
        sent[i] = (net.send(ref, ref, second_up), net.send(ref, ref, second_down))

    def on(i):
        sent[i][0].wait_recv()
        ref = low(slab(i, -1))
        up = net.send(ref, ref, second_up)
        share(i, -1)
        yield
        sent[i][1].wait_recv()
        ref = high(slab(i, 1))
        halves[i] = (up, net.send(ref, ref, second_down))
        share(i, 1)
        yield

    own = slab(0, 0)
    ring = len(first) == 2
    around = [net.send(own, own, to) for to in first]
    go(0)
    share(0, 0)
    yield
    if ring:
        around[0].wait_recv()
        ref = low(slab(-1, 0))
        f0 = net.send(ref, ref, first[0])
        go(-1)
        share(-1, 0)
        yield
        around[1].wait_recv()
        ref = high(slab(1, 0))
        f1 = net.send(ref, ref, first[1])
        go(1)
        share(1, 0)
        yield
        yield from on(0)
        f0.wait_recv()
        f1.wait_recv()
        go(2)
        share(2, 0)
        yield
        for i in (-1, 1, 2):
            yield from on(i)
    else:
        around[0].wait_recv()
        go(1)
        share(1, 0)
        yield
        for i in (0, 1):
            yield from on(i)
    for i in sent:
        halves[i][0].wait_recv()
        halves[i][1].wait_recv()
        share(i, 2)
        yield
    for copied in shared:
        copied.wait_recv()


def reduce_plane(net, mine, other, from_sib, got_half, got_up, got_down, last_bufs, cut, add, first, second):
    low, high = cut
    sib = net.device(dc=1)
    up, down = second
    ring = len(first) == 2
    steps = (0, 1, 3, 2) if ring else (0, 1)
    shared = {}
    for j in (2, 1, 3, 0):
        for i in steps:
            shared[i, j] = net.send(other(i, j), from_sib(i, j), sib)
    yield
    halves, full, last = {}, {}, {}
    for i in steps:
        shared[i, 2].wait_recv()
        add(None, mine(i, 2), from_sib(i, 2))
        halves[i] = (
            net.send(low(mine(i, 2)), low(got_half(i)), up),
            net.send(high(mine(i, 2)), high(got_half(i)), down),
        )
        yield
    for i in steps:
        shared[i, 1].wait_recv()
        halves[i][0].wait_recv()
        add(0, mine(i, 1), from_sib(i, 1), got_half(i))
        add(1, mine(i, 1), from_sib(i, 1))
        u = net.send(mine(i, 1), got_up(i), up)
        yield
        shared[i, 3].wait_recv()
        halves[i][1].wait_recv()
        add(0, mine(i, 3), from_sib(i, 3))
        add(1, mine(i, 3), from_sib(i, 3), got_half(i))
        full[i] = (u, net.send(mine(i, 3), got_down(i), down))
        yield
    for i in reversed(steps):
        shared[i, 0].wait_recv()
        full[i][0].wait_recv()
        full[i][1].wait_recv()
        add(None, mine(i, 0), from_sib(i, 0), got_up(i), got_down(i))
        if ring and i == 2:
            ref, to = mine(2, 0), last_bufs(2)
            last[2] = (net.send(low(ref), low(to), first[0]), net.send(high(ref), high(to), first[1]))
        if ring and i == 3:
            last[2][1].wait_recv()
            add(1, mine(3, 0), last_bufs(2))
            last[3] = net.send(mine(3, 0), last_bufs(1), first[1])
        if ring and i == 1:
            last[2][0].wait_recv()
            add(0, mine(1, 0), last_bufs(2))
        if i == 1:
            last[1] = net.send(mine(1, 0), last_bufs(0), first[0])
        yield
    last[1].wait_recv()
    if ring:
        last[3].wait_recv()
        add(None, mine(0, 0), last_bufs(0), last_bufs(1))
    else:
        add(None, mine(0, 0), last_bufs(0))


ATT_CUT = (lambda ref: ref.at[:, pl.ds(0, 64), :], lambda ref: ref.at[:, pl.ds(64, 64), :])


def add_in(cut, total):
    def add(part, dst, *terms):
        begin, n = {None: (0, total), 0: (0, cut), 1: (cut, total - cut)}[part]

        def piece(at, size):
            here = pl.ds(at, size)
            value = dst[here, :].astype(jnp.float32)
            for term in terms:
                value = value + term[here, :].astype(jnp.float32)
            dst[here, :] = value.astype(dst.dtype)

        def step(i, _):
            piece(pl.multiple_of(begin + i * 160, 16), 160)
            return 0

        lax.fori_loop(0, n // 160, step, 0)
        if n % 160:
            piece(begin + n // 160 * 160, n % 160)

    return add


def cut_at(cut, total):
    return (lambda ref: ref.at[pl.ds(0, cut), :], lambda ref: ref.at[pl.ds(cut, total - cut), :])


OD, OD_CUT = 944, 480
GU, GU_CUT = 1376, 688
QKV, QKV_CUT = 768, 384


def plane_slab(net, ref, kind, i, j):
    x = lax.rem(net.x + jnp.where(kind == 0, i, j) + 4, 4)
    y = lax.rem(net.y + jnp.where(kind == 0, j, i) + 4, 4)
    at = pl.ds(pl.multiple_of((y * 4 + lax.div(x, 2) * 2 + kind) * 128, 128), 128)
    return ref.at[lax.rem(x, 2), :, at]


def att_at(net, kind, i, j):
    x, y = lax.rem(net.x + 2 * i + 4, 4), lax.rem(net.y + j + 4, 4)
    return pl.ds(pl.multiple_of((y * 4 + lax.div(x, 2) * 2 + kind) * 128, 128), 128)


def forward(chain):
    next(chain, None)


def run(chains, order):
    for name in "".join(order):
        next(chains[name], None)
    for chain in chains.values():
        for _ in chain:
            pass


def start(copies):
    for copy in copies:
        copy.start()
    return copies


def sequence_starts(lengths, at, rows):
    index = lax.broadcasted_iota(jnp.int32, (rows, 1), 0) + at
    limit, first = lengths[0, 0], jnp.zeros((rows, 1), jnp.int32)
    for s in range(8):
        first = jnp.where(index >= limit, limit, first)
        if s < 7:
            limit = limit + lengths[0, s + 1]
    return index, first


def params(collective, mib=58):
    return pltpu.CompilerParams(collective_id=collective, has_side_effects=True, vmem_limit_bytes=mib << 20)


def sems(n, local):
    return [pltpu.SemaphoreType.DMA((n,)), pltpu.SemaphoreType.DMA((n,)), pltpu.SemaphoreType.DMA((local,))]


FRONT_ORDER = (
    "twbbbbltttwwwtllllwwwtclwlwlttllttlllltlcctllutt",
    "ttcuuttuuuuuuutthuuuhuuuuttttttttzztttgzzgmgggmm",
    "ggzmggmmggmggmzzgzzgggzgo",
)
BACK_ORDER = (
    "eteeeemtteeeeeeteettttttetswewswwwstwweestwwswwe",
    "ttmmwwtmw",
)


TILES = ((0, 256), (256, 256), (512, 176))


def front_kernel(tok, cot, lengths, gain, mlp_gain, rates, wq, wk, wv, wo, wg, wu, wd,
                 n1_out, w_out, q_out, k_out, v_out, p_out, table_out, h1, dh1, do_out, m_out, od_grad, gain_part, gu_grad,
                 wo_turned, n1, w, q, k, v, p, table, o, branches, w1, w2, g, n2, dgate, turned, da, do, sums, got,
                 sib, got_half, got_up, got_down, last, send_sems, recv_sems, local):
    net = Net(send_sems, recv_sems)
    bf, f32 = jnp.bfloat16, jnp.float32
    hid, dup = 0, 1024
    own_rows = att_at(net, net.c, 0, 0)
    own_od, own_gu = plane_slab(net, w1, net.c, 0, 0), plane_slab(net, w2, net.c, 0, 0)
    wo_turned[...] = wo[...].T
    own = start(
        [
            pltpu.make_async_copy(src, dst, local.at[n])
            for n, (src, dst) in enumerate(
                (
                    (wq, w.at[0, own_rows, :]), (wk, w.at[1, own_rows, :]), (wv, w.at[2, own_rows, :]),
                    (wo_turned, own_od.at[pl.ds(0, 256), :]), (wd, own_od.at[pl.ds(256, FFB), :]),
                    (wg, own_gu.at[pl.ds(0, FFB), :]), (wu, own_gu.at[pl.ds(FFB, FFB), :]), (cot, g.at[block(net.z), :]),
                )
            )
        ]
    )

    def norm(at, _):
        here = pl.ds(at, 16)
        value = tok[here, :].astype(f32)
        r = lax.rsqrt(jnp.mean(value * value, axis=-1, keepdims=True) + EPS)
        n1[pl.ds(pl.multiple_of(net.t * ROWS + at, 16), 16), :] = (value * r * gain[...]).astype(bf)

    each_half(norm)
    net.greet([net.device(dx=s) for s in (1, 2, 3)] + [net.device(dy=1), net.device(dy=-1), net.device(dz=1), net.device(dz=-1), net.device(dc=1)])
    part, m_part = n1.at[pl.ds(0, 512), :], n1.at[pl.ds(512, 512), :]
    saves = {}

    def save(n, src, dst):
        saves[n] = pltpu.make_async_copy(src, dst, local.at[n])
        saves[n].start()

    def project(i, _):
        here = pl.ds(pl.multiple_of(i * QROWS, QROWS), QROWS)
        left = n1[here, :]
        cos, sin = table[0, here, :], table[1, here, :]
        for m, dst in ((0, q), (1, k)):
            u = jnp.dot(left, w[m], preferred_element_type=f32)
            for h in range(2):
                uh = u[:, h * 128 : h * 128 + 128]
                dst[h, here, :] = (uh * cos + pltpu.roll(uh, 64, 1) * sin).astype(bf)
        u = jnp.dot(left, w[2], preferred_element_type=f32).astype(bf)
        for h in range(2):
            v[h, here, :] = u[:, h * 128 : h * 128 + 128]
        return 0

    def attend(b):
        rows = slice(b * QROWS, b * QROWS + QROWS)
        first, until = max(0, b - 2) * QROWS, (b + 1) * QROWS
        index, begin = sequence_starts(lengths, b * QROWS, QROWS)
        key = lax.broadcasted_iota(jnp.int32, (QROWS, until - first), 1) + first
        allowed = (key <= index) & (key >= begin)
        for h in range(2):
            s = lax.dot_general(q[h, rows, :], k[h, first:until, :], NT, preferred_element_type=f32)
            s = jnp.where(allowed, s * HEAD_DIM ** (-0.5), -1e30)
            e = jnp.exp(s - jnp.max(s, axis=-1, keepdims=True))
            weights = (e / jnp.sum(e, axis=-1, keepdims=True)).astype(bf)
            p[(h * 4 + b) * QROWS : (h * 4 + b + 1) * QROWS, 0 : until - first] = weights
            o[rows, h * 128 : h * 128 + 128] = jnp.dot(weights, v[h, first:until, :], preferred_element_type=f32).astype(bf)

    def exchange(n):
        src = o.at[pl.ds(pl.multiple_of((1 - net.xl) * 512 + n * QROWS, QROWS), QROWS), :]
        return net.send(src, branches.at[net.xl, pl.ds(n * QROWS, QROWS), :], net.beside)

    def branch(z):
        here = block(z)
        u = jnp.dot(branches[0, here, :], w1[0, :256, :], preferred_element_type=f32)
        u = u + jnp.dot(branches[1, here, :], w1[1, :256, :], preferred_element_type=f32)
        part[here, :] = u.astype(bf)

    def second_norm(at, half_at):
        here = pl.ds(at, 16)
        h = tok[here, :].astype(f32) + reduced(net, part, got, at, half_at)
        h1[here, :] = h
        r = lax.rsqrt(jnp.mean(h * h, axis=-1, keepdims=True) + EPS)
        n2[pl.ds(pl.multiple_of(net.z * ROWS + at, 16), 16), :] = (h * r * mlp_gain[...]).astype(bf)

    def ahead(b):
        for at, n in TILES:
            gate = lax.dot_general(n2[...], w2[b, at : at + n, :], NT, preferred_element_type=f32)
            up = lax.dot_general(n2[...], w2[b, FFB + at : FFB + at + n, :], NT, preferred_element_type=f32)
            dh = dgate[b, :, at : at + n].astype(f32)
            sig = jax.nn.sigmoid(gate)
            act = gate * sig
            dg, du, hi = (dh * up * sig * (1.0 + gate * (1.0 - sig))).astype(bf), (dh * act).astype(bf), (act * up).astype(bf)
            dgate[b, :, at : at + n] = dg
            p[dup + b * 512 : dup + b * 512 + 512, at : at + n] = du
            p[hid + b * 512 : hid + b * 512 + 512, at : at + n] = hi
            for m, value in enumerate((dg, du, hi)):
                turned[m, b, at : at + n, :] = value.T

    def back(i, _):
        at = pl.ds(pl.multiple_of(i * 256, 256), 256)
        d = jnp.dot(dgate[0], w2[0, :FFB, at], preferred_element_type=f32)
        d = d + jnp.dot(dgate[1], w2[1, :FFB, at], preferred_element_type=f32)
        d = d + jnp.dot(p[dup : dup + 512, :FFB], w2[0, FFB:, at], preferred_element_type=f32)
        d = d + jnp.dot(p[dup + 512 : dup + 1024, :FFB], w2[1, FFB:, at], preferred_element_type=f32)
        part[:, at] = d.astype(bf)
        return 0

    def outer(i):
        at = pl.ds(i * 512, 512)
        for m in range(2):
            for b in range(2):
                w2[b, m * FFB : m * FFB + FFB, at] = jnp.dot(turned[m, b], n2[:, at], preferred_element_type=f32).astype(bf)

    lanes = {name: net.lane() for name in "twlucaxyzg"}
    back_a = reduce_z(lanes["x"], part, sums, got, pl.ds(0, D // 2))
    back_b = reduce_z(lanes["y"], part, sums, got, pl.ds(D // 2, D // 2))

    def main():
        yield from gather_8(lanes["t"], n1.at[block8(net.xl, net.z), :], n1)
        yield
        save(8, n1, n1_out)
        save(9, w, w_out)
        save(10, table, table_out)
        lax.fori_loop(0, 2, project, 0)
        yield
        lax.fori_loop(2, 4, project, 0)
        for n, (src, dst) in enumerate(((q, q_out), (k, k_out), (v, v_out))):
            save(11 + n, src, dst)
        yield
        attend(0)
        yield
        attend(2)
        swapped = [exchange(0)]
        yield
        attend(1)
        yield
        attend(3)
        swapped.append(exchange(1))
        kept = pltpu.make_async_copy(o.at[pl.ds(pl.multiple_of(net.xl * 512, 512), 512), :], branches.at[net.xl], local.at[15])
        kept.start()
        save(14, p, p_out)
        yield
        for sent in swapped:
            sent.wait_recv()
        kept.wait()
        saves.pop(8).wait()
        lanes["t"].flush()
        yield from reduce_z(lanes["a"], part, sums, got, make=branch)
        each_half(second_norm)
        yield
        yield from gather_z(lanes["z"], n2.at[block(net.z), :], n2)
        lanes["a"].flush()
        saves.pop(14).wait()
        yield
        ahead(0)
        yield
        ahead(1)
        yield
        lax.fori_loop(0, 4, back, 0)
        forward(back_a)
        yield
        lax.fori_loop(4, 8, back, 0)
        forward(back_b)
        lanes["u"].flush()
        for i in range(4):
            yield
            outer(i)

    def norm_back(at, half_at):
        here = pl.ds(at, 16)
        h = h1[here, :]
        r = lax.rsqrt(jnp.mean(h * h, axis=-1, keepdims=True) + EPS)
        d = reduced(net, part, got, at, half_at)
        inner = d * mlp_gain[...]
        grad = r * inner - h * (r * r * r) * jnp.mean(h * inner, axis=-1, keepdims=True)
        grad = cot[here, :].astype(f32) + grad
        dh1[here, :] = grad
        da[pl.ds(pl.multiple_of(net.z * ROWS + at, 16), 16), :] = grad.astype(bf)
        gain_part[...] += jnp.sum(d * h * r, axis=0, keepdims=True)

    swapped_back = []

    def back_out(z):
        here = block(z)
        for b in range(2):
            do[b, here, :] = lax.dot_general(da[here, :], w1[b, :256, :], NT, preferred_element_type=f32).astype(bf)
        rows = pl.ds(pl.multiple_of(net.xl * 512 + lax.rem(z + 8, 4) * ROWS, ROWS), ROWS)
        swapped_back.append(net.send(do.at[1 - net.xl, here, :], do_out.at[rows, :], net.beside))
        save(15 + len(swapped_back), do.at[net.xl, here, :], do_out.at[rows, :])

    def tail():
        for chain in (back_a, back_a, back_b, back_b, back_a):
            forward(chain)
            yield
        forward(back_b)
        gain_part[...] = jnp.zeros_like(gain_part)
        each_half(norm_back)
        yield
        yield from gather_z(lanes["z"], da.at[block(net.z), :], da, back_out)

    def weights():
        for copied in own[:5]:
            copied.wait()
        yield from gather_plane(lanes["w"], lambda i, j: w.at[:, att_at(net, net.c, i, j), :], ATT_CUT, (net.across,), (net.device(dy=1), net.device(dy=-1)))

    def later():
        yield from gather_plane(lanes["l"], lambda i, j: plane_slab(net, w1, net.c, i, j), cut_at(OD_CUT, OD), net.along(True), net.along(False))

    def last_weights():
        for copied in own[5:7]:
            copied.wait()
        yield from gather_plane(lanes["u"], lambda i, j: plane_slab(net, w2, net.c, i, j), cut_at(GU_CUT, GU), net.along(True), net.along(False))

    def cotangent():
        own[7].wait()
        yield from gather_z(lanes["c"], cot, g)

    def hidden_grad():
        for b in range(2):
            if b:
                yield
            for at, n in TILES:
                u = lax.dot_general(g[...], w1[b, 256 + at : 256 + at + n, :], NT, preferred_element_type=f32)
                dgate[b, :, at : at + n] = u.astype(bf)

    def tables():
        def rows(i, _):
            at = pl.multiple_of(i * 128, 128)
            index, first = sequence_starts(lengths, at, 128)
            angle = (index - first).astype(f32) * rates[...]
            lane = lax.broadcasted_iota(jnp.int32, (128, 128), 1)
            table[0, pl.ds(at, 128), :] = jnp.cos(angle)
            sin = jnp.sin(angle)
            table[1, pl.ds(at, 128), :] = jnp.where(lane < 64, -sin, sin)
            return 0

        for i in range(4):
            if i:
                yield
            lax.fori_loop(2 * i, 2 * i + 2, rows, 0)

    def mixed_part():
        def columns(i, _):
            at = pl.ds(pl.multiple_of(i * 256, 256), 256)
            u = jnp.dot(p[hid : hid + 512, :FFB], w1[0, 256:, at], preferred_element_type=f32)
            u = u + jnp.dot(p[hid + 512 : hid + 1024, :FFB], w1[1, 256:, at], preferred_element_type=f32)
            m_part[:, at] = u.astype(bf)
            return 0

        for i in range(4):
            lax.fori_loop(2 * i, 2 * i + 2, columns, 0)
            yield
        save(20, m_part, m_out)
        lanes["l"].flush()
        for i in range(4):
            if i:
                yield
            at = pl.ds(i * 512, 512)
            for b in range(2):
                w1[b, 256:, at] = jnp.dot(turned[2, b], g[:, at], preferred_element_type=f32).astype(bf)
        save(21, w1.at[:, pl.ds(256, FFB), :], od_grad.at[:, pl.ds(256, FFB), :])

    def outer_out():
        for sent in swapped_back:
            sent.wait_recv()

        def columns(i, _):
            at = pl.ds(pl.multiple_of(i * 512, 512), 512)
            for b in range(2):
                w1[b, :256, at] = lax.dot_general(branches[b], da[:, at], TN, preferred_element_type=f32).astype(bf)
            return 0

        lax.fori_loop(0, 4, columns, 0)
        save(22, w1.at[:, pl.ds(0, 256), :], od_grad.at[:, pl.ds(0, 256), :])
        yield

    def grads():
        yield from reduce_plane(
            lanes["g"], lambda i, j: plane_slab(net, w2, net.c, i, j), lambda i, j: plane_slab(net, w2, 1 - net.c, i, j),
            lambda i, j: sib.at[i, j], lambda i: got_half.at[i], lambda i: got_up.at[i], lambda i: got_down.at[i], lambda i: last.at[i],
            cut_at(GU_CUT, GU), add_in(GU_CUT, GU), net.along(True), net.along(False),
        )

    run(
        {
            "t": main(), "z": tail(), "w": weights(), "l": later(), "u": last_weights(), "c": cotangent(), "h": hidden_grad(),
            "b": tables(), "m": mixed_part(), "o": outer_out(), "g": grads(),
        },
        FRONT_ORDER,
    )
    gu_grad[...] = plane_slab(net, w2, net.c, 0, 0)[...]
    for saved in saves.values():
        saved.wait()
    net.finish()


def front(*args):
    bf, f32 = jnp.bfloat16, jnp.float32
    slab = (GU, 128)
    kept = (
        ((GROUP, D), bf), ((3, D, 256), bf), ((2, GROUP, 128), bf), ((2, GROUP, 128), bf), ((2, GROUP, 128), bf),
        ((2 * GROUP, 768), bf), ((2, GROUP, 128), f32),
    )
    outs = kept + (((ROWS, D), f32), ((ROWS, D), f32), ((GROUP, 256), bf), ((512, D), bf), ((2, OD, D), bf), ((1, D), f32), (slab, bf))
    scratch = (((256, 128), bf),) + kept + (
        ((GROUP, 256), bf), ((2, 512, 256), bf), ((2, OD, D), bf), ((2, GU, D), bf), ((512, D), bf), ((512, D), bf),
        ((2, 512, FFB), bf), ((3, 2, FFB, 512), bf), ((512, D), bf), ((2, 512, 256), bf), ((2, 64, D), bf), ((6, 64, D), bf),
        ((4, 4) + slab, bf), ((4,) + slab, bf), ((4,) + slab, bf), ((4,) + slab, bf), ((3,) + slab, bf),
    )
    return pl.pallas_call(
        front_kernel,
        name="front",
        out_shape=tuple(jax.ShapeDtypeStruct(*s) for s in outs),
        in_specs=[VMEM, VMEM, pl.BlockSpec(memory_space=pltpu.SMEM), VMEM, VMEM, VMEM, ANY, ANY, ANY, VMEM, ANY, ANY, ANY],
        out_specs=(ANY,) * 7 + (VMEM, VMEM, ANY, ANY, ANY, VMEM, VMEM),
        scratch_shapes=[pltpu.VMEM(*s) for s in scratch] + sems(192, 23),
        compiler_params=params(1, 64),
    )(*args)


def back_kernel(do_in, n1_in, w_in, q_in, k_in, v_in, p_in, table_in, m_in, od_in, tok, h1, dh1, gain, mlp_gain_part,
                    mixed, dx, gains, qkv_grad, od_grad,
                    do, n1, w, q, k, v, p, table, dqkv, dk, dv, part, sums, got, sums_half, got_half,
                    ga, sib, slab_half, slab_up, slab_down, slab_last, sum_z, sum_x, sum_y, sum_c,
                    m_part, sums_m, got_m, od, od_sib, od_half, od_up, od_down, od_last,
                    send_sems, recv_sems, local):
    net = Net(send_sems, recv_sems)
    bf, f32 = jnp.bfloat16, jnp.float32
    loads = start(
        [
            pltpu.make_async_copy(src, dst, local.at[m])
            for m, (src, dst) in enumerate(((do_in, do), (v_in, v), (p_in, p), (q_in, q), (k_in, k), (table_in, table), (m_in, m_part), (w_in, w), (n1_in, n1)))
        ]
    )
    slabs = start(
        [
            pltpu.make_async_copy(plane_slab(net, od_in, net.c, i, j), od.at[i, j], local.at[9 + n])
            for n, (i, j) in enumerate((i, j) for j in (2, 1, 3, 0) for i in (0, 1, 3, 2))
        ]
    )
    line_x = [net.device(dx=s) for s in (1, 2, 3)]
    line_y = [net.device(dy=s) for s in (1, 2, 3)]
    line_z = [net.device(dz=s) for s in (1, 2, 3)]
    net.greet(line_x + line_y + line_z + [net.device(dc=1)])

    def attend_back(h, b):
        rows = slice(b * QROWS, b * QROWS + QROWS)
        first, until = max(0, b - 2) * QROWS, (b + 1) * QROWS
        keys, old = slice(first, until), slice(first, b * QROWS)
        weights_b = p[(h * 4 + b) * QROWS : (h * 4 + b + 1) * QROWS, 0 : until - first]
        do_b = do[rows, h * 128 : h * 128 + 128]
        dp = lax.dot_general(do_b, v[h, keys, :], NT, preferred_element_type=f32)
        wide = weights_b.astype(f32)
        centre = jnp.sum(wide * dp, axis=-1, keepdims=True)
        ds = (wide * (dp - centre)).astype(bf)
        dvb = lax.dot_general(weights_b, do_b, TN, preferred_element_type=f32)
        dkb = lax.dot_general(ds, q[h, rows, :], TN, preferred_element_type=f32)
        if b > 0:
            dv[h, old, :] += dvb[: b * QROWS - first]
            dk[h, old, :] += dkb[: b * QROWS - first]
        dv[h, rows, :] = dvb[b * QROWS - first :]
        dk[h, rows, :] = dkb[b * QROWS - first :]
        dqb = jnp.dot(ds, k[h, keys, :], preferred_element_type=f32) * HEAD_DIM ** (-0.5)
        dqb = dqb * table[0, rows, :] - pltpu.roll(dqb, 64, 1) * table[1, rows, :]
        dqkv[rows, h * 128 : h * 128 + 128] = dqb.astype(bf)

    def turn(i, _):
        here = pl.ds(pl.multiple_of(i * QROWS, QROWS), QROWS)
        for h in range(2):
            u = dk[h, here, :] * HEAD_DIM ** (-0.5)
            u = u * table[0, here, :] - pltpu.roll(u, 64, 1) * table[1, here, :]
            dqkv[here, 256 + h * 128 : 384 + h * 128] = u.astype(bf)
            dqkv[here, 512 + h * 128 : 640 + h * 128] = dv[h, here, :].astype(bf)
        return 0

    def make(xl, z):
        here = block8(xl, z)
        left = dqkv[here, :]

        def columns(i, _):
            at = pl.ds(pl.multiple_of(i * 512, 512), 512)
            u = lax.dot_general(left[:, :256], w[0, at, :], NT, preferred_element_type=f32)
            u = u + lax.dot_general(left[:, 256:512], w[1, at, :], NT, preferred_element_type=f32)
            u = u + lax.dot_general(left[:, 512:], w[2, at, :], NT, preferred_element_type=f32)
            part[here, at] = u.astype(bf)
            sum_z[net.z, 0:1, at] += jnp.sum(u * n1[here, at].astype(f32), axis=0, keepdims=True)
            return 0

        lax.fori_loop(0, 4, columns, 0)

    out = []

    def step(at, k):
        here = pl.ds(at, 16)
        value = tok[here, :].astype(f32)
        r = lax.rsqrt(jnp.mean(value * value, axis=-1, keepdims=True) + EPS)
        inner = out[0](at, k) * gain[...]
        dx[here, :] = dh1[here, :] + r * inner - value * (r * r * r) * jnp.mean(value * inner, axis=-1, keepdims=True)

    def main():
        for copied in loads[:6]:
            copied.wait()
        yield
        for b in range(GROUP // QROWS):
            for h in range(2):
                attend_back(h, b)
            yield
        lax.fori_loop(0, GROUP // QROWS, turn, 0)
        for copied in loads[7:]:
            copied.wait()
        sum_z[net.z, 0:1, :] = jnp.zeros((1, D), f32)
        sum_z[net.z, 1:2, :] = mlp_gain_part[...]
        yield
        yield from reduce_8(net, make, part, sums, got, sums_half, got_half, out)
        each_half(step)

    def early():
        chain = reduce_plane(
            net, lambda i, j: od.at[i, j], lambda i, j: plane_slab(net, od_in, 1 - net.c, i, j), lambda i, j: od_sib.at[i, j],
            lambda i: od_half.at[i], lambda i: od_up.at[i], lambda i: od_down.at[i], lambda i: od_last.at[i],
            cut_at(OD_CUT, OD), add_in(OD_CUT, OD), net.along(True), net.along(False),
        )
        forward(chain)
        yield
        for copied in slabs:
            copied.wait()
        yield from chain
        od_grad[...] = od[0, 0]

    def mixing():
        loads[6].wait()
        yield from reduce_z(net, m_part, sums_m, got_m)

        def mix(at, k):
            here = pl.ds(at, 16)
            mixed[here, :] = (h1[here, :] + reduced(net, m_part, got_m, at, k)).astype(bf)

        each_half(mix)

    def slab(kind):
        return lambda i, j: ga.at[:, att_at(net, kind, i, j)]

    def weights():
        def outer(i, _):
            at = pl.ds(pl.multiple_of(i * 256, 256), 256)
            ga[:, at] = lax.dot_general(dqkv[...], n1[:, at], TN, preferred_element_type=f32).astype(bf)
            return 0

        for i in range(4):
            lax.fori_loop(2 * i, 2 * i + 2, outer, 0)
            yield
        yield from reduce_plane(
            net, slab(net.c), slab(1 - net.c), lambda i, j: sib.at[i, j], lambda i: slab_half.at[i], lambda i: slab_up.at[i],
            lambda i: slab_down.at[i], lambda i: slab_last.at[i], cut_at(QKV_CUT, QKV), add_in(QKV_CUT, QKV), (net.across,), (net.device(dy=1), net.device(dy=-1)),
        )
        qkv_grad[...] = slab(net.c)(0, 0)[...]

    def gain_sums():
        here = net.z
        for ref, line, then, place in ((sum_z, line_z, sum_x, net.x), (sum_x, line_x, sum_y, net.y), (sum_y, line_y, sum_c, net.c), (sum_c, [net.device(dc=1)], None, None)):
            sent = [net.send(ref.at[here], ref.at[here], to) for to in line]
            yield
            for copied in sent:
                copied.wait_recv()
            total = ref[0]
            for n in range(1, len(line) + 1):
                total = total + ref[n]
            if then is None:
                gains[0:1, :] = total[0:1] / gain[...]
                gains[1:2, :] = total[1:2]
            else:
                then[place] = total
                here = place

    run({"t": main(), "m": mixing(), "e": early(), "w": weights(), "s": gain_sums()}, BACK_ORDER)
    net.finish()


def back(do, n1, w, q, k, v, p, table, m, od, tok, h1, dh1, gain, mlp_gain_part):
    bf, f32 = jnp.bfloat16, jnp.float32
    slab, slab_od = (QKV, 128), (OD, 128)
    scratch = [
        ((GROUP, 256), bf), ((GROUP, D), bf), ((3, D, 256), bf), ((2, GROUP, 128), bf), ((2, GROUP, 128), bf), ((2, GROUP, 128), bf),
        ((2 * GROUP, 768), bf), ((2, GROUP, 128), f32), ((GROUP, QKV), bf),
        ((2, GROUP, 128), f32), ((2, GROUP, 128), f32), ((GROUP, D), bf), ((2, ROWS, D), bf), ((4, ROWS, D), bf),
        ((2, 64, D), bf), ((6, 64, D), bf), ((QKV, D), bf), ((2, 4) + slab, bf), ((2,) + slab, bf), ((2,) + slab, bf),
        ((2,) + slab, bf), ((1,) + slab, bf), ((4, 2, D), f32), ((4, 2, D), f32), ((4, 2, D), f32), ((2, 2, D), f32),
        ((512, D), bf), ((2, 64, D), bf), ((6, 64, D), bf), ((4, 4) + slab_od, bf), ((4, 4) + slab_od, bf),
        ((4,) + slab_od, bf), ((4,) + slab_od, bf), ((4,) + slab_od, bf), ((3,) + slab_od, bf),
    ]
    outs = (((ROWS, D), bf), ((ROWS, D), f32), ((2, D), f32), (slab, bf), (slab_od, bf))
    return pl.pallas_call(
        back_kernel,
        name="back",
        out_shape=tuple(jax.ShapeDtypeStruct(*s) for s in outs),
        in_specs=[ANY] * 10 + [VMEM] * 5,
        out_specs=(VMEM,) * 5,
        scratch_shapes=[pltpu.VMEM(*s) for s in scratch] + sems(112, 25),
        compiler_params=params(2),
    )(do, n1, w, q, k, v, p, table, m, od, tok, h1, dh1, gain, mlp_gain_part)


def finish_kernel(mixed_in, dx_in, gains_in, qkv_in, od_in, gu_in, mixed, dx, ag, gq, gk, gv, go, mg, gg, gu_out, gd, gains, qkv, od, gu, sems):
    f32 = jnp.float32
    pairs = ((gu_in, gu), (od_in, od), (qkv_in, qkv), (gains_in, gains), (mixed_in, mixed), (dx_in, dx))
    loads = start([pltpu.make_async_copy(src, dst, sems.at[n]) for n, (src, dst) in enumerate(pairs)])
    for load in loads[:4]:
        load.wait()
    gg[...] = gu[:FFB, :].astype(f32)
    gu_out[...] = gu[FFB:, :].astype(f32)
    go[...] = od[:256, :].astype(f32).T
    gd[...] = od[256:, :].astype(f32)
    for n, dst in enumerate((gq, gk, gv)):
        dst[...] = qkv[n * 256 : n * 256 + 256, :].astype(f32).T
    ag[...] = gains[0:1, :]
    mg[...] = gains[1:2, :]
    for load in loads[4:]:
        load.wait()


def finish(mixed, dx, gains, qkv, od, gu):
    f32, bf = jnp.float32, jnp.bfloat16
    outs = (
        ((ROWS, D), bf), ((ROWS, D), f32), ((1, D), f32), ((ROWS, 256), f32), ((ROWS, 256), f32), ((ROWS, 256), f32),
        ((ROWS, 256), f32), ((1, D), f32), ((FFB, 128), f32), ((FFB, 128), f32), ((FFB, 128), f32),
    )
    held = (((2, D), f32), ((QKV, 128), bf), ((OD, 128), bf), ((GU, 128), bf))
    return pl.pallas_call(
        finish_kernel,
        name="finish",
        out_shape=tuple(jax.ShapeDtypeStruct(*s) for s in outs),
        in_specs=[ANY] * 6,
        out_specs=(VMEM,) * 11,
        scratch_shapes=[pltpu.VMEM(*s) for s in held] + [pltpu.SemaphoreType.DMA((6,))],
        compiler_params=pltpu.CompilerParams(vmem_limit_bytes=60 << 20),
    )(mixed, dx, gains, qkv, od, gu)


def shards(
    tokens,
    lengths,
    attn_gain,
    query_weight,
    key_weight,
    value_weight,
    out_weight,
    mlp_gain,
    gate_weight,
    up_weight,
    down_weight,
    cotangent,
):
    half_rates = THETA ** (-(np.arange(64, dtype=np.float32) * np.float32(2.0 / HEAD_DIM)))
    rates = jnp.asarray(np.concatenate([half_rates, half_rates])[None].astype(np.float32))
    n1, w, q, k, v, p, table, h1, dh1, do, m, od_part, gain_part, gu = front(
        tokens, cotangent, lengths, attn_gain[None], mlp_gain[None], rates, query_weight, key_weight, value_weight, out_weight,
        gate_weight.T, up_weight.T, down_weight.T,
    )
    mixed, dx, gains, qkv, od_grad = back(do, n1, w, q, k, v, p, table, m, od_part, tokens, h1, dh1, attn_gain[None], gain_part)
    mixed, dx, ag, gq, gk, gv, go, mg, gg, gu, gd = finish(mixed, dx, gains, qkv, od_grad, gu)
    return (mixed, dx, ag[0], gq, gk, gv, go, mg[0], gg.T, gu.T, gd.T)


def solution(mesh):
    return jax.shard_map(
        shards,
        mesh=mesh,
        in_specs=(
            P(("dp", "tensor"), None),
            P("dp", None),
            P(),
            P("dp", "tensor"),
            P("dp", "tensor"),
            P("dp", "tensor"),
            P("dp", "tensor"),
            P(),
            P("dp", "tensor"),
            P("dp", "tensor"),
            P("dp", "tensor"),
            P(("dp", "tensor"), None),
        ),
        out_specs=(
            P(("dp", "tensor"), None),
            P(("dp", "tensor"), None),
            P(),
            P("dp", "tensor"),
            P("dp", "tensor"),
            P("dp", "tensor"),
            P("dp", "tensor"),
            P(),
            P("dp", "tensor"),
            P("dp", "tensor"),
            P("dp", "tensor"),
        ),
        check_vma=False,
    )
```

```python
import copy
import functools

import jax
import jax.numpy as jnp
import numpy as np
from jax import lax
from jax.experimental import pallas as pl
from jax.experimental.pallas import tpu as pltpu
from jax.sharding import PartitionSpec as P

HEAD_DIM = 128
EPS = 1e-05
THETA = 10000.0
D = 2048
ROWS = 128
GROUP = 1024
FFB = 688
QROWS = 256
MESH = pl.DeviceIdType.MESH
ANY = pl.BlockSpec(memory_space=pl.ANY)
VMEM = pl.BlockSpec(memory_space=pltpu.VMEM)
NT = (((1,), (1,)), ((), ()))
TN = (((0,), (0,)), ((), ()))


class Net:
    def __init__(self, send_sems, recv_sems):
        dp, t = lax.axis_index("dp"), lax.axis_index("tensor")
        self.y, self.c = lax.div(dp, 4), lax.rem(dp, 2)
        self.xl, self.z = lax.div(t, 4), lax.rem(t, 4)
        self.x = lax.rem(lax.div(dp, 2), 2) * 2 + self.xl
        self.dp, self.t = dp, t
        self.send_sems, self.recv_sems = send_sems, recv_sems
        self.used = [0]
        self.sent = []
        self.lanes = [self]

    def lane(self):
        other = copy.copy(self)
        other.sent = []
        self.lanes.append(other)
        return other

    def device(self, dx=0, dy=0, dz=0, dc=0):
        x, y = lax.rem(self.x + dx + 4, 4), lax.rem(self.y + dy + 4, 4)
        z, c = lax.rem(self.z + dz + 4, 4), lax.rem(self.c + dc, 2)
        return (y * 4 + lax.div(x, 2) * 2 + c, lax.rem(x, 2) * 4 + z)

    @property
    def beside(self):
        return (self.dp, (1 - self.xl) * 4 + self.z)

    @property
    def across(self):
        return self.device(dx=2)

    def along(self, first):
        on_x = self.c == (0 if first else 1)
        both = []
        for step in (1, -1):
            by_x, by_y = self.device(dx=step), self.device(dy=step)
            both.append(tuple(jnp.where(on_x, u, v) for u, v in zip(by_x, by_y)))
        return both

    def send(self, src, dst, to):
        k = self.used[0]
        self.used[0] += 1
        sent = pltpu.make_async_remote_copy(
            src_ref=src,
            dst_ref=dst,
            send_sem=self.send_sems.at[k],
            recv_sem=self.recv_sems.at[k],
            device_id=to,
            device_id_type=MESH,
        )
        sent.start()
        self.sent.append(sent)
        return sent

    def flush(self):
        for sent in self.sent:
            sent.wait_send()
        self.sent.clear()

    def finish(self):
        for lane in self.lanes:
            lane.flush()

    def greet(self, devices):
        for device in devices:
            pl.semaphore_signal(pltpu.get_barrier_semaphore(), inc=1, device_id=device, device_id_type=MESH)
        self.greeted = len(devices)

    def met(self):
        pl.semaphore_wait(pltpu.get_barrier_semaphore(), self.greeted)


def block(z):
    return pl.ds(pl.multiple_of(lax.rem(z + 8, 4) * ROWS, ROWS), ROWS)


def half(z, k):
    return pl.ds(pl.multiple_of(lax.rem(z + 8, 4) * ROWS + k * 64, 64), 64)


def block8(xl, z):
    return pl.ds(pl.multiple_of((xl * 4 + lax.rem(z + 8, 4)) * ROWS, ROWS), ROWS)


def half8(xl, z, k):
    return pl.ds(pl.multiple_of((xl * 4 + lax.rem(z + 8, 4)) * ROWS + k * 64, 64), 64)


def add_rows(rows, dst, *terms):
    def step(i, _):
        at = pl.ds(pl.multiple_of(i * 16, 16), 16)
        total = terms[0][at, :].astype(jnp.float32)
        for term in terms[1:]:
            total = total + term[at, :].astype(jnp.float32)
        dst[at, :] = total.astype(dst.dtype)
        return 0

    lax.fori_loop(0, rows // 16, step, 0)


def gather_z(net, own, dst, fill=None, arrived=None):
    up, down = net.device(dz=1), net.device(dz=-1)
    z = net.z
    place = [dst.at[half(z, k), :] for k in (0, 1)]
    if fill:
        fill(0)
    up_0 = net.send(own(0), place[0], up)
    if fill:
        yield
        fill(1)
    down_1 = net.send(own(1), place[1], down)
    up_1 = net.send(own(1), place[1], up)
    down_0 = net.send(own(0), place[0], down)
    yield
    if arrived:
        arrived(z)
        yield
    up_0.wait_recv()
    ref = dst.at[half(z - 1, 0), :]
    on_0 = net.send(ref, ref, up)
    yield
    down_1.wait_recv()
    ref = dst.at[half(z + 1, 1), :]
    on_1 = net.send(ref, ref, down)
    yield
    up_1.wait_recv()
    if arrived:
        arrived(z - 1)
    yield
    down_0.wait_recv()
    if arrived:
        arrived(z + 1)
    yield
    on_0.wait_recv()
    on_1.wait_recv()
    if arrived:
        arrived(z + 2)


def reduce_z(net, part, sums, got, cols=pl.ds(0, D), make=None):
    up, down = net.device(dz=1), net.device(dz=-1)
    z = net.z
    if make:
        make(z + 2)
    c0 = net.send(part.at[half(z + 2, 0), cols], got.at[0, :, cols], up)
    c1 = net.send(part.at[half(z + 2, 1), cols], got.at[1, :, cols], down)
    if make:
        yield
        make(z + 1)
    d1 = net.send(part.at[half(z + 1, 1), cols], got.at[3, :, cols], up)
    if make:
        yield
        make(z - 1)
    d2 = net.send(part.at[half(z - 1, 0), cols], got.at[4, :, cols], down)
    if make:
        yield
        make(z)
    yield
    c0.wait_recv()
    add_rows(64, sums.at[0, :, cols], part.at[half(z + 1, 0), cols], got.at[0, :, cols])
    d0 = net.send(sums.at[0, :, cols], got.at[2, :, cols], up)
    yield
    c1.wait_recv()
    add_rows(64, sums.at[1, :, cols], part.at[half(z - 1, 1), cols], got.at[1, :, cols])
    d3 = net.send(sums.at[1, :, cols], got.at[5, :, cols], down)
    yield
    for sent in (d0, d1, d2, d3):
        sent.wait_recv()


def reduced(net, part, got, at, k):
    here = pl.ds(pl.multiple_of(at - 64 * k, 16), 16)
    total = part[pl.ds(pl.multiple_of(net.z * ROWS + at, 16), 16), :].astype(jnp.float32)
    return total + got[2 + k, here, :].astype(jnp.float32) + got[4 + k, here, :].astype(jnp.float32)


def gather_8(net, dst):
    up, down, beside = net.device(dz=1), net.device(dz=-1), net.beside
    xl, z = net.xl, net.z

    def send(x, dz, k, to):
        ref = dst.at[half8(x, z + dz, k), :]
        return net.send(ref, ref, to)

    up_0, down_1 = send(xl, 0, 0, up), send(xl, 0, 1, down)
    up_1, down_0 = send(xl, 0, 1, up), send(xl, 0, 0, down)
    side_0, side_1 = send(xl, 0, 0, beside), send(xl, 0, 1, beside)
    yield
    up_0.wait_recv()
    on_0 = send(xl, -1, 0, up)
    yield
    down_1.wait_recv()
    on_1 = send(xl, 1, 1, down)
    yield
    side_0.wait_recv()
    rest = [send(1 - xl, 0, 0, up), send(1 - xl, 0, 0, down)]
    yield
    side_1.wait_recv()
    rest += [send(1 - xl, 0, 1, up), send(1 - xl, 0, 1, down)]
    yield
    on_0.wait_recv()
    rest.append(send(xl, 2, 0, beside))
    yield
    on_1.wait_recv()
    rest.append(send(xl, 2, 1, beside))
    yield
    for sent in [up_1, down_0] + rest:
        sent.wait_recv()


def reduce_8(net, make, part, sums, got, sums_half, got_half, out):
    up, down, beside = net.device(dz=1), net.device(dz=-1), net.beside
    xl, z = net.xl, net.z
    halves = [pl.ds(0, 64), pl.ds(64, 64)]
    make(1 - xl, z + 2)
    a = [net.send(part.at[half8(1 - xl, z + 2, k), :], got.at[0, halves[k], :], beside) for k in (0, 1)]
    yield
    make(1 - xl, z + 1)
    b0 = net.send(part.at[block8(1 - xl, z + 1), :], got.at[1], up)
    yield
    make(1 - xl, z - 1)
    b1 = net.send(part.at[block8(1 - xl, z - 1), :], got.at[2], down)
    yield
    for step in (2, 1, -1):
        make(xl, z + step)
        yield
    a[0].wait_recv()
    add_rows(64, sums.at[0, halves[0], :], part.at[half8(xl, z + 2, 0), :], got.at[0, halves[0], :])
    c0 = net.send(sums.at[0, halves[0], :], got_half.at[0], up)
    yield
    a[1].wait_recv()
    add_rows(64, sums.at[0, halves[1], :], part.at[half8(xl, z + 2, 1), :], got.at[0, halves[1], :])
    c1 = net.send(sums.at[0, halves[1], :], got_half.at[1], down)
    d1 = net.send(part.at[half8(xl, z + 1, 1), :], got_half.at[3], up)
    d2 = net.send(part.at[half8(xl, z - 1, 0), :], got_half.at[4], down)
    yield
    make(1 - xl, z)
    yield
    make(xl, z)
    yield
    b0.wait_recv()
    b1.wait_recv()
    add_rows(128, sums.at[1], part.at[block8(1 - xl, z), :], got.at[1], got.at[2])
    e = net.send(sums.at[1], got.at[3], beside)
    yield
    c0.wait_recv()
    add_rows(64, sums_half.at[0], part.at[half8(xl, z + 1, 0), :], got_half.at[0])
    d0 = net.send(sums_half.at[0], got_half.at[2], up)
    yield
    c1.wait_recv()
    add_rows(64, sums_half.at[1], part.at[half8(xl, z - 1, 1), :], got_half.at[1])
    d3 = net.send(sums_half.at[1], got_half.at[5], down)
    yield
    for sent in (e, d0, d1, d2, d3):
        sent.wait_recv()

    def rows(at, k):
        here = pl.ds(pl.multiple_of(at - 64 * k, 16), 16)
        total = part[pl.ds(pl.multiple_of(net.t * ROWS + at, 16), 16), :].astype(jnp.float32)
        total = total + got[3, pl.ds(pl.multiple_of(at, 16), 16), :].astype(jnp.float32)
        return total + got_half[2 + k, here, :].astype(jnp.float32) + got_half[4 + k, here, :].astype(jnp.float32)

    out.append(rows)


def on_half(step, k):
    def body(i, _):
        step(pl.multiple_of(k * 64 + i * 16, 16), k)
        return 0

    lax.fori_loop(0, 4, body, 0)


def each_half(step):
    for k in (0, 1):
        on_half(step, k)


def gather_plane(net, slab, cut, first, second):
    low, high = cut
    sib = net.device(dc=1)
    second_up, second_down = second
    shared, halves, sent = [], {}, {}

    def share(i, j):
        ref = slab(i, j)
        shared.append(net.send(ref, ref, sib))

    def go(i):
        ref = slab(i, 0)
        sent[i] = (net.send(ref, ref, second_up), net.send(ref, ref, second_down))

    def on(i):
        sent[i][0].wait_recv()
        ref = low(slab(i, -1))
        up = net.send(ref, ref, second_up)
        share(i, -1)
        yield
        sent[i][1].wait_recv()
        ref = high(slab(i, 1))
        halves[i] = (up, net.send(ref, ref, second_down))
        share(i, 1)
        yield

    own = slab(0, 0)
    ring = len(first) == 2
    around = [net.send(own, own, to) for to in first]
    go(0)
    share(0, 0)
    yield
    if ring:
        around[0].wait_recv()
        ref = low(slab(-1, 0))
        f0 = net.send(ref, ref, first[0])
        go(-1)
        share(-1, 0)
        yield
        around[1].wait_recv()
        ref = high(slab(1, 0))
        f1 = net.send(ref, ref, first[1])
        go(1)
        share(1, 0)
        yield
        yield from on(0)
        f0.wait_recv()
        f1.wait_recv()
        go(2)
        share(2, 0)
        yield
        for i in (-1, 1, 2):
            yield from on(i)
    else:
        around[0].wait_recv()
        go(1)
        share(1, 0)
        yield
        for i in (0, 1):
            yield from on(i)
    for i in sent:
        halves[i][0].wait_recv()
        halves[i][1].wait_recv()
        share(i, 2)
        yield
    for copied in shared:
        copied.wait_recv()


def reduce_plane(net, mine, other, from_sib, got_half, got_up, got_down, last_bufs, cut, add, first, second):
    low, high = cut
    sib = net.device(dc=1)
    up, down = second
    ring = len(first) == 2
    steps = (2, 3, 1, 0) if ring else (1, 0)
    shared = {}
    for j in (2, 1, 3, 0):
        for i in steps:
            shared[i, j] = net.send(other(i, j), from_sib(i, j), sib)
    yield
    halves, full, last = {}, {}, {}
    for i in steps:
        shared[i, 2].wait_recv()
        add(None, mine(i, 2), from_sib(i, 2))
        halves[i] = (
            net.send(low(mine(i, 2)), low(got_half(i)), up),
            net.send(high(mine(i, 2)), high(got_half(i)), down),
        )
        yield
    for i in steps:
        shared[i, 1].wait_recv()
        halves[i][0].wait_recv()
        add(0, mine(i, 1), from_sib(i, 1), got_half(i))
        add(1, mine(i, 1), from_sib(i, 1))
        u = net.send(mine(i, 1), got_up(i), up)
        yield
        shared[i, 3].wait_recv()
        halves[i][1].wait_recv()
        add(0, mine(i, 3), from_sib(i, 3))
        add(1, mine(i, 3), from_sib(i, 3), got_half(i))
        full[i] = (u, net.send(mine(i, 3), got_down(i), down))
        yield
    for i in steps:
        shared[i, 0].wait_recv()
        full[i][0].wait_recv()
        full[i][1].wait_recv()
        add(None, mine(i, 0), from_sib(i, 0), got_up(i), got_down(i))
        if ring and i == 2:
            ref, to = mine(2, 0), last_bufs(2)
            last[2] = (net.send(low(ref), low(to), first[0]), net.send(high(ref), high(to), first[1]))
        if ring and i == 3:
            last[2][1].wait_recv()
            add(1, mine(3, 0), last_bufs(2))
            last[3] = net.send(mine(3, 0), last_bufs(1), first[1])
        if ring and i == 1:
            last[2][0].wait_recv()
            add(0, mine(1, 0), last_bufs(2))
        if i == 1:
            last[1] = net.send(mine(1, 0), last_bufs(0), first[0])
        yield
    last[1].wait_recv()
    if ring:
        last[3].wait_recv()
        add(None, mine(0, 0), last_bufs(0), last_bufs(1))
    else:
        add(None, mine(0, 0), last_bufs(0))


ATT_CUT = (lambda ref: ref.at[:, pl.ds(0, 64), :], lambda ref: ref.at[:, pl.ds(64, 64), :])


def add_in(cut, total):
    def add(part, dst, *terms):
        begin, n = {None: (0, total), 0: (0, cut), 1: (cut, total - cut)}[part]

        def piece(at, size):
            here = pl.ds(at, size)
            value = dst[here, :].astype(jnp.float32)
            for term in terms:
                value = value + term[here, :].astype(jnp.float32)
            dst[here, :] = value.astype(dst.dtype)

        def step(i, _):
            piece(pl.multiple_of(begin + i * 160, 16), 160)
            return 0

        lax.fori_loop(0, n // 160, step, 0)
        if n % 160:
            piece(begin + n // 160 * 160, n % 160)

    return add


def cut_at(cut, total):
    return (lambda ref: ref.at[pl.ds(0, cut), :], lambda ref: ref.at[pl.ds(cut, total - cut), :])


OD, OD_CUT = 944, 480
GU, GU_CUT = 1376, 688
QKV, QKV_CUT = 768, 384
OUT, FF_CUT = 256, 352


def plane_slab(net, ref, kind, i, j):
    x = lax.rem(net.x + jnp.where(kind == 0, i, j) + 4, 4)
    y = lax.rem(net.y + jnp.where(kind == 0, j, i) + 4, 4)
    at = pl.ds(pl.multiple_of((y * 4 + lax.div(x, 2) * 2 + kind) * 128, 128), 128)
    return ref.at[lax.rem(x, 2), :, at]


def att_at(net, kind, i, j):
    x, y = lax.rem(net.x + 2 * i + 4, 4), lax.rem(net.y + j + 4, 4)
    return pl.ds(pl.multiple_of((y * 4 + lax.div(x, 2) * 2 + kind) * 128, 128), 128)


def forward(chain):
    next(chain, None)


def run(chains, order):
    for name in "".join(order):
        next(chains[name], None)
    for chain in chains.values():
        for _ in chain:
            pass


def start(copies):
    for copy in copies:
        copy.start()
    return copies


def sequence_starts(lengths, at, rows):
    index = lax.broadcasted_iota(jnp.int32, (rows, 1), 0) + at
    limit, first = lengths[0, 0], jnp.zeros((rows, 1), jnp.int32)
    for s in range(8):
        first = jnp.where(index >= limit, limit, first)
        if s < 7:
            limit = limit + lengths[0, s + 1]
    return index, first


def params(collective, mib=58):
    return pltpu.CompilerParams(collective_id=collective, has_side_effects=True, vmem_limit_bytes=mib << 20)


def sems(n, local):
    return [pltpu.SemaphoreType.DMA((n,)), pltpu.SemaphoreType.DMA((n,)), pltpu.SemaphoreType.DMA((local,))]


FRONT_ORDER = (
    "twobbbbttttcttoowwwoowwwwtdowtoooottddddcctooooo",
    "ttccddduddcoottttdddduuttuuddduuuttthuuhtuuutuut",
    "ututtttttzztgtggggzztggiggggggiiziimgmzzzzmmmmii",
    "iimiimiizgzggizzigiziqiq",
)
BACK_ORDER = (
    "emeeeetteeeetttttttttteeeeewwwtwwewwtttmmstwwwte",
    "ewtsswwmestsw",
)


TILES = ((0, 256), (256, 256), (512, 176))


def front_kernel(tok, cot, lengths, gain, mlp_gain, rates, wq, wk, wv, wo, wg, wu, wd,
                 n1_out, w_out, q_out, k_out, v_out, p_out, table_out, h1_out, dh1_out, do_out, m_out, od_grad, gain_part, gu_grad,
                 wo_turned, n1, w, q, k, v, p, table, h1, dh1, o, branches, branches_turned, w1, w2, g, n2, dgate, turned, da, do, sums, got,
                 sib, got_half, got_up, got_down, last, send_sems, recv_sems, local):
    net = Net(send_sems, recv_sems)
    bf, f32 = jnp.bfloat16, jnp.float32
    net.greet([net.device(dx=s) for s in (1, 2, 3)] + [net.device(dy=1), net.device(dy=-1), net.device(dz=1), net.device(dz=-1), net.device(dc=1)])
    hid, dup = 0, 1024
    own_rows = att_at(net, net.c, 0, 0)
    own_od, own_gu = plane_slab(net, w1, net.c, 0, 0), plane_slab(net, w2, net.c, 0, 0)
    wo_turned[...] = wo[...].T
    own = start(
        [
            pltpu.make_async_copy(src, dst, local.at[n])
            for n, (src, dst) in enumerate(
                (
                    (wq, w.at[0, own_rows, :]), (wk, w.at[1, own_rows, :]), (wv, w.at[2, own_rows, :]),
                    (wo_turned, own_od.at[pl.ds(0, 256), :]), (wd, own_od.at[pl.ds(256, FFB), :]),
                    (wg, own_gu.at[pl.ds(0, FFB), :]), (wu, own_gu.at[pl.ds(FFB, FFB), :]), (cot, g.at[block(net.z), :]),
                )
            )
        ]
    )

    def norm(at, _):
        here = pl.ds(at, 16)
        value = tok[here, :].astype(f32)
        r = lax.rsqrt(jnp.mean(value * value, axis=-1, keepdims=True) + EPS)
        n1[pl.ds(pl.multiple_of(net.t * ROWS + at, 16), 16), :] = (value * r * gain[...]).astype(bf)

    each_half(norm)
    net.met()
    part, m_part = n1.at[pl.ds(0, 512), :], n1.at[pl.ds(512, 512), :]
    saves = {}

    def save(n, src, dst):
        saves[n] = pltpu.make_async_copy(src, dst, local.at[n])
        saves[n].start()

    def project(i, _):
        here = pl.ds(pl.multiple_of(i * QROWS, QROWS), QROWS)
        left = n1[here, :]
        cos, sin = table[0, here, :], table[1, here, :]
        for m, dst in ((0, q), (1, k)):
            u = jnp.dot(left, w[m], preferred_element_type=f32)
            for h in range(2):
                uh = u[:, h * 128 : h * 128 + 128]
                dst[h, here, :] = (uh * cos + pltpu.roll(uh, 64, 1) * sin).astype(bf)
        u = jnp.dot(left, w[2], preferred_element_type=f32).astype(bf)
        for h in range(2):
            v[h, here, :] = u[:, h * 128 : h * 128 + 128]
        return 0

    def attend(b, heads=(0, 1)):
        rows = slice(b * QROWS, b * QROWS + QROWS)
        first, until = max(0, b - 2) * QROWS, (b + 1) * QROWS
        index, begin = sequence_starts(lengths, b * QROWS, QROWS)
        key = lax.broadcasted_iota(jnp.int32, (QROWS, until - first), 1) + first
        allowed = (key <= index) & (key >= begin)
        for h in heads:
            s = lax.dot_general(q[h, rows, :], k[h, first:until, :], NT, preferred_element_type=f32)
            s = jnp.where(allowed, s * HEAD_DIM ** (-0.5), -1e30)
            e = jnp.exp(s - jnp.max(s, axis=-1, keepdims=True))
            weights = (e / jnp.sum(e, axis=-1, keepdims=True)).astype(bf)
            p[(h * 4 + b) * QROWS : (h * 4 + b + 1) * QROWS, 0 : until - first] = weights
            o[rows, h * 128 : h * 128 + 128] = jnp.dot(weights, v[h, first:until, :], preferred_element_type=f32).astype(bf)

    def exchange(n, at, size):
        src = o.at[pl.ds(pl.multiple_of((1 - net.xl) * 512 + n * QROWS, QROWS), QROWS), pl.ds(at, size)]
        return net.send(src, branches.at[net.xl, pl.ds(n * QROWS, QROWS), pl.ds(at, size)], net.beside)

    def branch(z):
        here = block(z)
        u = jnp.dot(branches[0, here, :], w1[0, :256, :], preferred_element_type=f32)
        u = u + jnp.dot(branches[1, here, :], w1[1, :256, :], preferred_element_type=f32)
        part[here, :] = u.astype(bf)

    def second_norm(at, half_at):
        here = pl.ds(at, 16)
        h = tok[here, :].astype(f32) + reduced(net, part, got, at, half_at)
        h1[here, :] = h
        r = lax.rsqrt(jnp.mean(h * h, axis=-1, keepdims=True) + EPS)
        n2[pl.ds(pl.multiple_of(net.z * ROWS + at, 16), 16), :] = (h * r * mlp_gain[...]).astype(bf)

    def ahead(b):
        for at, n in TILES:
            gate = lax.dot_general(n2[...], w2[b, at : at + n, :], NT, preferred_element_type=f32)
            up = lax.dot_general(n2[...], w2[b, FFB + at : FFB + at + n, :], NT, preferred_element_type=f32)
            dh = dgate[b, :, at : at + n].astype(f32)
            sig = jax.nn.sigmoid(gate)
            act = gate * sig
            dg, du, hi = (dh * up * sig * (1.0 + gate * (1.0 - sig))).astype(bf), (dh * act).astype(bf), (act * up).astype(bf)
            dgate[b, :, at : at + n] = dg
            p[dup + b * 512 : dup + b * 512 + 512, at : at + n] = du
            p[hid + b * 512 : hid + b * 512 + 512, at : at + n] = hi
            for m, value in enumerate((dg, du, hi)):
                turned[m, b, at : at + n, :] = value.T

    def back(i, _):
        at = pl.ds(pl.multiple_of(i * 256, 256), 256)
        d = jnp.dot(dgate[0], w2[0, :FFB, at], preferred_element_type=f32)
        d = d + jnp.dot(dgate[1], w2[1, :FFB, at], preferred_element_type=f32)
        d = d + jnp.dot(p[dup : dup + 512, :FFB], w2[0, FFB:, at], preferred_element_type=f32)
        d = d + jnp.dot(p[dup + 512 : dup + 1024, :FFB], w2[1, FFB:, at], preferred_element_type=f32)
        part[:, at] = d.astype(bf)
        return 0

    def outer(m, i):
        at = pl.ds(i * 512, 512)
        for b in range(2):
            w2[b, m * FFB : m * FFB + FFB, at] = jnp.dot(turned[m, b], n2[:, at], preferred_element_type=f32).astype(bf)

    lanes = {name: net.lane() for name in "twoducaxyzg"}
    back_a = reduce_z(lanes["x"], part, sums, got, pl.ds(0, D // 2))
    back_b = reduce_z(lanes["y"], part, sums, got, pl.ds(D // 2, D // 2))

    def main():
        yield from gather_8(lanes["t"], n1)
        yield
        save(8, n1, n1_out)
        save(9, w, w_out)
        save(10, table, table_out)
        lax.fori_loop(0, 2, project, 0)
        yield
        lax.fori_loop(2, 4, project, 0)
        for n, (src, dst) in enumerate(((q, q_out), (k, k_out), (v, v_out))):
            save(11 + n, src, dst)
        yield
        attend(0)
        yield
        attend(2)
        swapped = [exchange(0, 0, 256)]
        for h in (0, 1):
            yield
            attend(1, (h,))
            attend(3, (h,))
            swapped.append(exchange(1, h * 128, 128))
        kept = pltpu.make_async_copy(o.at[pl.ds(pl.multiple_of(net.xl * 512, 512), 512), :], branches.at[net.xl], local.at[15])
        kept.start()
        save(14, p, p_out)
        yield
        for sent in swapped:
            sent.wait_recv()
        kept.wait()
        saves.pop(8).wait()
        lanes["t"].flush()
        yield from reduce_z(lanes["a"], part, sums, got, make=branch)
        yield
        yield from gather_z(lanes["z"], lambda k: n2.at[half(net.z, k), :], n2, functools.partial(on_half, second_norm))
        save(23, h1, h1_out)
        lanes["a"].flush()
        saves.pop(14).wait()
        yield
        ahead(0)
        yield
        ahead(1)
        yield
        lax.fori_loop(0, 4, back, 0)
        forward(back_a)
        yield
        lax.fori_loop(4, 8, back, 0)
        forward(back_b)
        lanes["u"].flush()
        for i in range(4):
            yield
            outer(i // 2, i % 2 * 2)
            outer(i // 2, i % 2 * 2 + 1)

    def norm_back(at, half_at):
        here = pl.ds(at, 16)
        h = h1[here, :]
        r = lax.rsqrt(jnp.mean(h * h, axis=-1, keepdims=True) + EPS)
        d = reduced(net, part, got, at, half_at)
        inner = d * mlp_gain[...]
        grad = r * inner - h * (r * r * r) * jnp.mean(h * inner, axis=-1, keepdims=True)
        grad = cot[here, :].astype(f32) + grad
        dh1[here, :] = grad
        da[pl.ds(pl.multiple_of(net.z * ROWS + at, 16), 16), :] = grad.astype(bf)
        gain_part[...] += jnp.sum(d * h * r, axis=0, keepdims=True)

    swapped_back = []

    def back_out(z):
        here = block(z)
        for b in range(2):
            do[b, here, :] = lax.dot_general(da[here, :], w1[b, :256, :], NT, preferred_element_type=f32).astype(bf)
        rows = pl.ds(pl.multiple_of(net.xl * 512 + lax.rem(z + 8, 4) * ROWS, ROWS), ROWS)
        swapped_back.append(net.send(do.at[1 - net.xl, here, :], do_out.at[rows, :], net.beside))
        save(15 + len(swapped_back), do.at[net.xl, here, :], do_out.at[rows, :])

    def tail():
        for chain in (back_a, back_a, back_b, back_b, back_a):
            forward(chain)
            yield
        forward(back_b)
        gain_part[...] = jnp.zeros_like(gain_part)
        yield
        yield from gather_z(lanes["z"], lambda k: da.at[half(net.z, k), :], da, functools.partial(on_half, norm_back), back_out)
        save(24, dh1, dh1_out)

    def weights():
        for copied in own[:3]:
            copied.wait()
        yield from gather_plane(lanes["w"], lambda i, j: w.at[:, att_at(net, net.c, i, j), :], ATT_CUT, (net.across,), (net.device(dy=1), net.device(dy=-1)))

    def plane(lane, held, ref, at, cut, rows):
        for copied in held:
            copied.wait()
        yield from gather_plane(
            lane, lambda i, j: plane_slab(net, ref, net.c, i, j).at[pl.ds(at, rows), :], cut_at(cut, rows), net.along(True), net.along(False)
        )

    def cotangent():
        own[7].wait()
        yield from gather_z(lanes["c"], lambda k: cot.at[pl.ds(k * 64, 64), :], g)

    def hidden_grad():
        for b in range(2):
            if b:
                yield
            for at, n in TILES:
                u = lax.dot_general(g[...], w1[b, 256 + at : 256 + at + n, :], NT, preferred_element_type=f32)
                dgate[b, :, at : at + n] = u.astype(bf)

    def tables():
        def rows(i, _):
            at = pl.multiple_of(i * 128, 128)
            index, first = sequence_starts(lengths, at, 128)
            angle = (index - first).astype(f32) * rates[...]
            lane = lax.broadcasted_iota(jnp.int32, (128, 128), 1)
            table[0, pl.ds(at, 128), :] = jnp.cos(angle)
            sin = jnp.sin(angle)
            table[1, pl.ds(at, 128), :] = jnp.where(lane < 64, -sin, sin)
            return 0

        for i in range(4):
            if i:
                yield
            lax.fori_loop(2 * i, 2 * i + 2, rows, 0)

    def mixed_part():
        def columns(i, _):
            at = pl.ds(pl.multiple_of(i * 256, 256), 256)
            u = jnp.dot(p[hid : hid + 512, :FFB], w1[0, 256:, at], preferred_element_type=f32)
            u = u + jnp.dot(p[hid + 512 : hid + 1024, :FFB], w1[1, 256:, at], preferred_element_type=f32)
            m_part[:, at] = u.astype(bf)
            return 0

        for i in range(4):
            lax.fori_loop(2 * i, 2 * i + 2, columns, 0)
            yield
        save(20, m_part, m_out)
        for b in range(2):
            branches_turned[b] = branches[b].T
        lanes["d"].flush()
        for i in range(4):
            if i:
                yield
            at = pl.ds(i * 512, 512)
            for b in range(2):
                w1[b, 256:, at] = jnp.dot(turned[2, b], g[:, at], preferred_element_type=f32).astype(bf)
        save(21, w1.at[:, pl.ds(256, FFB), :], od_grad.at[:, pl.ds(256, FFB), :])

    def outer_out():
        lanes["o"].flush()

        def columns(i, _):
            at = pl.ds(pl.multiple_of(i * 512, 512), 512)
            for b in range(2):
                w1[b, :256, at] = jnp.dot(branches_turned[b], da[:, at], preferred_element_type=f32).astype(bf)
            return 0

        lax.fori_loop(0, 4, columns, 0)
        save(22, w1.at[:, pl.ds(0, 256), :], od_grad.at[:, pl.ds(0, 256), :])
        yield
        for sent in swapped_back:
            sent.wait_recv()

    def grads(m):
        def slab(kind):
            return lambda i, j: plane_slab(net, w2, kind, i, j).at[pl.ds(m * FFB, FFB), :]

        yield from reduce_plane(
            lanes["g"], slab(net.c), slab(1 - net.c),
            lambda i, j: sib.at[m, i, j], lambda i: got_half.at[m, i], lambda i: got_up.at[m, i], lambda i: got_down.at[m, i], lambda i: last.at[m, i],
            cut_at(FF_CUT, FFB), add_in(FF_CUT, FFB), net.along(True), net.along(False),
        )

    run(
        {
            "t": main(), "z": tail(), "w": weights(), "o": plane(lanes["o"], own[3:4], w1, 0, OUT // 2, OUT),
            "d": plane(lanes["d"], own[4:5], w1, OUT, FF_CUT, FFB), "u": plane(lanes["u"], own[5:7], w2, 0, GU_CUT, GU),
            "c": cotangent(), "h": hidden_grad(), "b": tables(), "m": mixed_part(), "q": outer_out(), "g": grads(0), "i": grads(1),
        },
        FRONT_ORDER,
    )
    gu_grad[...] = plane_slab(net, w2, net.c, 0, 0)[...]
    for saved in saves.values():
        saved.wait()
    net.finish()


def front(*args):
    bf, f32 = jnp.bfloat16, jnp.float32
    slab = (GU, 128)
    kept = (
        ((GROUP, D), bf), ((3, D, 256), bf), ((2, GROUP, 128), bf), ((2, GROUP, 128), bf), ((2, GROUP, 128), bf),
        ((2 * GROUP, 768), bf), ((2, GROUP, 128), f32),
    )
    kept += (((ROWS, D), f32), ((ROWS, D), f32))
    outs = kept + (((GROUP, 256), bf), ((512, D), bf), ((2, OD, D), bf), ((1, D), f32), (slab, bf))
    scratch = (((256, 128), bf),) + kept + (
        ((GROUP, 256), bf), ((2, 512, 256), bf), ((2, 256, 512), bf), ((2, OD, D), bf), ((2, GU, D), bf), ((512, D), bf), ((512, D), bf),
        ((2, 512, FFB), bf), ((3, 2, FFB, 512), bf), ((512, D), bf), ((2, 512, 256), bf), ((2, 64, D), bf), ((6, 64, D), bf),
        ((2, 4, 4, FFB, 128), bf), ((2, 4, FFB, 128), bf), ((2, 4, FFB, 128), bf), ((2, 4, FFB, 128), bf), ((2, 3, FFB, 128), bf),
    )
    return pl.pallas_call(
        front_kernel,
        name="front",
        out_shape=tuple(jax.ShapeDtypeStruct(*s) for s in outs),
        in_specs=[VMEM, VMEM, pl.BlockSpec(memory_space=pltpu.SMEM), VMEM, VMEM, VMEM, ANY, ANY, ANY, VMEM, ANY, ANY, ANY],
        out_specs=(ANY,) * 12 + (VMEM, VMEM),
        scratch_shapes=[pltpu.VMEM(*s) for s in scratch] + sems(272, 25),
        compiler_params=params(1, 64),
    )(*args)


def back_kernel(do_in, n1_in, w_in, q_in, k_in, v_in, p_in, table_in, m_in, od_in, tok_in, h1_in, dh1_in, gain, mlp_gain_part,
                    mixed, dx, gains, qkv_grad, od_grad,
                    tok, h1, dh1, do, n1, w, q, k, v, p, table, dqkv, dqkv_turned, dk, dv, part, sums, got, sums_half, got_half,
                    ga, sib, slab_half, slab_up, slab_down, slab_last, sum_z, sum_x, sum_y, sum_c,
                    m_part, sums_m, got_m, od, od_sib, od_half, od_up, od_down, od_last,
                    send_sems, recv_sems, local):
    net = Net(send_sems, recv_sems)
    bf, f32 = jnp.bfloat16, jnp.float32
    line_x = [net.device(dx=s) for s in (1, 2, 3)]
    line_y = [net.device(dy=s) for s in (1, 2, 3)]
    line_z = [net.device(dz=s) for s in (1, 2, 3)]
    net.greet(line_x + line_y + line_z + [net.device(dc=1)])
    loads = start(
        [
            pltpu.make_async_copy(src, dst, local.at[m])
            for m, (src, dst) in enumerate(
                (
                    (m_in, m_part), (do_in, do), (v_in, v), (p_in, p), (q_in, q), (k_in, k), (table_in, table), (w_in, w), (n1_in, n1),
                    (h1_in, h1), (tok_in, tok), (dh1_in, dh1),
                )
            )
        ]
    )
    slabs = start(
        [
            pltpu.make_async_copy(plane_slab(net, od_in, net.c, i, j), od.at[i, j], local.at[12 + n])
            for n, (i, j) in enumerate((i, j) for j in (2, 1, 3, 0) for i in (2, 3, 1, 0))
        ]
    )
    net.met()

    def attend_back(h, b):
        rows = slice(b * QROWS, b * QROWS + QROWS)
        first, until = max(0, b - 2) * QROWS, (b + 1) * QROWS
        keys, old = slice(first, until), slice(first, b * QROWS)
        weights_b = p[(h * 4 + b) * QROWS : (h * 4 + b + 1) * QROWS, 0 : until - first]
        do_b = do[rows, h * 128 : h * 128 + 128]
        dp = lax.dot_general(do_b, v[h, keys, :], NT, preferred_element_type=f32)
        wide = weights_b.astype(f32)
        centre = jnp.sum(wide * dp, axis=-1, keepdims=True)
        ds = (wide * (dp - centre)).astype(bf)
        dvb = lax.dot_general(weights_b, do_b, TN, preferred_element_type=f32)
        dkb = lax.dot_general(ds, q[h, rows, :], TN, preferred_element_type=f32)
        if b > 0:
            dv[h, old, :] += dvb[: b * QROWS - first]
            dk[h, old, :] += dkb[: b * QROWS - first]
        dv[h, rows, :] = dvb[b * QROWS - first :]
        dk[h, rows, :] = dkb[b * QROWS - first :]
        dqb = jnp.dot(ds, k[h, keys, :], preferred_element_type=f32) * HEAD_DIM ** (-0.5)
        dqb = dqb * table[0, rows, :] - pltpu.roll(dqb, 64, 1) * table[1, rows, :]
        dqkv[rows, h * 128 : h * 128 + 128] = dqb.astype(bf)

    def turn(i, _):
        here = pl.ds(pl.multiple_of(i * QROWS, QROWS), QROWS)
        for h in range(2):
            u = dk[h, here, :] * HEAD_DIM ** (-0.5)
            u = u * table[0, here, :] - pltpu.roll(u, 64, 1) * table[1, here, :]
            dqkv[here, 256 + h * 128 : 384 + h * 128] = u.astype(bf)
            dqkv[here, 512 + h * 128 : 640 + h * 128] = dv[h, here, :].astype(bf)
        dqkv_turned[:, here] = dqkv[here, :].T
        return 0

    def make(xl, z):
        here = block8(xl, z)
        left = dqkv[here, :]

        def columns(i, _):
            at = pl.ds(pl.multiple_of(i * 512, 512), 512)
            u = lax.dot_general(left[:, :256], w[0, at, :], NT, preferred_element_type=f32)
            u = u + lax.dot_general(left[:, 256:512], w[1, at, :], NT, preferred_element_type=f32)
            u = u + lax.dot_general(left[:, 512:], w[2, at, :], NT, preferred_element_type=f32)
            part[here, at] = u.astype(bf)
            sum_y[net.y, 0:1, at] += jnp.sum(u * n1[here, at].astype(f32), axis=0, keepdims=True)
            return 0

        lax.fori_loop(0, 4, columns, 0)

    out = []

    def step(at, k):
        here = pl.ds(at, 16)
        value = tok[here, :].astype(f32)
        r = lax.rsqrt(jnp.mean(value * value, axis=-1, keepdims=True) + EPS)
        inner = out[0](at, k) * gain[...]
        dx[here, :] = dh1[here, :] + r * inner - value * (r * r * r) * jnp.mean(value * inner, axis=-1, keepdims=True)

    def main():
        for copied in loads[1:7]:
            copied.wait()
        yield
        for b in range(GROUP // QROWS):
            for h in range(2):
                attend_back(h, b)
            yield
        lax.fori_loop(0, GROUP // QROWS, turn, 0)
        for copied in loads[7:9]:
            copied.wait()
        sum_y[net.y, 0:1, :] = jnp.zeros((1, D), f32)
        sum_y[net.y, 1:2, :] = mlp_gain_part[...]
        yield
        yield from reduce_8(net, make, part, sums, got, sums_half, got_half, out)
        for copied in loads[10:]:
            copied.wait()
        each_half(step)

    def early():
        chain = reduce_plane(
            net, lambda i, j: od.at[i, j], lambda i, j: plane_slab(net, od_in, 1 - net.c, i, j), lambda i, j: od_sib.at[i, j],
            lambda i: od_half.at[i], lambda i: od_up.at[i], lambda i: od_down.at[i], lambda i: od_last.at[i],
            cut_at(OD_CUT, OD), add_in(OD_CUT, OD), net.along(True), net.along(False),
        )
        forward(chain)
        yield
        for copied in slabs:
            copied.wait()
        yield from chain
        od_grad[...] = od[0, 0]

    def mixing():
        loads[0].wait()
        yield from reduce_z(net, m_part, sums_m, got_m)

        def mix(at, k):
            here = pl.ds(at, 16)
            mixed[here, :] = (h1[here, :] + reduced(net, m_part, got_m, at, k)).astype(bf)

        loads[9].wait()
        each_half(mix)

    def slab(kind):
        return lambda i, j: ga.at[:, att_at(net, kind, i, j)]

    def weights():
        def outer(i, _):
            at = pl.ds(pl.multiple_of(i * 256, 256), 256)
            ga[:, at] = jnp.dot(dqkv_turned[...], n1[:, at], preferred_element_type=f32).astype(bf)
            return 0

        for i in range(4):
            lax.fori_loop(2 * i, 2 * i + 2, outer, 0)
            yield
        yield from reduce_plane(
            net, slab(net.c), slab(1 - net.c), lambda i, j: sib.at[i, j], lambda i: slab_half.at[i], lambda i: slab_up.at[i],
            lambda i: slab_down.at[i], lambda i: slab_last.at[i], cut_at(QKV_CUT, QKV), add_in(QKV_CUT, QKV), (net.across,), (net.device(dy=1), net.device(dy=-1)),
        )
        qkv_grad[...] = slab(net.c)(0, 0)[...]

    def gain_sums():
        here = net.y
        stages = ((sum_y, line_y, sum_c, net.c), (sum_c, [net.device(dc=1)], sum_x, net.x), (sum_x, line_x, sum_z, net.z), (sum_z, line_z, None, None))
        for ref, line, then, place in stages:
            sent = [net.send(ref.at[here], ref.at[here], to) for to in line]
            yield
            for copied in sent:
                copied.wait_recv()
            total = ref[0]
            for n in range(1, len(line) + 1):
                total = total + ref[n]
            if then is None:
                gains[0:1, :] = total[0:1] / gain[...]
                gains[1:2, :] = total[1:2]
            else:
                then[place] = total
                here = place

    run({"t": main(), "m": mixing(), "e": early(), "w": weights(), "s": gain_sums()}, BACK_ORDER)
    net.finish()


def back(do, n1, w, q, k, v, p, table, m, od, tok, h1, dh1, gain, mlp_gain_part):
    bf, f32 = jnp.bfloat16, jnp.float32
    slab, slab_od = (QKV, 128), (OD, 128)
    scratch = [
        ((ROWS, D), bf), ((ROWS, D), f32), ((ROWS, D), f32),
        ((GROUP, 256), bf), ((GROUP, D), bf), ((3, D, 256), bf), ((2, GROUP, 128), bf), ((2, GROUP, 128), bf), ((2, GROUP, 128), bf),
        ((2 * GROUP, 768), bf), ((2, GROUP, 128), f32), ((GROUP, QKV), bf), ((QKV, GROUP), bf),
        ((2, GROUP, 128), f32), ((2, GROUP, 128), f32), ((GROUP, D), bf), ((2, ROWS, D), bf), ((4, ROWS, D), bf),
        ((2, 64, D), bf), ((6, 64, D), bf), ((QKV, D), bf), ((2, 4) + slab, bf), ((2,) + slab, bf), ((2,) + slab, bf),
        ((2,) + slab, bf), ((1,) + slab, bf), ((4, 2, D), f32), ((4, 2, D), f32), ((4, 2, D), f32), ((2, 2, D), f32),
        ((512, D), bf), ((2, 64, D), bf), ((6, 64, D), bf), ((4, 4) + slab_od, bf), ((4, 4) + slab_od, bf),
        ((4,) + slab_od, bf), ((4,) + slab_od, bf), ((4,) + slab_od, bf), ((3,) + slab_od, bf),
    ]
    outs = (((ROWS, D), bf), ((ROWS, D), f32), ((2, D), f32), (slab, bf), (slab_od, bf))
    return pl.pallas_call(
        back_kernel,
        name="back",
        out_shape=tuple(jax.ShapeDtypeStruct(*s) for s in outs),
        in_specs=[ANY] * 13 + [VMEM] * 2,
        out_specs=(VMEM,) * 5,
        scratch_shapes=[pltpu.VMEM(*s) for s in scratch] + sems(128, 28),
        compiler_params=params(2),
    )(do, n1, w, q, k, v, p, table, m, od, tok, h1, dh1, gain, mlp_gain_part)


def finish_kernel(mixed_in, dx_in, gains_in, qkv_in, od_in, gu_in, mixed, dx, ag, gq, gk, gv, go, mg, gg, gu_out, gd, gains, qkv, od, gu, sems):
    f32 = jnp.float32
    pairs = ((gu_in, gu), (od_in, od), (qkv_in, qkv), (gains_in, gains), (mixed_in, mixed), (dx_in, dx))
    loads = start([pltpu.make_async_copy(src, dst, sems.at[n]) for n, (src, dst) in enumerate(pairs)])
    for load in loads[:4]:
        load.wait()
    gg[...] = gu[:FFB, :].astype(f32)
    gu_out[...] = gu[FFB:, :].astype(f32)
    go[...] = od[:256, :].astype(f32).T
    gd[...] = od[256:, :].astype(f32)
    for n, dst in enumerate((gq, gk, gv)):
        dst[...] = qkv[n * 256 : n * 256 + 256, :].astype(f32).T
    ag[...] = gains[0:1, :]
    mg[...] = gains[1:2, :]
    for load in loads[4:]:
        load.wait()


def finish(mixed, dx, gains, qkv, od, gu):
    f32, bf = jnp.float32, jnp.bfloat16
    outs = (
        ((ROWS, D), bf), ((ROWS, D), f32), ((1, D), f32), ((ROWS, 256), f32), ((ROWS, 256), f32), ((ROWS, 256), f32),
        ((ROWS, 256), f32), ((1, D), f32), ((FFB, 128), f32), ((FFB, 128), f32), ((FFB, 128), f32),
    )
    held = (((2, D), f32), ((QKV, 128), bf), ((OD, 128), bf), ((GU, 128), bf))
    return pl.pallas_call(
        finish_kernel,
        name="finish",
        out_shape=tuple(jax.ShapeDtypeStruct(*s) for s in outs),
        in_specs=[ANY] * 6,
        out_specs=(VMEM,) * 11,
        scratch_shapes=[pltpu.VMEM(*s) for s in held] + [pltpu.SemaphoreType.DMA((6,))],
        compiler_params=pltpu.CompilerParams(vmem_limit_bytes=60 << 20),
    )(mixed, dx, gains, qkv, od, gu)


def shards(
    tokens,
    lengths,
    attn_gain,
    query_weight,
    key_weight,
    value_weight,
    out_weight,
    mlp_gain,
    gate_weight,
    up_weight,
    down_weight,
    cotangent,
):
    half_rates = THETA ** (-(np.arange(64, dtype=np.float32) * np.float32(2.0 / HEAD_DIM)))
    rates = jnp.asarray(np.concatenate([half_rates, half_rates])[None].astype(np.float32))
    n1, w, q, k, v, p, table, h1, dh1, do, m, od_part, gain_part, gu = front(
        tokens, cotangent, lengths, attn_gain[None], mlp_gain[None], rates, query_weight, key_weight, value_weight, out_weight,
        gate_weight.T, up_weight.T, down_weight.T,
    )
    mixed, dx, gains, qkv, od_grad = back(do, n1, w, q, k, v, p, table, m, od_part, tokens, h1, dh1, attn_gain[None], gain_part)
    mixed, dx, ag, gq, gk, gv, go, mg, gg, gu, gd = finish(mixed, dx, gains, qkv, od_grad, gu)
    return (mixed, dx, ag[0], gq, gk, gv, go, mg[0], gg.T, gu.T, gd.T)


def solution(mesh):
    return jax.shard_map(
        shards,
        mesh=mesh,
        in_specs=(
            P(("dp", "tensor"), None),
            P("dp", None),
            P(),
            P("dp", "tensor"),
            P("dp", "tensor"),
            P("dp", "tensor"),
            P("dp", "tensor"),
            P(),
            P("dp", "tensor"),
            P("dp", "tensor"),
            P("dp", "tensor"),
            P(("dp", "tensor"), None),
        ),
        out_specs=(
            P(("dp", "tensor"), None),
            P(("dp", "tensor"), None),
            P(),
            P("dp", "tensor"),
            P("dp", "tensor"),
            P("dp", "tensor"),
            P("dp", "tensor"),
            P(),
            P("dp", "tensor"),
            P("dp", "tensor"),
            P("dp", "tensor"),
        ),
        check_vma=False,
    )
```

```python
import copy
import functools

import jax
import jax.numpy as jnp
import numpy as np
from jax import lax
from jax.experimental import pallas as pl
from jax.experimental.pallas import tpu as pltpu
from jax.sharding import PartitionSpec as P

HEAD_DIM = 128
EPS = 1e-05
THETA = 10000.0
D = 2048
ROWS = 128
GROUP = 1024
FFB = 688
QROWS = 256
MESH = pl.DeviceIdType.MESH
ANY = pl.BlockSpec(memory_space=pl.ANY)
VMEM = pl.BlockSpec(memory_space=pltpu.VMEM)
NT = (((1,), (1,)), ((), ()))
TN = (((0,), (0,)), ((), ()))


class Net:
    def __init__(self, send_sems, recv_sems):
        dp, t = lax.axis_index("dp"), lax.axis_index("tensor")
        self.y, self.c = lax.div(dp, 4), lax.rem(dp, 2)
        self.xl, self.z = lax.div(t, 4), lax.rem(t, 4)
        self.x = lax.rem(lax.div(dp, 2), 2) * 2 + self.xl
        self.dp, self.t = dp, t
        self.send_sems, self.recv_sems = send_sems, recv_sems
        self.used = [0]
        self.sent = []
        self.lanes = [self]

    def lane(self):
        other = copy.copy(self)
        other.sent = []
        self.lanes.append(other)
        return other

    def device(self, dx=0, dy=0, dz=0, dc=0):
        x, y = lax.rem(self.x + dx + 4, 4), lax.rem(self.y + dy + 4, 4)
        z, c = lax.rem(self.z + dz + 4, 4), lax.rem(self.c + dc, 2)
        return (y * 4 + lax.div(x, 2) * 2 + c, lax.rem(x, 2) * 4 + z)

    @property
    def beside(self):
        return (self.dp, (1 - self.xl) * 4 + self.z)

    @property
    def across(self):
        return self.device(dx=2)

    def along(self, first):
        on_x = self.c == (0 if first else 1)
        both = []
        for step in (1, -1):
            by_x, by_y = self.device(dx=step), self.device(dy=step)
            both.append(tuple(jnp.where(on_x, u, v) for u, v in zip(by_x, by_y)))
        return both

    def send(self, src, dst, to):
        k = self.used[0]
        self.used[0] += 1
        sent = pltpu.make_async_remote_copy(
            src_ref=src,
            dst_ref=dst,
            send_sem=self.send_sems.at[k],
            recv_sem=self.recv_sems.at[k],
            device_id=to,
            device_id_type=MESH,
        )
        sent.start()
        self.sent.append(sent)
        return sent

    def flush(self):
        for sent in self.sent:
            sent.wait_send()
        self.sent.clear()

    def finish(self):
        for lane in self.lanes:
            lane.flush()

    def greet(self, devices):
        for device in devices:
            pl.semaphore_signal(pltpu.get_barrier_semaphore(), inc=1, device_id=device, device_id_type=MESH)
        self.greeted = len(devices)

    def met(self):
        pl.semaphore_wait(pltpu.get_barrier_semaphore(), self.greeted)


def block(z):
    return pl.ds(pl.multiple_of(lax.rem(z + 8, 4) * ROWS, ROWS), ROWS)


def half(z, k):
    return pl.ds(pl.multiple_of(lax.rem(z + 8, 4) * ROWS + k * 64, 64), 64)


def block8(xl, z):
    return pl.ds(pl.multiple_of((xl * 4 + lax.rem(z + 8, 4)) * ROWS, ROWS), ROWS)


def half8(xl, z, k):
    return pl.ds(pl.multiple_of((xl * 4 + lax.rem(z + 8, 4)) * ROWS + k * 64, 64), 64)


def add_rows(rows, dst, *terms):
    def step(i, _):
        at = pl.ds(pl.multiple_of(i * 16, 16), 16)
        total = terms[0][at, :].astype(jnp.float32)
        for term in terms[1:]:
            total = total + term[at, :].astype(jnp.float32)
        dst[at, :] = total.astype(dst.dtype)
        return 0

    lax.fori_loop(0, rows // 16, step, 0)


def gather_z(net, own, dst, fill=None, arrived=None):
    up, down = net.device(dz=1), net.device(dz=-1)
    z = net.z
    place = [dst.at[half(z, k), :] for k in (0, 1)]
    if fill:
        fill(0)
    up_0 = net.send(own(0), place[0], up)
    if fill:
        yield
        fill(1)
    down_1 = net.send(own(1), place[1], down)
    up_1 = net.send(own(1), place[1], up)
    down_0 = net.send(own(0), place[0], down)
    yield
    if arrived:
        arrived(z)
        yield
    up_0.wait_recv()
    ref = dst.at[half(z - 1, 0), :]
    on_0 = net.send(ref, ref, up)
    yield
    down_1.wait_recv()
    ref = dst.at[half(z + 1, 1), :]
    on_1 = net.send(ref, ref, down)
    yield
    up_1.wait_recv()
    if arrived:
        arrived(z - 1)
    yield
    down_0.wait_recv()
    if arrived:
        arrived(z + 1)
    yield
    on_0.wait_recv()
    on_1.wait_recv()
    if arrived:
        arrived(z + 2)


def reduce_z(net, part, sums, got, cols=pl.ds(0, D), make=None):
    up, down = net.device(dz=1), net.device(dz=-1)
    z = net.z
    if make:
        make(z + 2)
    c0 = net.send(part.at[half(z + 2, 0), cols], got.at[0, :, cols], up)
    c1 = net.send(part.at[half(z + 2, 1), cols], got.at[1, :, cols], down)
    if make:
        yield
        make(z + 1)
    d1 = net.send(part.at[half(z + 1, 1), cols], got.at[3, :, cols], up)
    if make:
        yield
        make(z - 1)
    d2 = net.send(part.at[half(z - 1, 0), cols], got.at[4, :, cols], down)
    if make:
        yield
        make(z)
    yield
    c0.wait_recv()
    add_rows(64, sums.at[0, :, cols], part.at[half(z + 1, 0), cols], got.at[0, :, cols])
    d0 = net.send(sums.at[0, :, cols], got.at[2, :, cols], up)
    yield
    c1.wait_recv()
    add_rows(64, sums.at[1, :, cols], part.at[half(z - 1, 1), cols], got.at[1, :, cols])
    d3 = net.send(sums.at[1, :, cols], got.at[5, :, cols], down)
    yield
    for sent in (d0, d1, d2, d3):
        sent.wait_recv()


def reduced(net, part, got, at, k):
    here = pl.ds(pl.multiple_of(at - 64 * k, 16), 16)
    total = part[pl.ds(pl.multiple_of(net.z * ROWS + at, 16), 16), :].astype(jnp.float32)
    return total + got[2 + k, here, :].astype(jnp.float32) + got[4 + k, here, :].astype(jnp.float32)


def gather_8(net, dst):
    up, down, beside = net.device(dz=1), net.device(dz=-1), net.beside
    xl, z = net.xl, net.z

    def send(x, dz, k, to):
        ref = dst.at[half8(x, z + dz, k), :]
        return net.send(ref, ref, to)

    up_0, down_1 = send(xl, 0, 0, up), send(xl, 0, 1, down)
    up_1, down_0 = send(xl, 0, 1, up), send(xl, 0, 0, down)
    side_0, side_1 = send(xl, 0, 0, beside), send(xl, 0, 1, beside)
    yield
    up_0.wait_recv()
    on_0 = send(xl, -1, 0, up)
    yield
    down_1.wait_recv()
    on_1 = send(xl, 1, 1, down)
    yield
    side_0.wait_recv()
    rest = [send(1 - xl, 0, 0, up), send(1 - xl, 0, 0, down)]
    yield
    side_1.wait_recv()
    rest += [send(1 - xl, 0, 1, up), send(1 - xl, 0, 1, down)]
    yield
    on_0.wait_recv()
    rest.append(send(xl, 2, 0, beside))
    yield
    on_1.wait_recv()
    rest.append(send(xl, 2, 1, beside))
    yield
    for sent in [up_1, down_0] + rest:
        sent.wait_recv()


def reduce_8(net, make, part, sums, got, sums_half, got_half, out):
    up, down, beside = net.device(dz=1), net.device(dz=-1), net.beside
    xl, z = net.xl, net.z
    halves = [pl.ds(0, 64), pl.ds(64, 64)]
    make(1 - xl, z + 2)
    a = [net.send(part.at[half8(1 - xl, z + 2, k), :], got.at[0, halves[k], :], beside) for k in (0, 1)]
    yield
    make(1 - xl, z + 1)
    b0 = net.send(part.at[block8(1 - xl, z + 1), :], got.at[1], up)
    yield
    make(1 - xl, z - 1)
    b1 = net.send(part.at[block8(1 - xl, z - 1), :], got.at[2], down)
    yield
    for step in (2, 1, -1):
        make(xl, z + step)
        yield
    a[0].wait_recv()
    add_rows(64, sums.at[0, halves[0], :], part.at[half8(xl, z + 2, 0), :], got.at[0, halves[0], :])
    c0 = net.send(sums.at[0, halves[0], :], got_half.at[0], up)
    yield
    a[1].wait_recv()
    add_rows(64, sums.at[0, halves[1], :], part.at[half8(xl, z + 2, 1), :], got.at[0, halves[1], :])
    c1 = net.send(sums.at[0, halves[1], :], got_half.at[1], down)
    d1 = net.send(part.at[half8(xl, z + 1, 1), :], got_half.at[3], up)
    d2 = net.send(part.at[half8(xl, z - 1, 0), :], got_half.at[4], down)
    yield
    make(1 - xl, z)
    yield
    make(xl, z)
    yield
    b0.wait_recv()
    b1.wait_recv()
    add_rows(128, sums.at[1], part.at[block8(1 - xl, z), :], got.at[1], got.at[2])
    e = net.send(sums.at[1], got.at[3], beside)
    yield
    c0.wait_recv()
    add_rows(64, sums_half.at[0], part.at[half8(xl, z + 1, 0), :], got_half.at[0])
    d0 = net.send(sums_half.at[0], got_half.at[2], up)
    yield
    c1.wait_recv()
    add_rows(64, sums_half.at[1], part.at[half8(xl, z - 1, 1), :], got_half.at[1])
    d3 = net.send(sums_half.at[1], got_half.at[5], down)
    yield
    for sent in (e, d0, d1, d2, d3):
        sent.wait_recv()

    def rows(at, k):
        here = pl.ds(pl.multiple_of(at - 64 * k, 16), 16)
        total = part[pl.ds(pl.multiple_of(net.t * ROWS + at, 16), 16), :].astype(jnp.float32)
        total = total + got[3, pl.ds(pl.multiple_of(at, 16), 16), :].astype(jnp.float32)
        return total + got_half[2 + k, here, :].astype(jnp.float32) + got_half[4 + k, here, :].astype(jnp.float32)

    out.append(rows)


def on_half(step, k):
    def body(i, _):
        step(pl.multiple_of(k * 64 + i * 16, 16), k)
        return 0

    lax.fori_loop(0, 4, body, 0)


def each_half(step):
    for k in (0, 1):
        on_half(step, k)


def gather_plane(net, slab, cut, first, second):
    low, high = cut
    sib = net.device(dc=1)
    second_up, second_down = second
    shared, halves, sent = [], {}, {}

    def share(i, j):
        ref = slab(i, j)
        shared.append(net.send(ref, ref, sib))

    def go(i):
        ref = slab(i, 0)
        sent[i] = (net.send(ref, ref, second_up), net.send(ref, ref, second_down))

    def on(i):
        sent[i][0].wait_recv()
        ref = low(slab(i, -1))
        up = net.send(ref, ref, second_up)
        share(i, -1)
        yield
        sent[i][1].wait_recv()
        ref = high(slab(i, 1))
        halves[i] = (up, net.send(ref, ref, second_down))
        share(i, 1)
        yield

    own = slab(0, 0)
    ring = len(first) == 2
    around = [net.send(own, own, to) for to in first]
    go(0)
    share(0, 0)
    yield
    if ring:
        around[0].wait_recv()
        ref = low(slab(-1, 0))
        f0 = net.send(ref, ref, first[0])
        go(-1)
        share(-1, 0)
        yield
        around[1].wait_recv()
        ref = high(slab(1, 0))
        f1 = net.send(ref, ref, first[1])
        go(1)
        share(1, 0)
        yield
        yield from on(0)
        f0.wait_recv()
        f1.wait_recv()
        go(2)
        share(2, 0)
        yield
        for i in (-1, 1, 2):
            yield from on(i)
    else:
        around[0].wait_recv()
        go(1)
        share(1, 0)
        yield
        for i in (0, 1):
            yield from on(i)
    for i in sent:
        halves[i][0].wait_recv()
        halves[i][1].wait_recv()
        share(i, 2)
        yield
    for copied in shared:
        copied.wait_recv()


def reduce_plane(net, mine, other, from_sib, got_half, got_up, got_down, last_bufs, cut, add, first, second):
    low, high = cut
    sib = net.device(dc=1)
    up, down = second
    ring = len(first) == 2
    steps = (2, 3, 1, 0) if ring else (1, 0)
    shared = {}
    for j in (2, 1, 3, 0):
        for i in steps:
            shared[i, j] = net.send(other(i, j), from_sib(i, j), sib)
    yield
    halves, full, last = {}, {}, {}
    for i in steps:
        shared[i, 2].wait_recv()
        add(None, mine(i, 2), from_sib(i, 2))
        halves[i] = (
            net.send(low(mine(i, 2)), low(got_half(i)), up),
            net.send(high(mine(i, 2)), high(got_half(i)), down),
        )
        yield
    for i in steps:
        shared[i, 1].wait_recv()
        halves[i][0].wait_recv()
        add(0, mine(i, 1), from_sib(i, 1), got_half(i))
        add(1, mine(i, 1), from_sib(i, 1))
        u = net.send(mine(i, 1), got_up(i), up)
        yield
        shared[i, 3].wait_recv()
        halves[i][1].wait_recv()
        add(0, mine(i, 3), from_sib(i, 3))
        add(1, mine(i, 3), from_sib(i, 3), got_half(i))
        full[i] = (u, net.send(mine(i, 3), got_down(i), down))
        yield
    for i in steps:
        shared[i, 0].wait_recv()
        full[i][0].wait_recv()
        full[i][1].wait_recv()
        add(None, mine(i, 0), from_sib(i, 0), got_up(i), got_down(i))
        if ring and i == 2:
            ref, to = mine(2, 0), last_bufs(2)
            last[2] = (net.send(low(ref), low(to), first[0]), net.send(high(ref), high(to), first[1]))
        if ring and i == 3:
            last[2][1].wait_recv()
            add(1, mine(3, 0), last_bufs(2))
            last[3] = net.send(mine(3, 0), last_bufs(1), first[1])
        if ring and i == 1:
            last[2][0].wait_recv()
            add(0, mine(1, 0), last_bufs(2))
        if i == 1:
            last[1] = net.send(mine(1, 0), last_bufs(0), first[0])
        yield
    last[1].wait_recv()
    if ring:
        last[3].wait_recv()
        add(None, mine(0, 0), last_bufs(0), last_bufs(1))
    else:
        add(None, mine(0, 0), last_bufs(0))


ATT_CUT = (lambda ref: ref.at[:, pl.ds(0, 64), :], lambda ref: ref.at[:, pl.ds(64, 64), :])


def add_in(cut, total):
    def add(part, dst, *terms):
        begin, n = {None: (0, total), 0: (0, cut), 1: (cut, total - cut)}[part]

        def piece(at, size):
            here = pl.ds(at, size)
            value = dst[here, :].astype(jnp.float32)
            for term in terms:
                value = value + term[here, :].astype(jnp.float32)
            dst[here, :] = value.astype(dst.dtype)

        def step(i, _):
            piece(pl.multiple_of(begin + i * 160, 16), 160)
            return 0

        lax.fori_loop(0, n // 160, step, 0)
        if n % 160:
            piece(begin + n // 160 * 160, n % 160)

    return add


def cut_at(cut, total):
    return (lambda ref: ref.at[pl.ds(0, cut), :], lambda ref: ref.at[pl.ds(cut, total - cut), :])


OD, OD_CUT = 944, 480
GU, GU_CUT = 1376, 688
QKV, QKV_CUT = 768, 384
OUT, FF_CUT = 256, 352


def plane_slab(net, ref, kind, i, j):
    x = lax.rem(net.x + jnp.where(kind == 0, i, j) + 4, 4)
    y = lax.rem(net.y + jnp.where(kind == 0, j, i) + 4, 4)
    at = pl.ds(pl.multiple_of((y * 4 + lax.div(x, 2) * 2 + kind) * 128, 128), 128)
    return ref.at[lax.rem(x, 2), :, at]


def att_at(net, kind, i, j):
    x, y = lax.rem(net.x + 2 * i + 4, 4), lax.rem(net.y + j + 4, 4)
    return pl.ds(pl.multiple_of((y * 4 + lax.div(x, 2) * 2 + kind) * 128, 128), 128)


def forward(chain):
    next(chain, None)


def run(chains, order):
    for name in "".join(order):
        next(chains[name], None)
    for chain in chains.values():
        for _ in chain:
            pass


def start(copies):
    for copy in copies:
        copy.start()
    return copies


def sequence_starts(lengths, at, rows):
    index = lax.broadcasted_iota(jnp.int32, (rows, 1), 0) + at
    limit, first = lengths[0, 0], jnp.zeros((rows, 1), jnp.int32)
    for s in range(8):
        first = jnp.where(index >= limit, limit, first)
        if s < 7:
            limit = limit + lengths[0, s + 1]
    return index, first


def params(collective, mib=58):
    return pltpu.CompilerParams(collective_id=collective, has_side_effects=True, vmem_limit_bytes=mib << 20)


def sems(n, local):
    return [pltpu.SemaphoreType.DMA((n,)), pltpu.SemaphoreType.DMA((n,)), pltpu.SemaphoreType.DMA((local,))]


FRONT_ORDER = (
    "otwttoottttooowcwbwwwbbwboowootdwttottttococcddo",
    "oootcddddtttuttuuuucdtttdddduduuuuttddddhuuuhuuu",
    "tttuttttttgggzggztgzzggggtigiiiizzzzimiggiiiigmm",
    "mzziiimzmgzgiiigmzzmiqgq",
)
BACK_ORDER = (
    "emeetetetettttettttteeeeewwtwteewttwtwwttsmmwwsw",
    "wsweetsemwwse",
)


TILES = ((0, 256), (256, 256), (512, 176))


def front_kernel(tok, cot, lengths, gain, mlp_gain, rates, wq, wk, wv, wo, wg, wu, wd,
                 n1_out, w_out, q_out, k_out, v_out, p_out, table_out, h1_out, dh1_out, do_out, m_out, od_grad, gain_part, gu_grad,
                 wo_turned, n1, w, q, k, v, p, table, h1, dh1, o, branches, branches_turned, w1, w2, g, n2, dgate, turned, da, do, sums, got,
                 sib, got_half, got_up, got_down, last, send_sems, recv_sems, local):
    net = Net(send_sems, recv_sems)
    bf, f32 = jnp.bfloat16, jnp.float32
    net.greet([net.device(dx=s) for s in (1, 2, 3)] + [net.device(dy=1), net.device(dy=-1), net.device(dz=1), net.device(dz=-1), net.device(dc=1)])
    hid, dup = 0, 1024
    own_rows = att_at(net, net.c, 0, 0)
    own_od, own_gu = plane_slab(net, w1, net.c, 0, 0), plane_slab(net, w2, net.c, 0, 0)
    wo_turned[...] = wo[...].T
    own = start(
        [
            pltpu.make_async_copy(src, dst, local.at[n])
            for n, (src, dst) in enumerate(
                (
                    (wq, w.at[0, own_rows, :]), (wk, w.at[1, own_rows, :]), (wv, w.at[2, own_rows, :]),
                    (wo_turned, own_od.at[pl.ds(0, 256), :]), (wd, own_od.at[pl.ds(256, FFB), :]),
                    (wg, own_gu.at[pl.ds(0, FFB), :]), (wu, own_gu.at[pl.ds(FFB, FFB), :]), (cot, g.at[block(net.z), :]),
                )
            )
        ]
    )

    def norm(at, _):
        here = pl.ds(at, 16)
        value = tok[here, :].astype(f32)
        r = lax.rsqrt(jnp.mean(value * value, axis=-1, keepdims=True) + EPS)
        n1[pl.ds(pl.multiple_of(net.t * ROWS + at, 16), 16), :] = (value * r * gain[...]).astype(bf)

    each_half(norm)
    net.met()
    part, m_part = n1.at[pl.ds(0, 512), :], n1.at[pl.ds(512, 512), :]
    saves = {}

    def save(n, src, dst):
        saves[n] = pltpu.make_async_copy(src, dst, local.at[n])
        saves[n].start()

    def project(i, _):
        here = pl.ds(pl.multiple_of(i * QROWS, QROWS), QROWS)
        left = n1[here, :]
        cos, sin = table[0, here, :], table[1, here, :]
        for m, dst in ((0, q), (1, k)):
            u = jnp.dot(left, w[m], preferred_element_type=f32)
            for h in range(2):
                uh = u[:, h * 128 : h * 128 + 128]
                dst[h, here, :] = (uh * cos + pltpu.roll(uh, 64, 1) * sin).astype(bf)
        u = jnp.dot(left, w[2], preferred_element_type=f32).astype(bf)
        for h in range(2):
            v[h, here, :] = u[:, h * 128 : h * 128 + 128]
        return 0

    def attend(b, heads=(0, 1)):
        rows = slice(b * QROWS, b * QROWS + QROWS)
        first, until = max(0, b - 2) * QROWS, (b + 1) * QROWS
        index, begin = sequence_starts(lengths, b * QROWS, QROWS)
        key = lax.broadcasted_iota(jnp.int32, (QROWS, until - first), 1) + first
        allowed = (key <= index) & (key >= begin)
        for h in heads:
            s = lax.dot_general(q[h, rows, :], k[h, first:until, :], NT, preferred_element_type=f32)
            s = jnp.where(allowed, s * HEAD_DIM ** (-0.5), -1e30)
            e = jnp.exp(s - jnp.max(s, axis=-1, keepdims=True))
            weights = (e / jnp.sum(e, axis=-1, keepdims=True)).astype(bf)
            p[(h * 4 + b) * QROWS : (h * 4 + b + 1) * QROWS, 0 : until - first] = weights
            o[rows, h * 128 : h * 128 + 128] = jnp.dot(weights, v[h, first:until, :], preferred_element_type=f32).astype(bf)

    def exchange(n, at, size):
        src = o.at[pl.ds(pl.multiple_of((1 - net.xl) * 512 + n * QROWS, QROWS), QROWS), pl.ds(at, size)]
        return net.send(src, branches.at[net.xl, pl.ds(n * QROWS, QROWS), pl.ds(at, size)], net.beside)

    def branch(z):
        here = block(z)
        u = jnp.dot(branches[0, here, :], w1[0, :256, :], preferred_element_type=f32)
        u = u + jnp.dot(branches[1, here, :], w1[1, :256, :], preferred_element_type=f32)
        part[here, :] = u.astype(bf)

    def second_norm(at, half_at):
        here = pl.ds(at, 16)
        h = tok[here, :].astype(f32) + reduced(net, part, got, at, half_at)
        h1[here, :] = h
        r = lax.rsqrt(jnp.mean(h * h, axis=-1, keepdims=True) + EPS)
        n2[pl.ds(pl.multiple_of(net.z * ROWS + at, 16), 16), :] = (h * r * mlp_gain[...]).astype(bf)

    def ahead(b):
        for at, n in TILES:
            gate = lax.dot_general(n2[...], w2[b, at : at + n, :], NT, preferred_element_type=f32)
            up = lax.dot_general(n2[...], w2[b, FFB + at : FFB + at + n, :], NT, preferred_element_type=f32)
            dh = dgate[b, :, at : at + n].astype(f32)
            sig = jax.nn.sigmoid(gate)
            act = gate * sig
            dg, du, hi = (dh * up * sig * (1.0 + gate * (1.0 - sig))).astype(bf), (dh * act).astype(bf), (act * up).astype(bf)
            dgate[b, :, at : at + n] = dg
            p[dup + b * 512 : dup + b * 512 + 512, at : at + n] = du
            p[hid + b * 512 : hid + b * 512 + 512, at : at + n] = hi
            for m, value in enumerate((dg, du, hi)):
                turned[m, b, at : at + n, :] = value.T

    def back(i, _):
        at = pl.ds(pl.multiple_of(i * 256, 256), 256)
        d = jnp.dot(dgate[0], w2[0, :FFB, at], preferred_element_type=f32)
        d = d + jnp.dot(dgate[1], w2[1, :FFB, at], preferred_element_type=f32)
        d = d + jnp.dot(p[dup : dup + 512, :FFB], w2[0, FFB:, at], preferred_element_type=f32)
        d = d + jnp.dot(p[dup + 512 : dup + 1024, :FFB], w2[1, FFB:, at], preferred_element_type=f32)
        part[:, at] = d.astype(bf)
        return 0

    def outer(m, i):
        at = pl.ds(i * 512, 512)
        for b in range(2):
            w2[b, m * FFB : m * FFB + FFB, at] = jnp.dot(turned[m, b], n2[:, at], preferred_element_type=f32).astype(bf)

    lanes = {name: net.lane() for name in "twoducaxyzg"}
    back_a = reduce_z(lanes["x"], part, sums, got, pl.ds(0, D // 2))
    back_b = reduce_z(lanes["y"], part, sums, got, pl.ds(D // 2, D // 2))

    def main():
        yield from gather_8(lanes["t"], n1)
        yield
        save(8, n1, n1_out)
        save(9, w, w_out)
        save(10, table, table_out)
        lax.fori_loop(0, 2, project, 0)
        yield
        lax.fori_loop(2, 4, project, 0)
        for n, (src, dst) in enumerate(((q, q_out), (k, k_out), (v, v_out))):
            save(11 + n, src, dst)
        yield
        attend(0)
        yield
        attend(2)
        swapped = [exchange(0, 0, 256)]
        for h in (0, 1):
            yield
            attend(1, (h,))
            attend(3, (h,))
            swapped.append(exchange(1, h * 128, 128))
        kept = pltpu.make_async_copy(o.at[pl.ds(pl.multiple_of(net.xl * 512, 512), 512), :], branches.at[net.xl], local.at[15])
        kept.start()
        save(14, p, p_out)
        yield
        for sent in swapped:
            sent.wait_recv()
        kept.wait()
        saves.pop(8).wait()
        lanes["t"].flush()
        yield from reduce_z(lanes["a"], part, sums, got, make=branch)
        yield
        yield from gather_z(lanes["z"], lambda k: n2.at[half(net.z, k), :], n2, functools.partial(on_half, second_norm))
        save(23, h1, h1_out)
        lanes["a"].flush()
        saves.pop(14).wait()
        yield
        ahead(0)
        yield
        ahead(1)
        yield
        lax.fori_loop(0, 4, back, 0)
        forward(back_a)
        yield
        lax.fori_loop(4, 8, back, 0)
        forward(back_b)
        lanes["u"].flush()
        for i in range(4):
            yield
            outer(i // 2, i % 2 * 2)
            outer(i // 2, i % 2 * 2 + 1)

    def norm_back(at, half_at):
        here = pl.ds(at, 16)
        h = h1[here, :]
        r = lax.rsqrt(jnp.mean(h * h, axis=-1, keepdims=True) + EPS)
        d = reduced(net, part, got, at, half_at)
        inner = d * mlp_gain[...]
        grad = r * inner - h * (r * r * r) * jnp.mean(h * inner, axis=-1, keepdims=True)
        grad = cot[here, :].astype(f32) + grad
        dh1[here, :] = grad
        da[pl.ds(pl.multiple_of(net.z * ROWS + at, 16), 16), :] = grad.astype(bf)
        gain_part[...] += jnp.sum(d * h * r, axis=0, keepdims=True)

    swapped_back = []

    def back_out(z):
        here = block(z)
        for b in range(2):
            do[b, here, :] = lax.dot_general(da[here, :], w1[b, :256, :], NT, preferred_element_type=f32).astype(bf)
        rows = pl.ds(pl.multiple_of(net.xl * 512 + lax.rem(z + 8, 4) * ROWS, ROWS), ROWS)
        swapped_back.append(net.send(do.at[1 - net.xl, here, :], do_out.at[rows, :], net.beside))
        save(15 + len(swapped_back), do.at[net.xl, here, :], do_out.at[rows, :])

    def tail():
        for chain in (back_a, back_a, back_b, back_b, back_a):
            forward(chain)
            yield
        forward(back_b)
        gain_part[...] = jnp.zeros_like(gain_part)
        yield
        yield from gather_z(lanes["z"], lambda k: da.at[half(net.z, k), :], da, functools.partial(on_half, norm_back), back_out)
        save(24, dh1, dh1_out)

    def weights():
        for copied in own[:3]:
            copied.wait()
        yield from gather_plane(lanes["w"], lambda i, j: w.at[:, att_at(net, net.c, i, j), :], ATT_CUT, (net.across,), (net.device(dy=1), net.device(dy=-1)))

    def plane(lane, held, ref, at, cut, rows):
        for copied in held:
            copied.wait()
        yield from gather_plane(
            lane, lambda i, j: plane_slab(net, ref, net.c, i, j).at[pl.ds(at, rows), :], cut_at(cut, rows), net.along(True), net.along(False)
        )

    def cotangent():
        own[7].wait()
        yield from gather_z(lanes["c"], lambda k: cot.at[pl.ds(k * 64, 64), :], g)

    def hidden_grad():
        for b in range(2):
            if b:
                yield
            for at, n in TILES:
                u = lax.dot_general(g[...], w1[b, 256 + at : 256 + at + n, :], NT, preferred_element_type=f32)
                dgate[b, :, at : at + n] = u.astype(bf)

    def tables():
        def rows(i, _):
            at = pl.multiple_of(i * 128, 128)
            index, first = sequence_starts(lengths, at, 128)
            angle = (index - first).astype(f32) * rates[...]
            lane = lax.broadcasted_iota(jnp.int32, (128, 128), 1)
            table[0, pl.ds(at, 128), :] = jnp.cos(angle)
            sin = jnp.sin(angle)
            table[1, pl.ds(at, 128), :] = jnp.where(lane < 64, -sin, sin)
            return 0

        for i in range(4):
            if i:
                yield
            lax.fori_loop(2 * i, 2 * i + 2, rows, 0)

    def mixed_part():
        def columns(i, _):
            at = pl.ds(pl.multiple_of(i * 256, 256), 256)
            u = jnp.dot(p[hid : hid + 512, :FFB], w1[0, 256:, at], preferred_element_type=f32)
            u = u + jnp.dot(p[hid + 512 : hid + 1024, :FFB], w1[1, 256:, at], preferred_element_type=f32)
            m_part[:, at] = u.astype(bf)
            return 0

        for i in range(4):
            lax.fori_loop(2 * i, 2 * i + 2, columns, 0)
            yield
        save(20, m_part, m_out)
        for b in range(2):
            branches_turned[b] = branches[b].T
        lanes["d"].flush()
        for i in range(4):
            if i:
                yield
            at = pl.ds(i * 512, 512)
            for b in range(2):
                w1[b, 256:, at] = jnp.dot(turned[2, b], g[:, at], preferred_element_type=f32).astype(bf)
        save(21, w1.at[:, pl.ds(256, FFB), :], od_grad.at[:, pl.ds(256, FFB), :])

    def outer_out():
        lanes["o"].flush()

        def columns(i, _):
            at = pl.ds(pl.multiple_of(i * 512, 512), 512)
            for b in range(2):
                w1[b, :256, at] = jnp.dot(branches_turned[b], da[:, at], preferred_element_type=f32).astype(bf)
            return 0

        lax.fori_loop(0, 4, columns, 0)
        save(22, w1.at[:, pl.ds(0, 256), :], od_grad.at[:, pl.ds(0, 256), :])
        yield
        for sent in swapped_back:
            sent.wait_recv()

    def grads(m):
        def slab(kind):
            return lambda i, j: plane_slab(net, w2, kind, i, j).at[pl.ds(m * FFB, FFB), :]

        yield from reduce_plane(
            lanes["g"], slab(net.c), slab(1 - net.c),
            lambda i, j: sib.at[m, i, j], lambda i: got_half.at[m, i], lambda i: got_up.at[m, i], lambda i: got_down.at[m, i], lambda i: last.at[m, i],
            cut_at(FF_CUT, FFB), add_in(FF_CUT, FFB), net.along(True), net.along(False),
        )

    run(
        {
            "t": main(), "z": tail(), "w": weights(), "o": plane(lanes["o"], own[3:4], w1, 0, OUT // 2, OUT),
            "d": plane(lanes["d"], own[4:5], w1, OUT, FF_CUT, FFB), "u": plane(lanes["u"], own[5:7], w2, 0, GU_CUT, GU),
            "c": cotangent(), "h": hidden_grad(), "b": tables(), "m": mixed_part(), "q": outer_out(), "g": grads(0), "i": grads(1),
        },
        FRONT_ORDER,
    )
    gu_grad[...] = plane_slab(net, w2, net.c, 0, 0)[...]
    for saved in saves.values():
        saved.wait()
    net.finish()


def front(*args):
    bf, f32 = jnp.bfloat16, jnp.float32
    slab = (GU, 128)
    kept = (
        ((GROUP, D), bf), ((3, D, 256), bf), ((2, GROUP, 128), bf), ((2, GROUP, 128), bf), ((2, GROUP, 128), bf),
        ((2 * GROUP, 768), bf), ((2, GROUP, 128), f32),
    )
    kept += (((ROWS, D), f32), ((ROWS, D), f32))
    outs = kept + (((GROUP, 256), bf), ((512, D), bf), ((2, OD, D), bf), ((1, D), f32), (slab, bf))
    scratch = (((256, 128), bf),) + kept + (
        ((GROUP, 256), bf), ((2, 512, 256), bf), ((2, 256, 512), bf), ((2, OD, D), bf), ((2, GU, D), bf), ((512, D), bf), ((512, D), bf),
        ((2, 512, FFB), bf), ((3, 2, FFB, 512), bf), ((512, D), bf), ((2, 512, 256), bf), ((2, 64, D), bf), ((6, 64, D), bf),
        ((2, 4, 4, FFB, 128), bf), ((2, 4, FFB, 128), bf), ((2, 4, FFB, 128), bf), ((2, 4, FFB, 128), bf), ((2, 3, FFB, 128), bf),
    )
    return pl.pallas_call(
        front_kernel,
        name="front",
        out_shape=tuple(jax.ShapeDtypeStruct(*s) for s in outs),
        in_specs=[VMEM, VMEM, pl.BlockSpec(memory_space=pltpu.SMEM), VMEM, VMEM, VMEM, ANY, ANY, ANY, VMEM, ANY, ANY, ANY],
        out_specs=(ANY,) * 12 + (VMEM, VMEM),
        scratch_shapes=[pltpu.VMEM(*s) for s in scratch] + sems(272, 25),
        compiler_params=params(1, 64),
    )(*args)


def back_kernel(do_in, n1_in, w_in, q_in, k_in, v_in, p_in, table_in, m_in, od_in, tok_in, h1_in, dh1_in, gain, mlp_gain_part,
                    mixed, dx, gains, qkv_grad, od_grad,
                    tok, h1, dh1, do, n1, w, q, k, v, p, table, dqkv, dqkv_turned, dk, dv, part, sums, got, sums_half, got_half,
                    ga, sib, slab_half, slab_up, slab_down, slab_last, sum_z, sum_x, sum_y, sum_c,
                    m_part, sums_m, got_m, od, od_sib, od_half, od_up, od_down, od_last,
                    send_sems, recv_sems, local):
    net = Net(send_sems, recv_sems)
    bf, f32 = jnp.bfloat16, jnp.float32
    line_x = [net.device(dx=s) for s in (1, 2, 3)]
    line_y = [net.device(dy=s) for s in (1, 2, 3)]
    line_z = [net.device(dz=s) for s in (1, 2, 3)]
    net.greet(line_x + line_y + line_z + [net.device(dc=1)])
    loads = start(
        [
            pltpu.make_async_copy(src, dst, local.at[m])
            for m, (src, dst) in enumerate(
                (
                    (m_in, m_part), (do_in, do), (v_in, v), (p_in, p), (q_in, q), (k_in, k), (table_in, table), (w_in, w), (n1_in, n1),
                    (h1_in, h1), (tok_in, tok), (dh1_in, dh1),
                )
            )
        ]
    )
    slabs = start(
        [
            pltpu.make_async_copy(plane_slab(net, od_in, net.c, i, j), od.at[i, j], local.at[12 + n])
            for n, (i, j) in enumerate((i, j) for j in (2, 1, 3, 0) for i in (2, 3, 1, 0))
        ]
    )
    net.met()

    def attend_back(h, b):
        rows = slice(b * QROWS, b * QROWS + QROWS)
        first, until = max(0, b - 2) * QROWS, (b + 1) * QROWS
        keys, old = slice(first, until), slice(first, b * QROWS)
        weights_b = p[(h * 4 + b) * QROWS : (h * 4 + b + 1) * QROWS, 0 : until - first]
        do_b = do[rows, h * 128 : h * 128 + 128]
        dp = lax.dot_general(do_b, v[h, keys, :], NT, preferred_element_type=f32)
        wide = weights_b.astype(f32)
        centre = jnp.sum(wide * dp, axis=-1, keepdims=True)
        ds = (wide * (dp - centre)).astype(bf)
        dvb = lax.dot_general(weights_b, do_b, TN, preferred_element_type=f32)
        dkb = lax.dot_general(ds, q[h, rows, :], TN, preferred_element_type=f32)
        if b > 0:
            dv[h, old, :] += dvb[: b * QROWS - first]
            dk[h, old, :] += dkb[: b * QROWS - first]
        dv[h, rows, :] = dvb[b * QROWS - first :]
        dk[h, rows, :] = dkb[b * QROWS - first :]
        dqb = jnp.dot(ds, k[h, keys, :], preferred_element_type=f32) * HEAD_DIM ** (-0.5)
        dqb = dqb * table[0, rows, :] - pltpu.roll(dqb, 64, 1) * table[1, rows, :]
        dqkv[rows, h * 128 : h * 128 + 128] = dqb.astype(bf)

    def turn(i, _):
        here = pl.ds(pl.multiple_of(i * QROWS, QROWS), QROWS)
        for h in range(2):
            u = dk[h, here, :] * HEAD_DIM ** (-0.5)
            u = u * table[0, here, :] - pltpu.roll(u, 64, 1) * table[1, here, :]
            dqkv[here, 256 + h * 128 : 384 + h * 128] = u.astype(bf)
            dqkv[here, 512 + h * 128 : 640 + h * 128] = dv[h, here, :].astype(bf)
        dqkv_turned[:, here] = dqkv[here, :].T
        return 0

    def make(xl, z):
        here = block8(xl, z)
        left = dqkv[here, :]

        def columns(i, _):
            at = pl.ds(pl.multiple_of(i * 512, 512), 512)
            u = lax.dot_general(left[:, :256], w[0, at, :], NT, preferred_element_type=f32)
            u = u + lax.dot_general(left[:, 256:512], w[1, at, :], NT, preferred_element_type=f32)
            u = u + lax.dot_general(left[:, 512:], w[2, at, :], NT, preferred_element_type=f32)
            part[here, at] = u.astype(bf)
            sum_y[net.y, 0:1, at] += jnp.sum(u * n1[here, at].astype(f32), axis=0, keepdims=True)
            return 0

        lax.fori_loop(0, 4, columns, 0)

    out = []

    def step(at, k):
        here = pl.ds(at, 16)
        value = tok[here, :].astype(f32)
        r = lax.rsqrt(jnp.mean(value * value, axis=-1, keepdims=True) + EPS)
        inner = out[0](at, k) * gain[...]
        dx[here, :] = dh1[here, :] + r * inner - value * (r * r * r) * jnp.mean(value * inner, axis=-1, keepdims=True)

    def main():
        for copied in loads[1:7]:
            copied.wait()
        yield
        for b in range(GROUP // QROWS):
            for h in range(2):
                attend_back(h, b)
            yield
        lax.fori_loop(0, GROUP // QROWS, turn, 0)
        for copied in loads[7:9]:
            copied.wait()
        sum_y[net.y, 0:1, :] = jnp.zeros((1, D), f32)
        sum_y[net.y, 1:2, :] = mlp_gain_part[...]
        yield
        yield from reduce_8(net, make, part, sums, got, sums_half, got_half, out)
        for copied in loads[10:]:
            copied.wait()
        each_half(step)

    def early():
        chain = reduce_plane(
            net, lambda i, j: od.at[i, j], lambda i, j: plane_slab(net, od_in, 1 - net.c, i, j), lambda i, j: od_sib.at[i, j],
            lambda i: od_half.at[i], lambda i: od_up.at[i], lambda i: od_down.at[i], lambda i: od_last.at[i],
            cut_at(OD_CUT, OD), add_in(OD_CUT, OD), net.along(True), net.along(False),
        )
        forward(chain)
        yield
        for copied in slabs:
            copied.wait()
        yield from chain
        od_grad[...] = od[0, 0]

    def mixing():
        loads[0].wait()
        yield from reduce_z(net, m_part, sums_m, got_m)

        def mix(at, k):
            here = pl.ds(at, 16)
            mixed[here, :] = (h1[here, :] + reduced(net, m_part, got_m, at, k)).astype(bf)

        loads[9].wait()
        each_half(mix)

    def slab(kind):
        return lambda i, j: ga.at[:, att_at(net, kind, i, j)]

    def weights():
        def outer(i, _):
            at = pl.ds(pl.multiple_of(i * 256, 256), 256)
            ga[:, at] = jnp.dot(dqkv_turned[...], n1[:, at], preferred_element_type=f32).astype(bf)
            return 0

        for i in range(4):
            lax.fori_loop(2 * i, 2 * i + 2, outer, 0)
            yield
        yield from reduce_plane(
            net, slab(net.c), slab(1 - net.c), lambda i, j: sib.at[i, j], lambda i: slab_half.at[i], lambda i: slab_up.at[i],
            lambda i: slab_down.at[i], lambda i: slab_last.at[i], cut_at(QKV_CUT, QKV), add_in(QKV_CUT, QKV), (net.across,), (net.device(dy=1), net.device(dy=-1)),
        )
        qkv_grad[...] = slab(net.c)(0, 0)[...]

    def gain_sums():
        here = net.y
        stages = ((sum_y, line_y, sum_c, net.c), (sum_c, [net.device(dc=1)], sum_x, net.x), (sum_x, line_x, sum_z, net.z), (sum_z, line_z, None, None))
        for ref, line, then, place in stages:
            sent = [net.send(ref.at[here], ref.at[here], to) for to in line]
            yield
            for copied in sent:
                copied.wait_recv()
            total = ref[0]
            for n in range(1, len(line) + 1):
                total = total + ref[n]
            if then is None:
                gains[0:1, :] = total[0:1] / gain[...]
                gains[1:2, :] = total[1:2]
            else:
                then[place] = total
                here = place

    run({"t": main(), "m": mixing(), "e": early(), "w": weights(), "s": gain_sums()}, BACK_ORDER)
    net.finish()


def back(do, n1, w, q, k, v, p, table, m, od, tok, h1, dh1, gain, mlp_gain_part):
    bf, f32 = jnp.bfloat16, jnp.float32
    slab, slab_od = (QKV, 128), (OD, 128)
    scratch = [
        ((ROWS, D), bf), ((ROWS, D), f32), ((ROWS, D), f32),
        ((GROUP, 256), bf), ((GROUP, D), bf), ((3, D, 256), bf), ((2, GROUP, 128), bf), ((2, GROUP, 128), bf), ((2, GROUP, 128), bf),
        ((2 * GROUP, 768), bf), ((2, GROUP, 128), f32), ((GROUP, QKV), bf), ((QKV, GROUP), bf),
        ((2, GROUP, 128), f32), ((2, GROUP, 128), f32), ((GROUP, D), bf), ((2, ROWS, D), bf), ((4, ROWS, D), bf),
        ((2, 64, D), bf), ((6, 64, D), bf), ((QKV, D), bf), ((2, 4) + slab, bf), ((2,) + slab, bf), ((2,) + slab, bf),
        ((2,) + slab, bf), ((1,) + slab, bf), ((4, 2, D), f32), ((4, 2, D), f32), ((4, 2, D), f32), ((2, 2, D), f32),
        ((512, D), bf), ((2, 64, D), bf), ((6, 64, D), bf), ((4, 4) + slab_od, bf), ((4, 4) + slab_od, bf),
        ((4,) + slab_od, bf), ((4,) + slab_od, bf), ((4,) + slab_od, bf), ((3,) + slab_od, bf),
    ]
    outs = (((ROWS, D), bf), ((ROWS, D), f32), ((2, D), f32), (slab, bf), (slab_od, bf))
    return pl.pallas_call(
        back_kernel,
        name="back",
        out_shape=tuple(jax.ShapeDtypeStruct(*s) for s in outs),
        in_specs=[ANY] * 13 + [VMEM] * 2,
        out_specs=(VMEM,) * 5,
        scratch_shapes=[pltpu.VMEM(*s) for s in scratch] + sems(128, 28),
        compiler_params=params(2),
    )(do, n1, w, q, k, v, p, table, m, od, tok, h1, dh1, gain, mlp_gain_part)


def finish_kernel(mixed_in, dx_in, gains_in, qkv_in, od_in, gu_in, mixed, dx, ag, gq, gk, gv, go, mg, gg, gu_out, gd, gains, qkv, od, gu, sems):
    f32 = jnp.float32
    pairs = ((gu_in, gu), (od_in, od), (qkv_in, qkv), (gains_in, gains), (mixed_in, mixed), (dx_in, dx))
    loads = start([pltpu.make_async_copy(src, dst, sems.at[n]) for n, (src, dst) in enumerate(pairs)])
    for load in loads[:4]:
        load.wait()
    gg[...] = gu[:FFB, :].astype(f32)
    gu_out[...] = gu[FFB:, :].astype(f32)
    go[...] = od[:256, :].astype(f32).T
    gd[...] = od[256:, :].astype(f32)
    for n, dst in enumerate((gq, gk, gv)):
        dst[...] = qkv[n * 256 : n * 256 + 256, :].astype(f32).T
    ag[...] = gains[0:1, :]
    mg[...] = gains[1:2, :]
    for load in loads[4:]:
        load.wait()


def finish(mixed, dx, gains, qkv, od, gu):
    f32, bf = jnp.float32, jnp.bfloat16
    outs = (
        ((ROWS, D), bf), ((ROWS, D), f32), ((1, D), f32), ((ROWS, 256), f32), ((ROWS, 256), f32), ((ROWS, 256), f32),
        ((ROWS, 256), f32), ((1, D), f32), ((FFB, 128), f32), ((FFB, 128), f32), ((FFB, 128), f32),
    )
    held = (((2, D), f32), ((QKV, 128), bf), ((OD, 128), bf), ((GU, 128), bf))
    return pl.pallas_call(
        finish_kernel,
        name="finish",
        out_shape=tuple(jax.ShapeDtypeStruct(*s) for s in outs),
        in_specs=[ANY] * 6,
        out_specs=(VMEM,) * 11,
        scratch_shapes=[pltpu.VMEM(*s) for s in held] + [pltpu.SemaphoreType.DMA((6,))],
        compiler_params=pltpu.CompilerParams(vmem_limit_bytes=60 << 20),
    )(mixed, dx, gains, qkv, od, gu)


def shards(
    tokens,
    lengths,
    attn_gain,
    query_weight,
    key_weight,
    value_weight,
    out_weight,
    mlp_gain,
    gate_weight,
    up_weight,
    down_weight,
    cotangent,
):
    half_rates = THETA ** (-(np.arange(64, dtype=np.float32) * np.float32(2.0 / HEAD_DIM)))
    rates = jnp.asarray(np.concatenate([half_rates, half_rates])[None].astype(np.float32))
    n1, w, q, k, v, p, table, h1, dh1, do, m, od_part, gain_part, gu = front(
        tokens, cotangent, lengths, attn_gain[None], mlp_gain[None], rates, query_weight, key_weight, value_weight, out_weight,
        gate_weight.T, up_weight.T, down_weight.T,
    )
    mixed, dx, gains, qkv, od_grad = back(do, n1, w, q, k, v, p, table, m, od_part, tokens, h1, dh1, attn_gain[None], gain_part)
    mixed, dx, ag, gq, gk, gv, go, mg, gg, gu, gd = finish(mixed, dx, gains, qkv, od_grad, gu)
    return (mixed, dx, ag[0], gq, gk, gv, go, mg[0], gg.T, gu.T, gd.T)


def solution(mesh):
    return jax.shard_map(
        shards,
        mesh=mesh,
        in_specs=(
            P(("dp", "tensor"), None),
            P("dp", None),
            P(),
            P("dp", "tensor"),
            P("dp", "tensor"),
            P("dp", "tensor"),
            P("dp", "tensor"),
            P(),
            P("dp", "tensor"),
            P("dp", "tensor"),
            P("dp", "tensor"),
            P(("dp", "tensor"), None),
        ),
        out_specs=(
            P(("dp", "tensor"), None),
            P(("dp", "tensor"), None),
            P(),
            P("dp", "tensor"),
            P("dp", "tensor"),
            P("dp", "tensor"),
            P("dp", "tensor"),
            P(),
            P("dp", "tensor"),
            P("dp", "tensor"),
            P("dp", "tensor"),
        ),
        check_vma=False,
    )
```

```python
import copy
import functools

import jax
import jax.numpy as jnp
import numpy as np
from jax import lax
from jax.experimental import pallas as pl
from jax.experimental.pallas import tpu as pltpu
from jax.sharding import PartitionSpec as P

HEAD_DIM = 128
EPS = 1e-05
THETA = 10000.0
D = 2048
ROWS = 128
GROUP = 1024
FFB = 688
QROWS = 256
MESH = pl.DeviceIdType.MESH
ANY = pl.BlockSpec(memory_space=pl.ANY)
VMEM = pl.BlockSpec(memory_space=pltpu.VMEM)
NT = (((1,), (1,)), ((), ()))
TN = (((0,), (0,)), ((), ()))


class Net:
    def __init__(self, send_sems, recv_sems):
        dp, t = lax.axis_index("dp"), lax.axis_index("tensor")
        self.y, self.c = lax.div(dp, 4), lax.rem(dp, 2)
        self.xl, self.z = lax.div(t, 4), lax.rem(t, 4)
        self.x = lax.rem(lax.div(dp, 2), 2) * 2 + self.xl
        self.dp, self.t = dp, t
        self.send_sems, self.recv_sems = send_sems, recv_sems
        self.used = [0]
        self.sent = []
        self.lanes = [self]

    def lane(self):
        other = copy.copy(self)
        other.sent = []
        self.lanes.append(other)
        return other

    def device(self, dx=0, dy=0, dz=0, dc=0):
        x, y = lax.rem(self.x + dx + 4, 4), lax.rem(self.y + dy + 4, 4)
        z, c = lax.rem(self.z + dz + 4, 4), lax.rem(self.c + dc, 2)
        return (y * 4 + lax.div(x, 2) * 2 + c, lax.rem(x, 2) * 4 + z)

    @property
    def beside(self):
        return (self.dp, (1 - self.xl) * 4 + self.z)

    @property
    def across(self):
        return self.device(dx=2)

    def along(self, first):
        on_x = self.c == (0 if first else 1)
        both = []
        for step in (1, -1):
            by_x, by_y = self.device(dx=step), self.device(dy=step)
            both.append(tuple(jnp.where(on_x, u, v) for u, v in zip(by_x, by_y)))
        return both

    def send(self, src, dst, to):
        k = self.used[0]
        self.used[0] += 1
        sent = pltpu.make_async_remote_copy(
            src_ref=src,
            dst_ref=dst,
            send_sem=self.send_sems.at[k],
            recv_sem=self.recv_sems.at[k],
            device_id=to,
            device_id_type=MESH,
        )
        sent.start()
        self.sent.append(sent)
        return sent

    def flush(self):
        for sent in self.sent:
            sent.wait_send()
        self.sent.clear()

    def finish(self):
        for lane in self.lanes:
            lane.flush()

    def greet(self, devices):
        for device in devices:
            pl.semaphore_signal(pltpu.get_barrier_semaphore(), inc=1, device_id=device, device_id_type=MESH)
        self.greeted = len(devices)

    def met(self):
        pl.semaphore_wait(pltpu.get_barrier_semaphore(), self.greeted)


def block(z):
    return pl.ds(pl.multiple_of(lax.rem(z + 8, 4) * ROWS, ROWS), ROWS)


def half(z, k):
    return pl.ds(pl.multiple_of(lax.rem(z + 8, 4) * ROWS + k * 64, 64), 64)


def block8(xl, z):
    return pl.ds(pl.multiple_of((xl * 4 + lax.rem(z + 8, 4)) * ROWS, ROWS), ROWS)


def half8(xl, z, k):
    return pl.ds(pl.multiple_of((xl * 4 + lax.rem(z + 8, 4)) * ROWS + k * 64, 64), 64)


def add_rows(rows, dst, *terms):
    def step(i, _):
        at = pl.ds(pl.multiple_of(i * 16, 16), 16)
        total = terms[0][at, :].astype(jnp.float32)
        for term in terms[1:]:
            total = total + term[at, :].astype(jnp.float32)
        dst[at, :] = total.astype(dst.dtype)
        return 0

    lax.fori_loop(0, rows // 16, step, 0)


def gather_z(net, own, dst, fill=None, arrived=None):
    up, down = net.device(dz=1), net.device(dz=-1)
    z = net.z
    place = [dst.at[half(z, k), :] for k in (0, 1)]
    if fill:
        fill(0)
    up_0 = net.send(own(0), place[0], up)
    if fill:
        yield
        fill(1)
    down_1 = net.send(own(1), place[1], down)
    up_1 = net.send(own(1), place[1], up)
    down_0 = net.send(own(0), place[0], down)
    yield
    if arrived:
        arrived(z)
        yield
    up_0.wait_recv()
    ref = dst.at[half(z - 1, 0), :]
    on_0 = net.send(ref, ref, up)
    yield
    down_1.wait_recv()
    ref = dst.at[half(z + 1, 1), :]
    on_1 = net.send(ref, ref, down)
    yield
    up_1.wait_recv()
    if arrived:
        arrived(z - 1)
    yield
    down_0.wait_recv()
    if arrived:
        arrived(z + 1)
    yield
    on_0.wait_recv()
    on_1.wait_recv()
    if arrived:
        arrived(z + 2)


def reduce_z(net, part, sums, got, cols=pl.ds(0, D), make=None):
    up, down = net.device(dz=1), net.device(dz=-1)
    z = net.z
    if make:
        make(z + 2)
    c0 = net.send(part.at[half(z + 2, 0), cols], got.at[0, :, cols], up)
    c1 = net.send(part.at[half(z + 2, 1), cols], got.at[1, :, cols], down)
    if make:
        yield
        make(z + 1)
    d1 = net.send(part.at[half(z + 1, 1), cols], got.at[3, :, cols], up)
    if make:
        yield
        make(z - 1)
    d2 = net.send(part.at[half(z - 1, 0), cols], got.at[4, :, cols], down)
    if make:
        yield
        make(z)
    yield
    c0.wait_recv()
    add_rows(64, sums.at[0, :, cols], part.at[half(z + 1, 0), cols], got.at[0, :, cols])
    d0 = net.send(sums.at[0, :, cols], got.at[2, :, cols], up)
    yield
    c1.wait_recv()
    add_rows(64, sums.at[1, :, cols], part.at[half(z - 1, 1), cols], got.at[1, :, cols])
    d3 = net.send(sums.at[1, :, cols], got.at[5, :, cols], down)
    yield
    for sent in (d0, d1, d2, d3):
        sent.wait_recv()


def reduced(net, part, got, at, k):
    here = pl.ds(pl.multiple_of(at - 64 * k, 16), 16)
    total = part[pl.ds(pl.multiple_of(net.z * ROWS + at, 16), 16), :].astype(jnp.float32)
    return total + got[2 + k, here, :].astype(jnp.float32) + got[4 + k, here, :].astype(jnp.float32)


def gather_8(net, dst):
    up, down, beside = net.device(dz=1), net.device(dz=-1), net.beside
    xl, z = net.xl, net.z

    def send(x, dz, k, to):
        ref = dst.at[half8(x, z + dz, k), :]
        return net.send(ref, ref, to)

    up_0, down_1 = send(xl, 0, 0, up), send(xl, 0, 1, down)
    up_1, down_0 = send(xl, 0, 1, up), send(xl, 0, 0, down)
    side_0, side_1 = send(xl, 0, 0, beside), send(xl, 0, 1, beside)
    yield
    up_0.wait_recv()
    on_0 = send(xl, -1, 0, up)
    yield
    down_1.wait_recv()
    on_1 = send(xl, 1, 1, down)
    yield
    side_0.wait_recv()
    rest = [send(1 - xl, 0, 0, up), send(1 - xl, 0, 0, down)]
    yield
    side_1.wait_recv()
    rest += [send(1 - xl, 0, 1, up), send(1 - xl, 0, 1, down)]
    yield
    on_0.wait_recv()
    rest.append(send(xl, 2, 0, beside))
    yield
    on_1.wait_recv()
    rest.append(send(xl, 2, 1, beside))
    yield
    for sent in [up_1, down_0] + rest:
        sent.wait_recv()


def reduce_8(net, make, part, sums, got, sums_half, got_half, out):
    up, down, beside = net.device(dz=1), net.device(dz=-1), net.beside
    xl, z = net.xl, net.z
    halves = [pl.ds(0, 64), pl.ds(64, 64)]
    make(1 - xl, z + 2)
    a = [net.send(part.at[half8(1 - xl, z + 2, k), :], got.at[0, halves[k], :], beside) for k in (0, 1)]
    yield
    make(1 - xl, z + 1)
    b0 = net.send(part.at[block8(1 - xl, z + 1), :], got.at[1], up)
    yield
    make(1 - xl, z - 1)
    b1 = net.send(part.at[block8(1 - xl, z - 1), :], got.at[2], down)
    yield
    for step in (2, 1, -1):
        make(xl, z + step)
        yield
    a[0].wait_recv()
    add_rows(64, sums.at[0, halves[0], :], part.at[half8(xl, z + 2, 0), :], got.at[0, halves[0], :])
    c0 = net.send(sums.at[0, halves[0], :], got_half.at[0], up)
    yield
    a[1].wait_recv()
    add_rows(64, sums.at[0, halves[1], :], part.at[half8(xl, z + 2, 1), :], got.at[0, halves[1], :])
    c1 = net.send(sums.at[0, halves[1], :], got_half.at[1], down)
    d1 = net.send(part.at[half8(xl, z + 1, 1), :], got_half.at[3], up)
    d2 = net.send(part.at[half8(xl, z - 1, 0), :], got_half.at[4], down)
    yield
    make(1 - xl, z)
    yield
    make(xl, z)
    yield
    b0.wait_recv()
    b1.wait_recv()
    add_rows(128, sums.at[1], part.at[block8(1 - xl, z), :], got.at[1], got.at[2])
    e = net.send(sums.at[1], got.at[3], beside)
    yield
    c0.wait_recv()
    add_rows(64, sums_half.at[0], part.at[half8(xl, z + 1, 0), :], got_half.at[0])
    d0 = net.send(sums_half.at[0], got_half.at[2], up)
    yield
    c1.wait_recv()
    add_rows(64, sums_half.at[1], part.at[half8(xl, z - 1, 1), :], got_half.at[1])
    d3 = net.send(sums_half.at[1], got_half.at[5], down)
    yield
    for sent in (e, d0, d1, d2, d3):
        sent.wait_recv()

    def rows(at, k):
        here = pl.ds(pl.multiple_of(at - 64 * k, 16), 16)
        total = part[pl.ds(pl.multiple_of(net.t * ROWS + at, 16), 16), :].astype(jnp.float32)
        total = total + got[3, pl.ds(pl.multiple_of(at, 16), 16), :].astype(jnp.float32)
        return total + got_half[2 + k, here, :].astype(jnp.float32) + got_half[4 + k, here, :].astype(jnp.float32)

    out.append(rows)


def on_half(step, k):
    def body(i, _):
        step(pl.multiple_of(k * 64 + i * 16, 16), k)
        return 0

    lax.fori_loop(0, 4, body, 0)


def each_half(step):
    for k in (0, 1):
        on_half(step, k)


def gather_plane(net, slab, cut, first, second):
    low, high = cut
    sib = net.device(dc=1)
    second_up, second_down = second
    shared, halves, sent = [], {}, {}

    def share(i, j):
        ref = slab(i, j)
        shared.append(net.send(ref, ref, sib))

    def go(i):
        ref = slab(i, 0)
        sent[i] = (net.send(ref, ref, second_up), net.send(ref, ref, second_down))

    def on(i):
        sent[i][0].wait_recv()
        ref = low(slab(i, -1))
        up = net.send(ref, ref, second_up)
        share(i, -1)
        yield
        sent[i][1].wait_recv()
        ref = high(slab(i, 1))
        halves[i] = (up, net.send(ref, ref, second_down))
        share(i, 1)
        yield

    own = slab(0, 0)
    ring = len(first) == 2
    around = [net.send(own, own, to) for to in first]
    go(0)
    share(0, 0)
    yield
    if ring:
        around[0].wait_recv()
        ref = low(slab(-1, 0))
        f0 = net.send(ref, ref, first[0])
        go(-1)
        share(-1, 0)
        yield
        around[1].wait_recv()
        ref = high(slab(1, 0))
        f1 = net.send(ref, ref, first[1])
        go(1)
        share(1, 0)
        yield
        yield from on(0)
        f0.wait_recv()
        f1.wait_recv()
        go(2)
        share(2, 0)
        yield
        for i in (-1, 1, 2):
            yield from on(i)
    else:
        around[0].wait_recv()
        go(1)
        share(1, 0)
        yield
        for i in (0, 1):
            yield from on(i)
    for i in sent:
        halves[i][0].wait_recv()
        halves[i][1].wait_recv()
        share(i, 2)
        yield
    for copied in shared:
        copied.wait_recv()


def reduce_plane(net, mine, other, from_sib, got_half, got_up, got_down, last_bufs, cut, add, first, second):
    low, high = cut
    sib = net.device(dc=1)
    up, down = second
    ring = len(first) == 2
    steps = (2, 3, 1, 0) if ring else (1, 0)
    shared = {}
    for j in (2, 1, 3, 0):
        for i in steps:
            shared[i, j] = net.send(other(i, j), from_sib(i, j), sib)
    yield
    halves, full, last = {}, {}, {}
    for i in steps:
        shared[i, 2].wait_recv()
        add(None, mine(i, 2), from_sib(i, 2))
        halves[i] = (
            net.send(low(mine(i, 2)), low(got_half(i)), up),
            net.send(high(mine(i, 2)), high(got_half(i)), down),
        )
        yield
    for i in steps:
        shared[i, 1].wait_recv()
        halves[i][0].wait_recv()
        add(0, mine(i, 1), from_sib(i, 1), got_half(i))
        add(1, mine(i, 1), from_sib(i, 1))
        u = net.send(mine(i, 1), got_up(i), up)
        yield
        shared[i, 3].wait_recv()
        halves[i][1].wait_recv()
        add(0, mine(i, 3), from_sib(i, 3))
        add(1, mine(i, 3), from_sib(i, 3), got_half(i))
        full[i] = (u, net.send(mine(i, 3), got_down(i), down))
        yield
    for i in steps:
        shared[i, 0].wait_recv()
        full[i][0].wait_recv()
        full[i][1].wait_recv()
        add(None, mine(i, 0), from_sib(i, 0), got_up(i), got_down(i))
        if ring and i == 2:
            ref, to = mine(2, 0), last_bufs(2)
            last[2] = (net.send(low(ref), low(to), first[0]), net.send(high(ref), high(to), first[1]))
        if ring and i == 3:
            last[2][1].wait_recv()
            add(1, mine(3, 0), last_bufs(2))
            last[3] = net.send(mine(3, 0), last_bufs(1), first[1])
        if ring and i == 1:
            last[2][0].wait_recv()
            add(0, mine(1, 0), last_bufs(2))
        if i == 1:
            last[1] = net.send(mine(1, 0), last_bufs(0), first[0])
        yield
    last[1].wait_recv()
    if ring:
        last[3].wait_recv()
        add(None, mine(0, 0), last_bufs(0), last_bufs(1))
    else:
        add(None, mine(0, 0), last_bufs(0))


ATT_CUT = (lambda ref: ref.at[:, pl.ds(0, 64), :], lambda ref: ref.at[:, pl.ds(64, 64), :])


def add_in(cut, total):
    def add(part, dst, *terms):
        begin, n = {None: (0, total), 0: (0, cut), 1: (cut, total - cut)}[part]

        def piece(at, size):
            here = pl.ds(at, size)
            value = dst[here, :].astype(jnp.float32)
            for term in terms:
                value = value + term[here, :].astype(jnp.float32)
            dst[here, :] = value.astype(dst.dtype)

        def step(i, _):
            piece(pl.multiple_of(begin + i * 160, 16), 160)
            return 0

        lax.fori_loop(0, n // 160, step, 0)
        if n % 160:
            piece(begin + n // 160 * 160, n % 160)

    return add


def cut_at(cut, total):
    return (lambda ref: ref.at[pl.ds(0, cut), :], lambda ref: ref.at[pl.ds(cut, total - cut), :])


OD, OD_CUT = 944, 480
GU, GU_CUT = 1376, 688
QKV, QKV_CUT = 768, 384
OUT, FF_CUT = 256, 352


def plane_slab(net, ref, kind, i, j):
    x = lax.rem(net.x + jnp.where(kind == 0, i, j) + 4, 4)
    y = lax.rem(net.y + jnp.where(kind == 0, j, i) + 4, 4)
    at = pl.ds(pl.multiple_of((y * 4 + lax.div(x, 2) * 2 + kind) * 128, 128), 128)
    return ref.at[lax.rem(x, 2), :, at]


def att_at(net, kind, i, j):
    x, y = lax.rem(net.x + 2 * i + 4, 4), lax.rem(net.y + j + 4, 4)
    return pl.ds(pl.multiple_of((y * 4 + lax.div(x, 2) * 2 + kind) * 128, 128), 128)


def forward(chain):
    next(chain, None)


def run(chains, order):
    for name in "".join(order):
        next(chains[name], None)
    for chain in chains.values():
        for _ in chain:
            pass


def start(copies):
    for copy in copies:
        copy.start()
    return copies


def sequence_starts(lengths, at, rows):
    index = lax.broadcasted_iota(jnp.int32, (rows, 1), 0) + at
    limit, first = lengths[0, 0], jnp.zeros((rows, 1), jnp.int32)
    for s in range(8):
        first = jnp.where(index >= limit, limit, first)
        if s < 7:
            limit = limit + lengths[0, s + 1]
    return index, first


def params(collective, mib=58):
    return pltpu.CompilerParams(collective_id=collective, has_side_effects=True, vmem_limit_bytes=mib << 20)


def sems(n, local):
    return [pltpu.SemaphoreType.DMA((n,)), pltpu.SemaphoreType.DMA((n,)), pltpu.SemaphoreType.DMA((local,))]


FRONT_ORDER = (
    "otwoobtobtbbttttwwwcwwwoooooowtdwtotttttccooodod",
    "ocotttdddddutttuudtttddddduuduuuuudccttdhuuuhuuu",
    "tttuttttttgzggzggtgzzggggtigiiiizzzziiimiiimiiim",
    "ggzzgzmmzziigmgmmzqggiiq",
)
BACK_ORDER = (
    "emeeeetteeettttttttttwwteeweeeettttwwswttwwwsemm",
    "seewwwstemwsw",
)


TILES = ((0, 256), (256, 256), (512, 176))


def front_kernel(tok, cot, lengths, gain, mlp_gain, rates, wq, wk, wv, wo, wg, wu, wd,
                 n1_out, w_out, q_out, k_out, v_out, p_out, table_out, h1_out, dh1_out, do_out, m_out, od_grad, gain_part, gu_grad,
                 wo_turned, n1, w, q, k, v, p, table, h1, dh1, o, branches, branches_turned, w1, w2, g, n2, dgate, turned, da, do, sums, got,
                 sib, got_half, got_up, got_down, last, send_sems, recv_sems, local):
    net = Net(send_sems, recv_sems)
    bf, f32 = jnp.bfloat16, jnp.float32
    net.greet([net.device(dx=s) for s in (1, 2, 3)] + [net.device(dy=1), net.device(dy=-1), net.device(dz=1), net.device(dz=-1), net.device(dc=1)])
    hid, dup = 0, 1024
    own_rows = att_at(net, net.c, 0, 0)
    own_od, own_gu = plane_slab(net, w1, net.c, 0, 0), plane_slab(net, w2, net.c, 0, 0)
    wo_turned[...] = wo[...].T
    own = start(
        [
            pltpu.make_async_copy(src, dst, local.at[n])
            for n, (src, dst) in enumerate(
                (
                    (wq, w.at[0, own_rows, :]), (wk, w.at[1, own_rows, :]), (wv, w.at[2, own_rows, :]),
                    (wo_turned, own_od.at[pl.ds(0, 256), :]), (wd, own_od.at[pl.ds(256, FFB), :]),
                    (wg, own_gu.at[pl.ds(0, FFB), :]), (wu, own_gu.at[pl.ds(FFB, FFB), :]), (cot, g.at[block(net.z), :]),
                )
            )
        ]
    )

    def norm(at, _):
        here = pl.ds(at, 16)
        value = tok[here, :].astype(f32)
        r = lax.rsqrt(jnp.mean(value * value, axis=-1, keepdims=True) + EPS)
        n1[pl.ds(pl.multiple_of(net.t * ROWS + at, 16), 16), :] = (value * r * gain[...]).astype(bf)

    each_half(norm)
    net.met()
    part, m_part = n1.at[pl.ds(0, 512), :], n1.at[pl.ds(512, 512), :]
    saves = {}

    def save(n, src, dst):
        saves[n] = pltpu.make_async_copy(src, dst, local.at[n])
        saves[n].start()

    def project(i, _):
        here = pl.ds(pl.multiple_of(i * QROWS, QROWS), QROWS)
        left = n1[here, :]
        cos, sin = table[0, here, :], table[1, here, :]
        for m, dst in ((0, q), (1, k)):
            u = jnp.dot(left, w[m], preferred_element_type=f32)
            for h in range(2):
                uh = u[:, h * 128 : h * 128 + 128]
                dst[h, here, :] = (uh * cos + pltpu.roll(uh, 64, 1) * sin).astype(bf)
        u = jnp.dot(left, w[2], preferred_element_type=f32).astype(bf)
        for h in range(2):
            v[h, here, :] = u[:, h * 128 : h * 128 + 128]
        return 0

    def attend(b, heads=(0, 1)):
        rows = slice(b * QROWS, b * QROWS + QROWS)
        first, until = max(0, b - 2) * QROWS, (b + 1) * QROWS
        index, begin = sequence_starts(lengths, b * QROWS, QROWS)
        key = lax.broadcasted_iota(jnp.int32, (QROWS, until - first), 1) + first
        allowed = (key <= index) & (key >= begin)
        for h in heads:
            s = lax.dot_general(q[h, rows, :], k[h, first:until, :], NT, preferred_element_type=f32)
            s = jnp.where(allowed, s * HEAD_DIM ** (-0.5), -1e30)
            e = jnp.exp(s - jnp.max(s, axis=-1, keepdims=True))
            weights = (e / jnp.sum(e, axis=-1, keepdims=True)).astype(bf)
            p[(h * 4 + b) * QROWS : (h * 4 + b + 1) * QROWS, 0 : until - first] = weights
            o[rows, h * 128 : h * 128 + 128] = jnp.dot(weights, v[h, first:until, :], preferred_element_type=f32).astype(bf)

    def exchange(n, at, size):
        src = o.at[pl.ds(pl.multiple_of((1 - net.xl) * 512 + n * QROWS, QROWS), QROWS), pl.ds(at, size)]
        return net.send(src, branches.at[net.xl, pl.ds(n * QROWS, QROWS), pl.ds(at, size)], net.beside)

    def branch(z):
        here = block(z)
        u = jnp.dot(branches[0, here, :], w1[0, :256, :], preferred_element_type=f32)
        u = u + jnp.dot(branches[1, here, :], w1[1, :256, :], preferred_element_type=f32)
        part[here, :] = u.astype(bf)

    def second_norm(at, half_at):
        here = pl.ds(at, 16)
        h = tok[here, :].astype(f32) + reduced(net, part, got, at, half_at)
        h1[here, :] = h
        r = lax.rsqrt(jnp.mean(h * h, axis=-1, keepdims=True) + EPS)
        n2[pl.ds(pl.multiple_of(net.z * ROWS + at, 16), 16), :] = (h * r * mlp_gain[...]).astype(bf)

    def ahead(b):
        for at, n in TILES:
            gate = lax.dot_general(n2[...], w2[b, at : at + n, :], NT, preferred_element_type=f32)
            up = lax.dot_general(n2[...], w2[b, FFB + at : FFB + at + n, :], NT, preferred_element_type=f32)
            dh = dgate[b, :, at : at + n].astype(f32)
            sig = jax.nn.sigmoid(gate)
            act = gate * sig
            dg, du, hi = (dh * up * sig * (1.0 + gate * (1.0 - sig))).astype(bf), (dh * act).astype(bf), (act * up).astype(bf)
            dgate[b, :, at : at + n] = dg
            p[dup + b * 512 : dup + b * 512 + 512, at : at + n] = du
            p[hid + b * 512 : hid + b * 512 + 512, at : at + n] = hi
            for m, value in enumerate((dg, du, hi)):
                turned[m, b, at : at + n, :] = value.T

    def back(i, _):
        at = pl.ds(pl.multiple_of(i * 256, 256), 256)
        d = jnp.dot(dgate[0], w2[0, :FFB, at], preferred_element_type=f32)
        d = d + jnp.dot(dgate[1], w2[1, :FFB, at], preferred_element_type=f32)
        d = d + jnp.dot(p[dup : dup + 512, :FFB], w2[0, FFB:, at], preferred_element_type=f32)
        d = d + jnp.dot(p[dup + 512 : dup + 1024, :FFB], w2[1, FFB:, at], preferred_element_type=f32)
        part[:, at] = d.astype(bf)
        return 0

    def outer(m, i):
        at = pl.ds(i * 512, 512)
        for b in range(2):
            w2[b, m * FFB : m * FFB + FFB, at] = jnp.dot(turned[m, b], n2[:, at], preferred_element_type=f32).astype(bf)

    lanes = {name: net.lane() for name in "twoducaxyzg"}
    back_a = reduce_z(lanes["x"], part, sums, got, pl.ds(0, D // 2))
    back_b = reduce_z(lanes["y"], part, sums, got, pl.ds(D // 2, D // 2))

    def main():
        yield from gather_8(lanes["t"], n1)
        yield
        save(8, n1, n1_out)
        save(9, w, w_out)
        save(10, table, table_out)
        lax.fori_loop(0, 2, project, 0)
        yield
        lax.fori_loop(2, 4, project, 0)
        for n, (src, dst) in enumerate(((q, q_out), (k, k_out), (v, v_out))):
            save(11 + n, src, dst)
        yield
        attend(0)
        yield
        attend(2)
        swapped = [exchange(0, 0, 256)]
        for h in (0, 1):
            yield
            attend(1, (h,))
            attend(3, (h,))
            swapped.append(exchange(1, h * 128, 128))
        kept = pltpu.make_async_copy(o.at[pl.ds(pl.multiple_of(net.xl * 512, 512), 512), :], branches.at[net.xl], local.at[15])
        kept.start()
        save(14, p, p_out)
        yield
        for sent in swapped:
            sent.wait_recv()
        kept.wait()
        saves.pop(8).wait()
        lanes["t"].flush()
        yield from reduce_z(lanes["a"], part, sums, got, make=branch)
        yield
        yield from gather_z(lanes["z"], lambda k: n2.at[half(net.z, k), :], n2, functools.partial(on_half, second_norm))
        save(23, h1, h1_out)
        lanes["a"].flush()
        saves.pop(14).wait()
        yield
        ahead(0)
        yield
        ahead(1)
        yield
        lax.fori_loop(0, 4, back, 0)
        forward(back_a)
        yield
        lax.fori_loop(4, 8, back, 0)
        forward(back_b)
        lanes["u"].flush()
        for i in range(4):
            yield
            outer(i // 2, i % 2 * 2)
            outer(i // 2, i % 2 * 2 + 1)

    def norm_back(at, half_at):
        here = pl.ds(at, 16)
        h = h1[here, :]
        r = lax.rsqrt(jnp.mean(h * h, axis=-1, keepdims=True) + EPS)
        d = reduced(net, part, got, at, half_at)
        inner = d * mlp_gain[...]
        grad = r * inner - h * (r * r * r) * jnp.mean(h * inner, axis=-1, keepdims=True)
        grad = cot[here, :].astype(f32) + grad
        dh1[here, :] = grad
        da[pl.ds(pl.multiple_of(net.z * ROWS + at, 16), 16), :] = grad.astype(bf)
        gain_part[...] += jnp.sum(d * h * r, axis=0, keepdims=True)

    swapped_back = []

    def back_out(z):
        here = block(z)
        for b in range(2):
            do[b, here, :] = lax.dot_general(da[here, :], w1[b, :256, :], NT, preferred_element_type=f32).astype(bf)
        rows = pl.ds(pl.multiple_of(net.xl * 512 + lax.rem(z + 8, 4) * ROWS, ROWS), ROWS)
        swapped_back.append(net.send(do.at[1 - net.xl, here, :], do_out.at[rows, :], net.beside))
        save(15 + len(swapped_back), do.at[net.xl, here, :], do_out.at[rows, :])

    def tail():
        for chain in (back_a, back_a, back_b, back_b, back_a):
            forward(chain)
            yield
        forward(back_b)
        gain_part[...] = jnp.zeros_like(gain_part)
        yield
        yield from gather_z(lanes["z"], lambda k: da.at[half(net.z, k), :], da, functools.partial(on_half, norm_back), back_out)
        save(24, dh1, dh1_out)

    def weights():
        for copied in own[:3]:
            copied.wait()
        yield from gather_plane(lanes["w"], lambda i, j: w.at[:, att_at(net, net.c, i, j), :], ATT_CUT, (net.across,), (net.device(dy=1), net.device(dy=-1)))

    def plane(lane, held, ref, at, cut, rows):
        for copied in held:
            copied.wait()
        yield from gather_plane(
            lane, lambda i, j: plane_slab(net, ref, net.c, i, j).at[pl.ds(at, rows), :], cut_at(cut, rows), net.along(True), net.along(False)
        )

    def cotangent():
        own[7].wait()
        yield from gather_z(lanes["c"], lambda k: cot.at[pl.ds(k * 64, 64), :], g)

    def hidden_grad():
        for b in range(2):
            if b:
                yield
            for at, n in TILES:
                u = lax.dot_general(g[...], w1[b, 256 + at : 256 + at + n, :], NT, preferred_element_type=f32)
                dgate[b, :, at : at + n] = u.astype(bf)

    def tables():
        def rows(i, _):
            at = pl.multiple_of(i * 128, 128)
            index, first = sequence_starts(lengths, at, 128)
            angle = (index - first).astype(f32) * rates[...]
            lane = lax.broadcasted_iota(jnp.int32, (128, 128), 1)
            table[0, pl.ds(at, 128), :] = jnp.cos(angle)
            sin = jnp.sin(angle)
            table[1, pl.ds(at, 128), :] = jnp.where(lane < 64, -sin, sin)
            return 0

        for i in range(4):
            if i:
                yield
            lax.fori_loop(2 * i, 2 * i + 2, rows, 0)

    def mixed_part():
        def columns(i, _):
            at = pl.ds(pl.multiple_of(i * 256, 256), 256)
            u = jnp.dot(p[hid : hid + 512, :FFB], w1[0, 256:, at], preferred_element_type=f32)
            u = u + jnp.dot(p[hid + 512 : hid + 1024, :FFB], w1[1, 256:, at], preferred_element_type=f32)
            m_part[:, at] = u.astype(bf)
            return 0

        for i in range(4):
            lax.fori_loop(2 * i, 2 * i + 2, columns, 0)
            yield
        save(20, m_part, m_out)
        for b in range(2):
            branches_turned[b] = branches[b].T
        lanes["d"].flush()
        for i in range(4):
            if i:
                yield
            at = pl.ds(i * 512, 512)
            for b in range(2):
                w1[b, 256:, at] = jnp.dot(turned[2, b], g[:, at], preferred_element_type=f32).astype(bf)
        save(21, w1.at[:, pl.ds(256, FFB), :], od_grad.at[:, pl.ds(256, FFB), :])

    def outer_out():
        lanes["o"].flush()

        def columns(i, _):
            at = pl.ds(pl.multiple_of(i * 512, 512), 512)
            for b in range(2):
                w1[b, :256, at] = jnp.dot(branches_turned[b], da[:, at], preferred_element_type=f32).astype(bf)
            return 0

        lax.fori_loop(0, 4, columns, 0)
        save(22, w1.at[:, pl.ds(0, 256), :], od_grad.at[:, pl.ds(0, 256), :])
        yield
        for sent in swapped_back:
            sent.wait_recv()

    def grads(m):
        def slab(kind):
            return lambda i, j: plane_slab(net, w2, kind, i, j).at[pl.ds(m * FFB, FFB), :]

        yield from reduce_plane(
            lanes["g"], slab(net.c), slab(1 - net.c),
            lambda i, j: sib.at[m, i, j], lambda i: got_half.at[m, i], lambda i: got_up.at[m, i], lambda i: got_down.at[m, i], lambda i: last.at[m, i],
            cut_at(FF_CUT, FFB), add_in(FF_CUT, FFB), net.along(True), net.along(False),
        )

    run(
        {
            "t": main(), "z": tail(), "w": weights(), "o": plane(lanes["o"], own[3:4], w1, 0, OUT // 2, OUT),
            "d": plane(lanes["d"], own[4:5], w1, OUT, FF_CUT, FFB), "u": plane(lanes["u"], own[5:7], w2, 0, GU_CUT, GU),
            "c": cotangent(), "h": hidden_grad(), "b": tables(), "m": mixed_part(), "q": outer_out(), "g": grads(0), "i": grads(1),
        },
        FRONT_ORDER,
    )
    gu_grad[...] = plane_slab(net, w2, net.c, 0, 0)[...]
    for saved in saves.values():
        saved.wait()
    net.finish()


def front(*args):
    bf, f32 = jnp.bfloat16, jnp.float32
    slab = (GU, 128)
    kept = (
        ((GROUP, D), bf), ((3, D, 256), bf), ((2, GROUP, 128), bf), ((2, GROUP, 128), bf), ((2, GROUP, 128), bf),
        ((2 * GROUP, 768), bf), ((2, GROUP, 128), f32),
    )
    kept += (((ROWS, D), f32), ((ROWS, D), f32))
    outs = kept + (((GROUP, 256), bf), ((512, D), bf), ((2, OD, D), bf), ((1, D), f32), (slab, bf))
    scratch = (((256, 128), bf),) + kept + (
        ((GROUP, 256), bf), ((2, 512, 256), bf), ((2, 256, 512), bf), ((2, OD, D), bf), ((2, GU, D), bf), ((512, D), bf), ((512, D), bf),
        ((2, 512, FFB), bf), ((3, 2, FFB, 512), bf), ((512, D), bf), ((2, 512, 256), bf), ((2, 64, D), bf), ((6, 64, D), bf),
        ((2, 4, 4, FFB, 128), bf), ((2, 4, FFB, 128), bf), ((2, 4, FFB, 128), bf), ((2, 4, FFB, 128), bf), ((2, 3, FFB, 128), bf),
    )
    return pl.pallas_call(
        front_kernel,
        name="front",
        out_shape=tuple(jax.ShapeDtypeStruct(*s) for s in outs),
        in_specs=[VMEM, VMEM, pl.BlockSpec(memory_space=pltpu.SMEM), VMEM, VMEM, VMEM, ANY, ANY, ANY, VMEM, ANY, ANY, ANY],
        out_specs=(ANY,) * 12 + (VMEM, VMEM),
        scratch_shapes=[pltpu.VMEM(*s) for s in scratch] + sems(272, 25),
        compiler_params=params(1, 64),
    )(*args)


def back_kernel(do_in, n1_in, w_in, q_in, k_in, v_in, p_in, table_in, m_in, od_in, tok_in, h1_in, dh1_in, gain, mlp_gain_part,
                    mixed, dx, gains, qkv_grad, od_grad,
                    tok, h1, dh1, do, n1, w, q, k, v, p, table, dqkv, dqkv_turned, dk, dv, part, sums, got, sums_half, got_half,
                    ga, sib, slab_half, slab_up, slab_down, slab_last, sum_z, sum_x, sum_y, sum_c,
                    m_part, sums_m, got_m, od, od_sib, od_half, od_up, od_down, od_last,
                    send_sems, recv_sems, local):
    net = Net(send_sems, recv_sems)
    bf, f32 = jnp.bfloat16, jnp.float32
    line_x = [net.device(dx=s) for s in (1, 2, 3)]
    line_y = [net.device(dy=s) for s in (1, 2, 3)]
    line_z = [net.device(dz=s) for s in (1, 2, 3)]
    net.greet(line_x + line_y + line_z + [net.device(dc=1)])
    loads = start(
        [
            pltpu.make_async_copy(src, dst, local.at[m])
            for m, (src, dst) in enumerate(
                (
                    (m_in, m_part), (do_in, do), (v_in, v), (p_in, p), (q_in, q), (k_in, k), (table_in, table), (w_in, w), (n1_in, n1),
                    (h1_in, h1), (tok_in, tok), (dh1_in, dh1),
                )
            )
        ]
    )
    slabs = start(
        [
            pltpu.make_async_copy(plane_slab(net, od_in, net.c, i, j), od.at[i, j], local.at[12 + n])
            for n, (i, j) in enumerate((i, j) for j in (2, 1, 3, 0) for i in (2, 3, 1, 0))
        ]
    )
    net.met()

    def attend_back(h, b):
        rows = slice(b * QROWS, b * QROWS + QROWS)
        first, until = max(0, b - 2) * QROWS, (b + 1) * QROWS
        keys, old = slice(first, until), slice(first, b * QROWS)
        weights_b = p[(h * 4 + b) * QROWS : (h * 4 + b + 1) * QROWS, 0 : until - first]
        do_b = do[rows, h * 128 : h * 128 + 128]
        dp = lax.dot_general(do_b, v[h, keys, :], NT, preferred_element_type=f32)
        wide = weights_b.astype(f32)
        centre = jnp.sum(wide * dp, axis=-1, keepdims=True)
        ds = (wide * (dp - centre)).astype(bf)
        dvb = lax.dot_general(weights_b, do_b, TN, preferred_element_type=f32)
        dkb = lax.dot_general(ds, q[h, rows, :], TN, preferred_element_type=f32)
        if b > 0:
            dv[h, old, :] += dvb[: b * QROWS - first]
            dk[h, old, :] += dkb[: b * QROWS - first]
        dv[h, rows, :] = dvb[b * QROWS - first :]
        dk[h, rows, :] = dkb[b * QROWS - first :]
        dqb = jnp.dot(ds, k[h, keys, :], preferred_element_type=f32) * HEAD_DIM ** (-0.5)
        dqb = dqb * table[0, rows, :] - pltpu.roll(dqb, 64, 1) * table[1, rows, :]
        dqkv[rows, h * 128 : h * 128 + 128] = dqb.astype(bf)

    def turn(i, _):
        here = pl.ds(pl.multiple_of(i * QROWS, QROWS), QROWS)
        for h in range(2):
            u = dk[h, here, :] * HEAD_DIM ** (-0.5)
            u = u * table[0, here, :] - pltpu.roll(u, 64, 1) * table[1, here, :]
            dqkv[here, 256 + h * 128 : 384 + h * 128] = u.astype(bf)
            dqkv[here, 512 + h * 128 : 640 + h * 128] = dv[h, here, :].astype(bf)
        dqkv_turned[:, here] = dqkv[here, :].T
        return 0

    def make(xl, z):
        here = block8(xl, z)
        left = dqkv[here, :]

        def columns(i, _):
            at = pl.ds(pl.multiple_of(i * 512, 512), 512)
            u = lax.dot_general(left[:, :256], w[0, at, :], NT, preferred_element_type=f32)
            u = u + lax.dot_general(left[:, 256:512], w[1, at, :], NT, preferred_element_type=f32)
            u = u + lax.dot_general(left[:, 512:], w[2, at, :], NT, preferred_element_type=f32)
            part[here, at] = u.astype(bf)
            sum_y[net.y, 0:1, at] += jnp.sum(u * n1[here, at].astype(f32), axis=0, keepdims=True)
            return 0

        lax.fori_loop(0, 4, columns, 0)

    out = []

    def step(at, k):
        here = pl.ds(at, 16)
        value = tok[here, :].astype(f32)
        r = lax.rsqrt(jnp.mean(value * value, axis=-1, keepdims=True) + EPS)
        inner = out[0](at, k) * gain[...]
        dx[here, :] = dh1[here, :] + r * inner - value * (r * r * r) * jnp.mean(value * inner, axis=-1, keepdims=True)

    def main():
        for copied in loads[1:7]:
            copied.wait()
        yield
        for b in range(GROUP // QROWS):
            for h in range(2):
                attend_back(h, b)
            yield
        lax.fori_loop(0, GROUP // QROWS, turn, 0)
        for copied in loads[7:9]:
            copied.wait()
        sum_y[net.y, 0:1, :] = jnp.zeros((1, D), f32)
        sum_y[net.y, 1:2, :] = mlp_gain_part[...]
        yield
        yield from reduce_8(net, make, part, sums, got, sums_half, got_half, out)
        for copied in loads[10:]:
            copied.wait()
        each_half(step)

    def early():
        chain = reduce_plane(
            net, lambda i, j: od.at[i, j], lambda i, j: plane_slab(net, od_in, 1 - net.c, i, j), lambda i, j: od_sib.at[i, j],
            lambda i: od_half.at[i], lambda i: od_up.at[i], lambda i: od_down.at[i], lambda i: od_last.at[i],
            cut_at(OD_CUT, OD), add_in(OD_CUT, OD), net.along(True), net.along(False),
        )
        forward(chain)
        yield
        for copied in slabs:
            copied.wait()
        yield from chain
        od_grad[...] = od[0, 0]

    def mixing():
        loads[0].wait()
        yield from reduce_z(net, m_part, sums_m, got_m)

        def mix(at, k):
            here = pl.ds(at, 16)
            mixed[here, :] = (h1[here, :] + reduced(net, m_part, got_m, at, k)).astype(bf)

        loads[9].wait()
        each_half(mix)

    def slab(kind):
        return lambda i, j: ga.at[:, att_at(net, kind, i, j)]

    def weights():
        def outer(i, _):
            at = pl.ds(pl.multiple_of(i * 256, 256), 256)
            ga[:, at] = jnp.dot(dqkv_turned[...], n1[:, at], preferred_element_type=f32).astype(bf)
            return 0

        for i in range(4):
            lax.fori_loop(2 * i, 2 * i + 2, outer, 0)
            yield
        yield from reduce_plane(
            net, slab(net.c), slab(1 - net.c), lambda i, j: sib.at[i, j], lambda i: slab_half.at[i], lambda i: slab_up.at[i],
            lambda i: slab_down.at[i], lambda i: slab_last.at[i], cut_at(QKV_CUT, QKV), add_in(QKV_CUT, QKV), (net.across,), (net.device(dy=1), net.device(dy=-1)),
        )
        qkv_grad[...] = slab(net.c)(0, 0)[...]

    def gain_sums():
        here = net.y
        stages = ((sum_y, line_y, sum_c, net.c), (sum_c, [net.device(dc=1)], sum_x, net.x), (sum_x, line_x, sum_z, net.z), (sum_z, line_z, None, None))
        for ref, line, then, place in stages:
            sent = [net.send(ref.at[here], ref.at[here], to) for to in line]
            yield
            for copied in sent:
                copied.wait_recv()
            total = ref[0]
            for n in range(1, len(line) + 1):
                total = total + ref[n]
            if then is None:
                gains[0:1, :] = total[0:1] / gain[...]
                gains[1:2, :] = total[1:2]
            else:
                then[place] = total
                here = place

    run({"t": main(), "m": mixing(), "e": early(), "w": weights(), "s": gain_sums()}, BACK_ORDER)
    net.finish()


def back(do, n1, w, q, k, v, p, table, m, od, tok, h1, dh1, gain, mlp_gain_part):
    bf, f32 = jnp.bfloat16, jnp.float32
    slab, slab_od = (QKV, 128), (OD, 128)
    scratch = [
        ((ROWS, D), bf), ((ROWS, D), f32), ((ROWS, D), f32),
        ((GROUP, 256), bf), ((GROUP, D), bf), ((3, D, 256), bf), ((2, GROUP, 128), bf), ((2, GROUP, 128), bf), ((2, GROUP, 128), bf),
        ((2 * GROUP, 768), bf), ((2, GROUP, 128), f32), ((GROUP, QKV), bf), ((QKV, GROUP), bf),
        ((2, GROUP, 128), f32), ((2, GROUP, 128), f32), ((GROUP, D), bf), ((2, ROWS, D), bf), ((4, ROWS, D), bf),
        ((2, 64, D), bf), ((6, 64, D), bf), ((QKV, D), bf), ((2, 4) + slab, bf), ((2,) + slab, bf), ((2,) + slab, bf),
        ((2,) + slab, bf), ((1,) + slab, bf), ((4, 2, D), f32), ((4, 2, D), f32), ((4, 2, D), f32), ((2, 2, D), f32),
        ((512, D), bf), ((2, 64, D), bf), ((6, 64, D), bf), ((4, 4) + slab_od, bf), ((4, 4) + slab_od, bf),
        ((4,) + slab_od, bf), ((4,) + slab_od, bf), ((4,) + slab_od, bf), ((3,) + slab_od, bf),
    ]
    outs = (((ROWS, D), bf), ((ROWS, D), f32), ((2, D), f32), (slab, bf), (slab_od, bf))
    return pl.pallas_call(
        back_kernel,
        name="back",
        out_shape=tuple(jax.ShapeDtypeStruct(*s) for s in outs),
        in_specs=[ANY] * 13 + [VMEM] * 2,
        out_specs=(VMEM,) * 5,
        scratch_shapes=[pltpu.VMEM(*s) for s in scratch] + sems(128, 28),
        compiler_params=params(2),
    )(do, n1, w, q, k, v, p, table, m, od, tok, h1, dh1, gain, mlp_gain_part)


def finish_kernel(mixed_in, dx_in, gains_in, qkv_in, od_in, gu_in, mixed, dx, ag, gq, gk, gv, go, mg, gg, gu_out, gd, gains, qkv, od, gu, sems):
    f32 = jnp.float32
    pairs = ((gu_in, gu), (od_in, od), (qkv_in, qkv), (gains_in, gains), (mixed_in, mixed), (dx_in, dx))
    loads = start([pltpu.make_async_copy(src, dst, sems.at[n]) for n, (src, dst) in enumerate(pairs)])
    for load in loads[:4]:
        load.wait()
    gg[...] = gu[:FFB, :].astype(f32)
    gu_out[...] = gu[FFB:, :].astype(f32)
    go[...] = od[:256, :].astype(f32).T
    gd[...] = od[256:, :].astype(f32)
    for n, dst in enumerate((gq, gk, gv)):
        dst[...] = qkv[n * 256 : n * 256 + 256, :].astype(f32).T
    ag[...] = gains[0:1, :]
    mg[...] = gains[1:2, :]
    for load in loads[4:]:
        load.wait()


def finish(mixed, dx, gains, qkv, od, gu):
    f32, bf = jnp.float32, jnp.bfloat16
    outs = (
        ((ROWS, D), bf), ((ROWS, D), f32), ((1, D), f32), ((ROWS, 256), f32), ((ROWS, 256), f32), ((ROWS, 256), f32),
        ((ROWS, 256), f32), ((1, D), f32), ((FFB, 128), f32), ((FFB, 128), f32), ((FFB, 128), f32),
    )
    held = (((2, D), f32), ((QKV, 128), bf), ((OD, 128), bf), ((GU, 128), bf))
    return pl.pallas_call(
        finish_kernel,
        name="finish",
        out_shape=tuple(jax.ShapeDtypeStruct(*s) for s in outs),
        in_specs=[ANY] * 6,
        out_specs=(VMEM,) * 11,
        scratch_shapes=[pltpu.VMEM(*s) for s in held] + [pltpu.SemaphoreType.DMA((6,))],
        compiler_params=pltpu.CompilerParams(vmem_limit_bytes=60 << 20),
    )(mixed, dx, gains, qkv, od, gu)


def shards(
    tokens,
    lengths,
    attn_gain,
    query_weight,
    key_weight,
    value_weight,
    out_weight,
    mlp_gain,
    gate_weight,
    up_weight,
    down_weight,
    cotangent,
):
    half_rates = THETA ** (-(np.arange(64, dtype=np.float32) * np.float32(2.0 / HEAD_DIM)))
    rates = jnp.asarray(np.concatenate([half_rates, half_rates])[None].astype(np.float32))
    n1, w, q, k, v, p, table, h1, dh1, do, m, od_part, gain_part, gu = front(
        tokens, cotangent, lengths, attn_gain[None], mlp_gain[None], rates, query_weight, key_weight, value_weight, out_weight,
        gate_weight.T, up_weight.T, down_weight.T,
    )
    mixed, dx, gains, qkv, od_grad = back(do, n1, w, q, k, v, p, table, m, od_part, tokens, h1, dh1, attn_gain[None], gain_part)
    mixed, dx, ag, gq, gk, gv, go, mg, gg, gu, gd = finish(mixed, dx, gains, qkv, od_grad, gu)
    return (mixed, dx, ag[0], gq, gk, gv, go, mg[0], gg.T, gu.T, gd.T)


def solution(mesh):
    return jax.shard_map(
        shards,
        mesh=mesh,
        in_specs=(
            P(("dp", "tensor"), None),
            P("dp", None),
            P(),
            P("dp", "tensor"),
            P("dp", "tensor"),
            P("dp", "tensor"),
            P("dp", "tensor"),
            P(),
            P("dp", "tensor"),
            P("dp", "tensor"),
            P("dp", "tensor"),
            P(("dp", "tensor"), None),
        ),
        out_specs=(
            P(("dp", "tensor"), None),
            P(("dp", "tensor"), None),
            P(),
            P("dp", "tensor"),
            P("dp", "tensor"),
            P("dp", "tensor"),
            P("dp", "tensor"),
            P(),
            P("dp", "tensor"),
            P("dp", "tensor"),
            P("dp", "tensor"),
        ),
        check_vma=False,
    )
```

```python
import copy
import functools

import jax
import jax.numpy as jnp
import numpy as np
from jax import lax
from jax.experimental import pallas as pl
from jax.experimental.pallas import tpu as pltpu
from jax.sharding import PartitionSpec as P

HEAD_DIM = 128
EPS = 1e-05
THETA = 10000.0
D = 2048
ROWS = 128
GROUP = 1024
FFB = 688
QROWS = 256
MESH = pl.DeviceIdType.MESH
ANY = pl.BlockSpec(memory_space=pl.ANY)
VMEM = pl.BlockSpec(memory_space=pltpu.VMEM)
NT = (((1,), (1,)), ((), ()))
TN = (((0,), (0,)), ((), ()))


class Net:
    def __init__(self, send_sems, recv_sems):
        dp, t = lax.axis_index("dp"), lax.axis_index("tensor")
        self.y, self.c = lax.div(dp, 4), lax.rem(dp, 2)
        self.xl, self.z = lax.div(t, 4), lax.rem(t, 4)
        self.x = lax.rem(lax.div(dp, 2), 2) * 2 + self.xl
        self.dp, self.t = dp, t
        self.send_sems, self.recv_sems = send_sems, recv_sems
        self.used = [0]
        self.sent = []
        self.lanes = [self]

    def lane(self):
        other = copy.copy(self)
        other.sent = []
        self.lanes.append(other)
        return other

    def device(self, dx=0, dy=0, dz=0, dc=0):
        x, y = lax.rem(self.x + dx + 4, 4), lax.rem(self.y + dy + 4, 4)
        z, c = lax.rem(self.z + dz + 4, 4), lax.rem(self.c + dc, 2)
        return (y * 4 + lax.div(x, 2) * 2 + c, lax.rem(x, 2) * 4 + z)

    @property
    def beside(self):
        return (self.dp, (1 - self.xl) * 4 + self.z)

    @property
    def across(self):
        return self.device(dx=2)

    def along(self, first):
        on_x = self.c == (0 if first else 1)
        both = []
        for step in (1, -1):
            by_x, by_y = self.device(dx=step), self.device(dy=step)
            both.append(tuple(jnp.where(on_x, u, v) for u, v in zip(by_x, by_y)))
        return both

    def send(self, src, dst, to):
        k = self.used[0]
        self.used[0] += 1
        sent = pltpu.make_async_remote_copy(
            src_ref=src,
            dst_ref=dst,
            send_sem=self.send_sems.at[k],
            recv_sem=self.recv_sems.at[k],
            device_id=to,
            device_id_type=MESH,
        )
        sent.start()
        self.sent.append(sent)
        return sent

    def flush(self):
        for sent in self.sent:
            sent.wait_send()
        self.sent.clear()

    def finish(self):
        for lane in self.lanes:
            lane.flush()

    def greet(self, devices):
        for device in devices:
            pl.semaphore_signal(pltpu.get_barrier_semaphore(), inc=1, device_id=device, device_id_type=MESH)
        self.greeted = len(devices)

    def met(self):
        pl.semaphore_wait(pltpu.get_barrier_semaphore(), self.greeted)


def block(z):
    return pl.ds(pl.multiple_of(lax.rem(z + 8, 4) * ROWS, ROWS), ROWS)


def half(z, k):
    return pl.ds(pl.multiple_of(lax.rem(z + 8, 4) * ROWS + k * 64, 64), 64)


def block8(xl, z):
    return pl.ds(pl.multiple_of((xl * 4 + lax.rem(z + 8, 4)) * ROWS, ROWS), ROWS)


def half8(xl, z, k):
    return pl.ds(pl.multiple_of((xl * 4 + lax.rem(z + 8, 4)) * ROWS + k * 64, 64), 64)


def add_rows(rows, dst, *terms):
    def step(i, _):
        at = pl.ds(pl.multiple_of(i * 16, 16), 16)
        total = terms[0][at, :].astype(jnp.float32)
        for term in terms[1:]:
            total = total + term[at, :].astype(jnp.float32)
        dst[at, :] = total.astype(dst.dtype)
        return 0

    lax.fori_loop(0, rows // 16, step, 0)


def gather_z(net, own, dst, fill=None, arrived=None):
    up, down = net.device(dz=1), net.device(dz=-1)
    z = net.z
    place = [dst.at[half(z, k), :] for k in (0, 1)]
    if fill:
        fill(0)
    up_0 = net.send(own(0), place[0], up)
    if fill:
        yield
        fill(1)
    down_1 = net.send(own(1), place[1], down)
    up_1 = net.send(own(1), place[1], up)
    down_0 = net.send(own(0), place[0], down)
    yield
    if arrived:
        arrived(z)
        yield
    up_0.wait_recv()
    ref = dst.at[half(z - 1, 0), :]
    on_0 = net.send(ref, ref, up)
    yield
    down_1.wait_recv()
    ref = dst.at[half(z + 1, 1), :]
    on_1 = net.send(ref, ref, down)
    yield
    up_1.wait_recv()
    if arrived:
        arrived(z - 1)
    yield
    down_0.wait_recv()
    if arrived:
        arrived(z + 1)
    yield
    on_0.wait_recv()
    on_1.wait_recv()
    if arrived:
        arrived(z + 2)


def reduce_z(net, part, sums, got, cols=pl.ds(0, D), make=None):
    up, down = net.device(dz=1), net.device(dz=-1)
    z = net.z
    if make:
        make(z + 2)
    c0 = net.send(part.at[half(z + 2, 0), cols], got.at[0, :, cols], up)
    c1 = net.send(part.at[half(z + 2, 1), cols], got.at[1, :, cols], down)
    if make:
        yield
        make(z + 1)
    d1 = net.send(part.at[half(z + 1, 1), cols], got.at[3, :, cols], up)
    if make:
        yield
        make(z - 1)
    d2 = net.send(part.at[half(z - 1, 0), cols], got.at[4, :, cols], down)
    if make:
        yield
        make(z)
    yield
    c0.wait_recv()
    add_rows(64, sums.at[0, :, cols], part.at[half(z + 1, 0), cols], got.at[0, :, cols])
    d0 = net.send(sums.at[0, :, cols], got.at[2, :, cols], up)
    yield
    c1.wait_recv()
    add_rows(64, sums.at[1, :, cols], part.at[half(z - 1, 1), cols], got.at[1, :, cols])
    d3 = net.send(sums.at[1, :, cols], got.at[5, :, cols], down)
    yield
    for sent in (d0, d1, d2, d3):
        sent.wait_recv()


def reduced(net, part, got, at, k):
    here = pl.ds(pl.multiple_of(at - 64 * k, 16), 16)
    total = part[pl.ds(pl.multiple_of(net.z * ROWS + at, 16), 16), :].astype(jnp.float32)
    return total + got[2 + k, here, :].astype(jnp.float32) + got[4 + k, here, :].astype(jnp.float32)


def gather_8(net, dst):
    up, down, beside = net.device(dz=1), net.device(dz=-1), net.beside
    xl, z = net.xl, net.z

    def send(x, dz, k, to):
        ref = dst.at[half8(x, z + dz, k), :]
        return net.send(ref, ref, to)

    up_0, down_1 = send(xl, 0, 0, up), send(xl, 0, 1, down)
    up_1, down_0 = send(xl, 0, 1, up), send(xl, 0, 0, down)
    side_0, side_1 = send(xl, 0, 0, beside), send(xl, 0, 1, beside)
    yield
    up_0.wait_recv()
    on_0 = send(xl, -1, 0, up)
    yield
    down_1.wait_recv()
    on_1 = send(xl, 1, 1, down)
    yield
    side_0.wait_recv()
    rest = [send(1 - xl, 0, 0, up), send(1 - xl, 0, 0, down)]
    yield
    side_1.wait_recv()
    rest += [send(1 - xl, 0, 1, up), send(1 - xl, 0, 1, down)]
    yield
    on_0.wait_recv()
    rest.append(send(xl, 2, 0, beside))
    yield
    on_1.wait_recv()
    rest.append(send(xl, 2, 1, beside))
    yield
    for sent in [up_1, down_0] + rest:
        sent.wait_recv()


def reduce_8(net, make, part, sums, got, sums_half, got_half, out):
    up, down, beside = net.device(dz=1), net.device(dz=-1), net.beside
    xl, z = net.xl, net.z
    halves = [pl.ds(0, 64), pl.ds(64, 64)]
    make(1 - xl, z + 2)
    a = [net.send(part.at[half8(1 - xl, z + 2, k), :], got.at[0, halves[k], :], beside) for k in (0, 1)]
    yield
    make(1 - xl, z + 1)
    b0 = net.send(part.at[block8(1 - xl, z + 1), :], got.at[1], up)
    yield
    make(1 - xl, z - 1)
    b1 = net.send(part.at[block8(1 - xl, z - 1), :], got.at[2], down)
    yield
    for step in (2, 1, -1):
        make(xl, z + step)
        yield
    a[0].wait_recv()
    add_rows(64, sums.at[0, halves[0], :], part.at[half8(xl, z + 2, 0), :], got.at[0, halves[0], :])
    c0 = net.send(sums.at[0, halves[0], :], got_half.at[0], up)
    yield
    a[1].wait_recv()
    add_rows(64, sums.at[0, halves[1], :], part.at[half8(xl, z + 2, 1), :], got.at[0, halves[1], :])
    c1 = net.send(sums.at[0, halves[1], :], got_half.at[1], down)
    d1 = net.send(part.at[half8(xl, z + 1, 1), :], got_half.at[3], up)
    d2 = net.send(part.at[half8(xl, z - 1, 0), :], got_half.at[4], down)
    yield
    make(1 - xl, z)
    yield
    make(xl, z)
    yield
    b0.wait_recv()
    b1.wait_recv()
    add_rows(128, sums.at[1], part.at[block8(1 - xl, z), :], got.at[1], got.at[2])
    e = net.send(sums.at[1], got.at[3], beside)
    yield
    c0.wait_recv()
    add_rows(64, sums_half.at[0], part.at[half8(xl, z + 1, 0), :], got_half.at[0])
    d0 = net.send(sums_half.at[0], got_half.at[2], up)
    yield
    c1.wait_recv()
    add_rows(64, sums_half.at[1], part.at[half8(xl, z - 1, 1), :], got_half.at[1])
    d3 = net.send(sums_half.at[1], got_half.at[5], down)
    yield
    for sent in (e, d0, d1, d2, d3):
        sent.wait_recv()

    def rows(at, k):
        here = pl.ds(pl.multiple_of(at - 64 * k, 16), 16)
        total = part[pl.ds(pl.multiple_of(net.t * ROWS + at, 16), 16), :].astype(jnp.float32)
        total = total + got[3, pl.ds(pl.multiple_of(at, 16), 16), :].astype(jnp.float32)
        return total + got_half[2 + k, here, :].astype(jnp.float32) + got_half[4 + k, here, :].astype(jnp.float32)

    out.append(rows)


def on_half(step, k):
    def body(i, _):
        step(pl.multiple_of(k * 64 + i * 16, 16), k)
        return 0

    lax.fori_loop(0, 4, body, 0)


def each_half(step):
    for k in (0, 1):
        on_half(step, k)


def gather_plane(net, slab, cut, first, second):
    low, high = cut
    sib = net.device(dc=1)
    second_up, second_down = second
    shared, halves, sent = [], {}, {}

    def share(i, j):
        ref = slab(i, j)
        shared.append(net.send(ref, ref, sib))

    def go(i):
        ref = slab(i, 0)
        sent[i] = (net.send(ref, ref, second_up), net.send(ref, ref, second_down))

    def on(i):
        sent[i][0].wait_recv()
        ref = low(slab(i, -1))
        up = net.send(ref, ref, second_up)
        share(i, -1)
        yield
        sent[i][1].wait_recv()
        ref = high(slab(i, 1))
        halves[i] = (up, net.send(ref, ref, second_down))
        share(i, 1)
        yield

    own = slab(0, 0)
    ring = len(first) == 2
    around = [net.send(own, own, to) for to in first]
    go(0)
    share(0, 0)
    yield
    if ring:
        around[0].wait_recv()
        ref = low(slab(-1, 0))
        f0 = net.send(ref, ref, first[0])
        go(-1)
        share(-1, 0)
        yield
        around[1].wait_recv()
        ref = high(slab(1, 0))
        f1 = net.send(ref, ref, first[1])
        go(1)
        share(1, 0)
        yield
        yield from on(0)
        f0.wait_recv()
        f1.wait_recv()
        go(2)
        share(2, 0)
        yield
        for i in (-1, 1, 2):
            yield from on(i)
    else:
        around[0].wait_recv()
        go(1)
        share(1, 0)
        yield
        for i in (0, 1):
            yield from on(i)
    for i in sent:
        halves[i][0].wait_recv()
        halves[i][1].wait_recv()
        share(i, 2)
        yield
    for copied in shared:
        copied.wait_recv()


def reduce_plane(net, mine, other, from_sib, got_half, got_up, got_down, last_bufs, cut, add, first, second):
    low, high = cut
    sib = net.device(dc=1)
    up, down = second
    ring = len(first) == 2
    steps = (2, 3, 1, 0) if ring else (1, 0)
    shared = {}
    for j in (2, 1, 3, 0):
        for i in steps:
            shared[i, j] = net.send(other(i, j), from_sib(i, j), sib)
    yield
    halves, full, last = {}, {}, {}
    for i in steps:
        shared[i, 2].wait_recv()
        add(None, mine(i, 2), from_sib(i, 2))
        halves[i] = (
            net.send(low(mine(i, 2)), low(got_half(i)), up),
            net.send(high(mine(i, 2)), high(got_half(i)), down),
        )
        yield
    for i in steps:
        shared[i, 1].wait_recv()
        halves[i][0].wait_recv()
        add(0, mine(i, 1), from_sib(i, 1), got_half(i))
        add(1, mine(i, 1), from_sib(i, 1))
        u = net.send(mine(i, 1), got_up(i), up)
        yield
        shared[i, 3].wait_recv()
        halves[i][1].wait_recv()
        add(0, mine(i, 3), from_sib(i, 3))
        add(1, mine(i, 3), from_sib(i, 3), got_half(i))
        full[i] = (u, net.send(mine(i, 3), got_down(i), down))
        yield
    for i in steps:
        shared[i, 0].wait_recv()
        full[i][0].wait_recv()
        full[i][1].wait_recv()
        add(None, mine(i, 0), from_sib(i, 0), got_up(i), got_down(i))
        if ring and i == 2:
            ref, to = mine(2, 0), last_bufs(2)
            last[2] = (net.send(low(ref), low(to), first[0]), net.send(high(ref), high(to), first[1]))
        if ring and i == 3:
            last[2][1].wait_recv()
            add(1, mine(3, 0), last_bufs(2))
            last[3] = net.send(mine(3, 0), last_bufs(1), first[1])
        if ring and i == 1:
            last[2][0].wait_recv()
            add(0, mine(1, 0), last_bufs(2))
        if i == 1:
            last[1] = net.send(mine(1, 0), last_bufs(0), first[0])
        yield
    last[1].wait_recv()
    if ring:
        last[3].wait_recv()
        add(None, mine(0, 0), last_bufs(0), last_bufs(1))
    else:
        add(None, mine(0, 0), last_bufs(0))


ATT_CUT = (lambda ref: ref.at[:, pl.ds(0, 64), :], lambda ref: ref.at[:, pl.ds(64, 64), :])


def add_in(cut, total):
    def add(part, dst, *terms):
        begin, n = {None: (0, total), 0: (0, cut), 1: (cut, total - cut)}[part]

        def piece(at, size):
            here = pl.ds(at, size)
            value = dst[here, :].astype(jnp.float32)
            for term in terms:
                value = value + term[here, :].astype(jnp.float32)
            dst[here, :] = value.astype(dst.dtype)

        def step(i, _):
            piece(pl.multiple_of(begin + i * 160, 16), 160)
            return 0

        lax.fori_loop(0, n // 160, step, 0)
        if n % 160:
            piece(begin + n // 160 * 160, n % 160)

    return add


def cut_at(cut, total):
    return (lambda ref: ref.at[pl.ds(0, cut), :], lambda ref: ref.at[pl.ds(cut, total - cut), :])


OD, OD_CUT = 944, 480
GU, GU_CUT = 1376, 688
QKV, QKV_CUT = 768, 384
OUT, FF_CUT = 256, 352


def plane_slab(net, ref, kind, i, j):
    x = lax.rem(net.x + jnp.where(kind == 0, i, j) + 4, 4)
    y = lax.rem(net.y + jnp.where(kind == 0, j, i) + 4, 4)
    at = pl.ds(pl.multiple_of((y * 4 + lax.div(x, 2) * 2 + kind) * 128, 128), 128)
    return ref.at[lax.rem(x, 2), :, at]


def att_at(net, kind, i, j):
    x, y = lax.rem(net.x + 2 * i + 4, 4), lax.rem(net.y + j + 4, 4)
    return pl.ds(pl.multiple_of((y * 4 + lax.div(x, 2) * 2 + kind) * 128, 128), 128)


def forward(chain):
    next(chain, None)


def run(chains, order):
    for name in "".join(order):
        next(chains[name], None)
    for chain in chains.values():
        for _ in chain:
            pass


def start(copies):
    for copy in copies:
        copy.start()
    return copies


def sequence_starts(lengths, at, rows):
    index = lax.broadcasted_iota(jnp.int32, (rows, 1), 0) + at
    limit, first = lengths[0, 0], jnp.zeros((rows, 1), jnp.int32)
    for s in range(8):
        first = jnp.where(index >= limit, limit, first)
        if s < 7:
            limit = limit + lengths[0, s + 1]
    return index, first


def params(collective, mib=58):
    return pltpu.CompilerParams(collective_id=collective, has_side_effects=True, vmem_limit_bytes=mib << 20)


def sems(n, local):
    return [pltpu.SemaphoreType.DMA((n,)), pltpu.SemaphoreType.DMA((n,)), pltpu.SemaphoreType.DMA((local,))]


FRONT_ORDER = (
    "otwoobtobtbbttttwwwcwwwoooooowtdwtotttttccooodod",
    "ocotttdddddutttuudtttddddduuduuuuudccttdhuuuhuuu",
    "tttuttttttgzggzggtgzzggggtigiiiizzzziiimiiimiiim",
    "ggzzgzmmzziigmgmmzqggiiq",
)
BACK_ORDER = (
    "emeeeetteeettttttttttwwteeweeeettttwwswttwwwsemm",
    "seewwwstemwsw",
)


TILES = ((0, 256), (256, 256), (512, 176))


def front_kernel(tok, cot, lengths, gain, mlp_gain, rates, wq, wk, wv, wo, wg, wu, wd,
                 n1_out, w_out, q_out, k_out, v_out, p_out, table_out, h1_out, dh1_out, do_out, m_out, od_grad, gain_part, gu_grad,
                 wo_turned, n1, w, q, k, v, p, table, h1, dh1, o, branches, branches_turned, w1, w2, g, n2, dgate, turned, da, do, sums, got,
                 sib, got_half, got_up, got_down, last, send_sems, recv_sems, local):
    net = Net(send_sems, recv_sems)
    bf, f32 = jnp.bfloat16, jnp.float32
    net.greet([net.device(dx=s) for s in (1, 2, 3)] + [net.device(dy=1), net.device(dy=-1), net.device(dz=1), net.device(dz=-1), net.device(dc=1)])
    hid, dup = 0, 1024
    own_rows = att_at(net, net.c, 0, 0)
    own_od, own_gu = plane_slab(net, w1, net.c, 0, 0), plane_slab(net, w2, net.c, 0, 0)
    wo_turned[...] = wo[...].T
    own = start(
        [
            pltpu.make_async_copy(src, dst, local.at[n])
            for n, (src, dst) in enumerate(
                (
                    (wq, w.at[0, own_rows, :]), (wk, w.at[1, own_rows, :]), (wv, w.at[2, own_rows, :]),
                    (wo_turned, own_od.at[pl.ds(0, 256), :]), (wd, own_od.at[pl.ds(256, FFB), :]),
                    (wg, own_gu.at[pl.ds(0, FFB), :]), (wu, own_gu.at[pl.ds(FFB, FFB), :]), (cot, g.at[block(net.z), :]),
                )
            )
        ]
    )

    def norm(at, _):
        here = pl.ds(at, 16)
        value = tok[here, :].astype(f32)
        r = lax.rsqrt(jnp.mean(value * value, axis=-1, keepdims=True) + EPS)
        n1[pl.ds(pl.multiple_of(net.t * ROWS + at, 16), 16), :] = (value * r * gain[...]).astype(bf)

    each_half(norm)
    net.met()
    part, m_part = n1.at[pl.ds(0, 512), :], n1.at[pl.ds(512, 512), :]
    saves = {}

    def save(n, src, dst):
        saves[n] = pltpu.make_async_copy(src, dst, local.at[n])
        saves[n].start()

    def project(i, _):
        here = pl.ds(pl.multiple_of(i * QROWS, QROWS), QROWS)
        left = n1[here, :]
        cos, sin = table[0, here, :], table[1, here, :]
        for m, dst in ((0, q), (1, k)):
            u = jnp.dot(left, w[m], preferred_element_type=f32)
            for h in range(2):
                uh = u[:, h * 128 : h * 128 + 128]
                dst[h, here, :] = (uh * cos + pltpu.roll(uh, 64, 1) * sin).astype(bf)
        u = jnp.dot(left, w[2], preferred_element_type=f32).astype(bf)
        for h in range(2):
            v[h, here, :] = u[:, h * 128 : h * 128 + 128]
        return 0

    def attend(b, heads=(0, 1)):
        rows = slice(b * QROWS, b * QROWS + QROWS)
        first, until = max(0, b - 2) * QROWS, (b + 1) * QROWS
        index, begin = sequence_starts(lengths, b * QROWS, QROWS)
        key = lax.broadcasted_iota(jnp.int32, (QROWS, until - first), 1) + first
        allowed = (key <= index) & (key >= begin)
        for h in heads:
            s = lax.dot_general(q[h, rows, :], k[h, first:until, :], NT, preferred_element_type=f32)
            s = jnp.where(allowed, s * HEAD_DIM ** (-0.5), -1e30)
            e = jnp.exp(s - jnp.max(s, axis=-1, keepdims=True))
            weights = (e / jnp.sum(e, axis=-1, keepdims=True)).astype(bf)
            p[(h * 4 + b) * QROWS : (h * 4 + b + 1) * QROWS, 0 : until - first] = weights
            o[rows, h * 128 : h * 128 + 128] = jnp.dot(weights, v[h, first:until, :], preferred_element_type=f32).astype(bf)

    def exchange(n, at, size):
        src = o.at[pl.ds(pl.multiple_of((1 - net.xl) * 512 + n * QROWS, QROWS), QROWS), pl.ds(at, size)]
        return net.send(src, branches.at[net.xl, pl.ds(n * QROWS, QROWS), pl.ds(at, size)], net.beside)

    def branch(z):
        here = block(z)
        u = jnp.dot(branches[0, here, :], w1[0, :256, :], preferred_element_type=f32)
        u = u + jnp.dot(branches[1, here, :], w1[1, :256, :], preferred_element_type=f32)
        part[here, :] = u.astype(bf)

    def second_norm(at, half_at):
        here = pl.ds(at, 16)
        h = tok[here, :].astype(f32) + reduced(net, part, got, at, half_at)
        h1[here, :] = h
        r = lax.rsqrt(jnp.mean(h * h, axis=-1, keepdims=True) + EPS)
        n2[pl.ds(pl.multiple_of(net.z * ROWS + at, 16), 16), :] = (h * r * mlp_gain[...]).astype(bf)

    def ahead(b):
        for at, n in TILES:
            gate = lax.dot_general(n2[...], w2[b, at : at + n, :], NT, preferred_element_type=f32)
            up = lax.dot_general(n2[...], w2[b, FFB + at : FFB + at + n, :], NT, preferred_element_type=f32)
            dh = dgate[b, :, at : at + n].astype(f32)
            sig = jax.nn.sigmoid(gate)
            act = gate * sig
            dg, du, hi = (dh * up * sig * (1.0 + gate * (1.0 - sig))).astype(bf), (dh * act).astype(bf), (act * up).astype(bf)
            dgate[b, :, at : at + n] = dg
            p[dup + b * 512 : dup + b * 512 + 512, at : at + n] = du
            p[hid + b * 512 : hid + b * 512 + 512, at : at + n] = hi
            for m, value in enumerate((dg, du, hi)):
                turned[m, b, at : at + n, :] = value.T

    def back(i, _):
        at = pl.ds(pl.multiple_of(i * 512, 512), 512)
        d = jnp.dot(dgate[0], w2[0, :FFB, at], preferred_element_type=f32)
        d = d + jnp.dot(dgate[1], w2[1, :FFB, at], preferred_element_type=f32)
        d = d + jnp.dot(p[dup : dup + 512, :FFB], w2[0, FFB:, at], preferred_element_type=f32)
        d = d + jnp.dot(p[dup + 512 : dup + 1024, :FFB], w2[1, FFB:, at], preferred_element_type=f32)
        part[:, at] = d.astype(bf)
        return 0

    def outer(m, i):
        at = pl.ds(i * 512, 512)
        for b in range(2):
            w2[b, m * FFB : m * FFB + FFB, at] = jnp.dot(turned[m, b], n2[:, at], preferred_element_type=f32).astype(bf)

    lanes = {name: net.lane() for name in "twoducaxyzg"}
    back_a = reduce_z(lanes["x"], part, sums, got, pl.ds(0, D // 2))
    back_b = reduce_z(lanes["y"], part, sums, got, pl.ds(D // 2, D // 2))

    def main():
        yield from gather_8(lanes["t"], n1)
        yield
        save(8, n1, n1_out)
        save(9, w, w_out)
        save(10, table, table_out)
        lax.fori_loop(0, 2, project, 0)
        yield
        lax.fori_loop(2, 4, project, 0)
        for n, (src, dst) in enumerate(((q, q_out), (k, k_out), (v, v_out))):
            save(11 + n, src, dst)
        yield
        attend(0)
        yield
        attend(2)
        swapped = [exchange(0, 0, 256)]
        for h in (0, 1):
            yield
            attend(1, (h,))
            attend(3, (h,))
            swapped.append(exchange(1, h * 128, 128))
        kept = pltpu.make_async_copy(o.at[pl.ds(pl.multiple_of(net.xl * 512, 512), 512), :], branches.at[net.xl], local.at[15])
        kept.start()
        save(14, p, p_out)
        yield
        for sent in swapped:
            sent.wait_recv()
        kept.wait()
        saves.pop(8).wait()
        lanes["t"].flush()
        yield from reduce_z(lanes["a"], part, sums, got, make=branch)
        yield
        yield from gather_z(lanes["z"], lambda k: n2.at[half(net.z, k), :], n2, functools.partial(on_half, second_norm))
        save(23, h1, h1_out)
        lanes["a"].flush()
        saves.pop(14).wait()
        yield
        ahead(0)
        yield
        ahead(1)
        yield
        lax.fori_loop(0, 2, back, 0)
        forward(back_a)
        yield
        lax.fori_loop(2, 4, back, 0)
        forward(back_b)
        lanes["u"].flush()
        for i in range(4):
            yield
            outer(i // 2, i % 2 * 2)
            outer(i // 2, i % 2 * 2 + 1)

    def norm_back(at, half_at):
        here = pl.ds(at, 16)
        h = h1[here, :]
        r = lax.rsqrt(jnp.mean(h * h, axis=-1, keepdims=True) + EPS)
        d = reduced(net, part, got, at, half_at)
        inner = d * mlp_gain[...]
        grad = r * inner - h * (r * r * r) * jnp.mean(h * inner, axis=-1, keepdims=True)
        grad = cot[here, :].astype(f32) + grad
        dh1[here, :] = grad
        da[pl.ds(pl.multiple_of(net.z * ROWS + at, 16), 16), :] = grad.astype(bf)
        gain_part[...] += jnp.sum(d * h * r, axis=0, keepdims=True)

    swapped_back = []

    def back_out(z):
        here = block(z)
        for b in range(2):
            do[b, here, :] = lax.dot_general(da[here, :], w1[b, :256, :], NT, preferred_element_type=f32).astype(bf)
        rows = pl.ds(pl.multiple_of(net.xl * 512 + lax.rem(z + 8, 4) * ROWS, ROWS), ROWS)
        swapped_back.append(net.send(do.at[1 - net.xl, here, :], do_out.at[rows, :], net.beside))
        save(15 + len(swapped_back), do.at[net.xl, here, :], do_out.at[rows, :])

    def tail():
        for chain in (back_a, back_a, back_b, back_b, back_a):
            forward(chain)
            yield
        forward(back_b)
        gain_part[...] = jnp.zeros_like(gain_part)
        yield
        yield from gather_z(lanes["z"], lambda k: da.at[half(net.z, k), :], da, functools.partial(on_half, norm_back), back_out)
        save(24, dh1, dh1_out)

    def weights():
        for copied in own[:3]:
            copied.wait()
        yield from gather_plane(lanes["w"], lambda i, j: w.at[:, att_at(net, net.c, i, j), :], ATT_CUT, (net.across,), (net.device(dy=1), net.device(dy=-1)))

    def plane(lane, held, ref, at, cut, rows):
        for copied in held:
            copied.wait()
        yield from gather_plane(
            lane, lambda i, j: plane_slab(net, ref, net.c, i, j).at[pl.ds(at, rows), :], cut_at(cut, rows), net.along(True), net.along(False)
        )

    def cotangent():
        own[7].wait()
        yield from gather_z(lanes["c"], lambda k: cot.at[pl.ds(k * 64, 64), :], g)

    def hidden_grad():
        for b in range(2):
            if b:
                yield
            for at, n in TILES:
                u = lax.dot_general(g[...], w1[b, 256 + at : 256 + at + n, :], NT, preferred_element_type=f32)
                dgate[b, :, at : at + n] = u.astype(bf)

    def tables():
        def rows(i, _):
            at = pl.multiple_of(i * 128, 128)
            index, first = sequence_starts(lengths, at, 128)
            angle = (index - first).astype(f32) * rates[...]
            lane = lax.broadcasted_iota(jnp.int32, (128, 128), 1)
            table[0, pl.ds(at, 128), :] = jnp.cos(angle)
            sin = jnp.sin(angle)
            table[1, pl.ds(at, 128), :] = jnp.where(lane < 64, -sin, sin)
            return 0

        for i in range(4):
            if i:
                yield
            lax.fori_loop(2 * i, 2 * i + 2, rows, 0)

    def mixed_part():
        def columns(i):
            at = pl.ds(i * 512, 512)
            u = jnp.dot(p[hid : hid + 512, :FFB], w1[0, 256:, at], preferred_element_type=f32)
            u = u + jnp.dot(p[hid + 512 : hid + 1024, :FFB], w1[1, 256:, at], preferred_element_type=f32)
            m_part[:, at] = u.astype(bf)

        for i in range(4):
            columns(i)
            yield
        save(20, m_part, m_out)
        for b in range(2):
            branches_turned[b] = branches[b].T
        lanes["d"].flush()
        for i in range(4):
            if i:
                yield
            at = pl.ds(i * 512, 512)
            for b in range(2):
                w1[b, 256:, at] = jnp.dot(turned[2, b], g[:, at], preferred_element_type=f32).astype(bf)
        save(21, w1.at[:, pl.ds(256, FFB), :], od_grad.at[:, pl.ds(256, FFB), :])

    def outer_out():
        lanes["o"].flush()

        def columns(i, _):
            at = pl.ds(pl.multiple_of(i * 512, 512), 512)
            for b in range(2):
                w1[b, :256, at] = jnp.dot(branches_turned[b], da[:, at], preferred_element_type=f32).astype(bf)
            return 0

        lax.fori_loop(0, 4, columns, 0)
        save(22, w1.at[:, pl.ds(0, 256), :], od_grad.at[:, pl.ds(0, 256), :])
        yield
        for sent in swapped_back:
            sent.wait_recv()

    def grads(m):
        def slab(kind):
            return lambda i, j: plane_slab(net, w2, kind, i, j).at[pl.ds(m * FFB, FFB), :]

        yield from reduce_plane(
            lanes["g"], slab(net.c), slab(1 - net.c),
            lambda i, j: sib.at[m, i, j], lambda i: got_half.at[m, i], lambda i: got_up.at[m, i], lambda i: got_down.at[m, i], lambda i: last.at[m, i],
            cut_at(FF_CUT, FFB), add_in(FF_CUT, FFB), net.along(True), net.along(False),
        )

    run(
        {
            "t": main(), "z": tail(), "w": weights(), "o": plane(lanes["o"], own[3:4], w1, 0, OUT // 2, OUT),
            "d": plane(lanes["d"], own[4:5], w1, OUT, FF_CUT, FFB), "u": plane(lanes["u"], own[5:7], w2, 0, GU_CUT, GU),
            "c": cotangent(), "h": hidden_grad(), "b": tables(), "m": mixed_part(), "q": outer_out(), "g": grads(0), "i": grads(1),
        },
        FRONT_ORDER,
    )
    gu_grad[...] = plane_slab(net, w2, net.c, 0, 0)[...]
    for saved in saves.values():
        saved.wait()
    net.finish()


def front(*args):
    bf, f32 = jnp.bfloat16, jnp.float32
    slab = (GU, 128)
    kept = (
        ((GROUP, D), bf), ((3, D, 256), bf), ((2, GROUP, 128), bf), ((2, GROUP, 128), bf), ((2, GROUP, 128), bf),
        ((2 * GROUP, 768), bf), ((2, GROUP, 128), f32),
    )
    kept += (((ROWS, D), f32), ((ROWS, D), f32))
    outs = kept + (((GROUP, 256), bf), ((512, D), bf), ((2, OD, D), bf), ((1, D), f32), (slab, bf))
    scratch = (((256, 128), bf),) + kept + (
        ((GROUP, 256), bf), ((2, 512, 256), bf), ((2, 256, 512), bf), ((2, OD, D), bf), ((2, GU, D), bf), ((512, D), bf), ((512, D), bf),
        ((2, 512, FFB), bf), ((3, 2, FFB, 512), bf), ((512, D), bf), ((2, 512, 256), bf), ((2, 64, D), bf), ((6, 64, D), bf),
        ((2, 4, 4, FFB, 128), bf), ((2, 4, FFB, 128), bf), ((2, 4, FFB, 128), bf), ((2, 4, FFB, 128), bf), ((2, 3, FFB, 128), bf),
    )
    return pl.pallas_call(
        front_kernel,
        name="front",
        out_shape=tuple(jax.ShapeDtypeStruct(*s) for s in outs),
        in_specs=[VMEM, VMEM, pl.BlockSpec(memory_space=pltpu.SMEM), VMEM, VMEM, VMEM, ANY, ANY, ANY, VMEM, ANY, ANY, ANY],
        out_specs=(ANY,) * 12 + (VMEM, VMEM),
        scratch_shapes=[pltpu.VMEM(*s) for s in scratch] + sems(272, 25),
        compiler_params=params(1, 64),
    )(*args)


def back_kernel(do_in, n1_in, w_in, q_in, k_in, v_in, p_in, table_in, m_in, od_in, tok_in, h1_in, dh1_in, gain, mlp_gain_part,
                    mixed, dx, gains, qkv_grad, od_grad,
                    tok, h1, dh1, do, n1, w, q, k, v, p, table, dqkv, dqkv_turned, dk, dv, part, sums, got, sums_half, got_half,
                    ga, sib, slab_half, slab_up, slab_down, slab_last, sum_z, sum_x, sum_y, sum_c,
                    m_part, sums_m, got_m, od, od_sib, od_half, od_up, od_down, od_last,
                    send_sems, recv_sems, local):
    net = Net(send_sems, recv_sems)
    bf, f32 = jnp.bfloat16, jnp.float32
    line_x = [net.device(dx=s) for s in (1, 2, 3)]
    line_y = [net.device(dy=s) for s in (1, 2, 3)]
    line_z = [net.device(dz=s) for s in (1, 2, 3)]
    net.greet(line_x + line_y + line_z + [net.device(dc=1)])
    loads = start(
        [
            pltpu.make_async_copy(src, dst, local.at[m])
            for m, (src, dst) in enumerate(
                (
                    (m_in, m_part), (do_in, do), (v_in, v), (p_in, p), (q_in, q), (k_in, k), (table_in, table), (w_in, w), (n1_in, n1),
                    (h1_in, h1), (tok_in, tok), (dh1_in, dh1),
                )
            )
        ]
    )
    slabs = start(
        [
            pltpu.make_async_copy(plane_slab(net, od_in, net.c, i, j), od.at[i, j], local.at[12 + n])
            for n, (i, j) in enumerate((i, j) for j in (2, 1, 3, 0) for i in (2, 3, 1, 0))
        ]
    )
    net.met()

    def attend_back(h, b):
        rows = slice(b * QROWS, b * QROWS + QROWS)
        first, until = max(0, b - 2) * QROWS, (b + 1) * QROWS
        keys, old = slice(first, until), slice(first, b * QROWS)
        weights_b = p[(h * 4 + b) * QROWS : (h * 4 + b + 1) * QROWS, 0 : until - first]
        do_b = do[rows, h * 128 : h * 128 + 128]
        dp = lax.dot_general(do_b, v[h, keys, :], NT, preferred_element_type=f32)
        wide = weights_b.astype(f32)
        centre = jnp.sum(wide * dp, axis=-1, keepdims=True)
        ds = (wide * (dp - centre)).astype(bf)
        dvb = lax.dot_general(weights_b, do_b, TN, preferred_element_type=f32)
        dkb = lax.dot_general(ds, q[h, rows, :], TN, preferred_element_type=f32)
        if b > 0:
            dv[h, old, :] += dvb[: b * QROWS - first]
            dk[h, old, :] += dkb[: b * QROWS - first]
        dv[h, rows, :] = dvb[b * QROWS - first :]
        dk[h, rows, :] = dkb[b * QROWS - first :]
        dqb = jnp.dot(ds, k[h, keys, :], preferred_element_type=f32) * HEAD_DIM ** (-0.5)
        dqb = dqb * table[0, rows, :] - pltpu.roll(dqb, 64, 1) * table[1, rows, :]
        dqkv[rows, h * 128 : h * 128 + 128] = dqb.astype(bf)

    def turn(i, _):
        here = pl.ds(pl.multiple_of(i * QROWS, QROWS), QROWS)
        for h in range(2):
            u = dk[h, here, :] * HEAD_DIM ** (-0.5)
            u = u * table[0, here, :] - pltpu.roll(u, 64, 1) * table[1, here, :]
            dqkv[here, 256 + h * 128 : 384 + h * 128] = u.astype(bf)
            dqkv[here, 512 + h * 128 : 640 + h * 128] = dv[h, here, :].astype(bf)
        dqkv_turned[:, here] = dqkv[here, :].T
        return 0

    def make(xl, z):
        here = block8(xl, z)
        left = dqkv[here, :]

        def columns(i, _):
            at = pl.ds(pl.multiple_of(i * 512, 512), 512)
            u = lax.dot_general(left[:, :256], w[0, at, :], NT, preferred_element_type=f32)
            u = u + lax.dot_general(left[:, 256:512], w[1, at, :], NT, preferred_element_type=f32)
            u = u + lax.dot_general(left[:, 512:], w[2, at, :], NT, preferred_element_type=f32)
            part[here, at] = u.astype(bf)
            sum_y[net.y, 0:1, at] += jnp.sum(u * n1[here, at].astype(f32), axis=0, keepdims=True)
            return 0

        lax.fori_loop(0, 4, columns, 0)

    out = []

    def step(at, k):
        here = pl.ds(at, 16)
        value = tok[here, :].astype(f32)
        r = lax.rsqrt(jnp.mean(value * value, axis=-1, keepdims=True) + EPS)
        inner = out[0](at, k) * gain[...]
        dx[here, :] = dh1[here, :] + r * inner - value * (r * r * r) * jnp.mean(value * inner, axis=-1, keepdims=True)

    def main():
        for copied in loads[1:7]:
            copied.wait()
        yield
        for b in range(GROUP // QROWS):
            for h in range(2):
                attend_back(h, b)
            yield
        lax.fori_loop(0, GROUP // QROWS, turn, 0)
        for copied in loads[7:9]:
            copied.wait()
        sum_y[net.y, 0:1, :] = jnp.zeros((1, D), f32)
        sum_y[net.y, 1:2, :] = mlp_gain_part[...]
        yield
        yield from reduce_8(net, make, part, sums, got, sums_half, got_half, out)
        for copied in loads[10:]:
            copied.wait()
        each_half(step)

    def early():
        chain = reduce_plane(
            net, lambda i, j: od.at[i, j], lambda i, j: plane_slab(net, od_in, 1 - net.c, i, j), lambda i, j: od_sib.at[i, j],
            lambda i: od_half.at[i], lambda i: od_up.at[i], lambda i: od_down.at[i], lambda i: od_last.at[i],
            cut_at(OD_CUT, OD), add_in(OD_CUT, OD), net.along(True), net.along(False),
        )
        forward(chain)
        yield
        for copied in slabs:
            copied.wait()
        yield from chain
        od_grad[...] = od[0, 0]

    def mixing():
        loads[0].wait()
        yield from reduce_z(net, m_part, sums_m, got_m)

        def mix(at, k):
            here = pl.ds(at, 16)
            mixed[here, :] = (h1[here, :] + reduced(net, m_part, got_m, at, k)).astype(bf)

        loads[9].wait()
        each_half(mix)

    def slab(kind):
        return lambda i, j: ga.at[:, att_at(net, kind, i, j)]

    def weights():
        for i in range(4):
            at = pl.ds(i * 512, 512)
            ga[:, at] = jnp.dot(dqkv_turned[...], n1[:, at], preferred_element_type=f32).astype(bf)
            yield
        yield from reduce_plane(
            net, slab(net.c), slab(1 - net.c), lambda i, j: sib.at[i, j], lambda i: slab_half.at[i], lambda i: slab_up.at[i],
            lambda i: slab_down.at[i], lambda i: slab_last.at[i], cut_at(QKV_CUT, QKV), add_in(QKV_CUT, QKV), (net.across,), (net.device(dy=1), net.device(dy=-1)),
        )
        qkv_grad[...] = slab(net.c)(0, 0)[...]

    def gain_sums():
        here = net.y
        stages = ((sum_y, line_y, sum_c, net.c), (sum_c, [net.device(dc=1)], sum_x, net.x), (sum_x, line_x, sum_z, net.z), (sum_z, line_z, None, None))
        for ref, line, then, place in stages:
            sent = [net.send(ref.at[here], ref.at[here], to) for to in line]
            yield
            for copied in sent:
                copied.wait_recv()
            total = ref[0]
            for n in range(1, len(line) + 1):
                total = total + ref[n]
            if then is None:
                gains[0:1, :] = total[0:1] / gain[...]
                gains[1:2, :] = total[1:2]
            else:
                then[place] = total
                here = place

    run({"t": main(), "m": mixing(), "e": early(), "w": weights(), "s": gain_sums()}, BACK_ORDER)
    net.finish()


def back(do, n1, w, q, k, v, p, table, m, od, tok, h1, dh1, gain, mlp_gain_part):
    bf, f32 = jnp.bfloat16, jnp.float32
    slab, slab_od = (QKV, 128), (OD, 128)
    scratch = [
        ((ROWS, D), bf), ((ROWS, D), f32), ((ROWS, D), f32),
        ((GROUP, 256), bf), ((GROUP, D), bf), ((3, D, 256), bf), ((2, GROUP, 128), bf), ((2, GROUP, 128), bf), ((2, GROUP, 128), bf),
        ((2 * GROUP, 768), bf), ((2, GROUP, 128), f32), ((GROUP, QKV), bf), ((QKV, GROUP), bf),
        ((2, GROUP, 128), f32), ((2, GROUP, 128), f32), ((GROUP, D), bf), ((2, ROWS, D), bf), ((4, ROWS, D), bf),
        ((2, 64, D), bf), ((6, 64, D), bf), ((QKV, D), bf), ((2, 4) + slab, bf), ((2,) + slab, bf), ((2,) + slab, bf),
        ((2,) + slab, bf), ((1,) + slab, bf), ((4, 2, D), f32), ((4, 2, D), f32), ((4, 2, D), f32), ((2, 2, D), f32),
        ((512, D), bf), ((2, 64, D), bf), ((6, 64, D), bf), ((4, 4) + slab_od, bf), ((4, 4) + slab_od, bf),
        ((4,) + slab_od, bf), ((4,) + slab_od, bf), ((4,) + slab_od, bf), ((3,) + slab_od, bf),
    ]
    outs = (((ROWS, D), bf), ((ROWS, D), f32), ((2, D), f32), (slab, bf), (slab_od, bf))
    return pl.pallas_call(
        back_kernel,
        name="back",
        out_shape=tuple(jax.ShapeDtypeStruct(*s) for s in outs),
        in_specs=[ANY] * 13 + [VMEM] * 2,
        out_specs=(VMEM,) * 5,
        scratch_shapes=[pltpu.VMEM(*s) for s in scratch] + sems(128, 28),
        compiler_params=params(2),
    )(do, n1, w, q, k, v, p, table, m, od, tok, h1, dh1, gain, mlp_gain_part)


def finish_kernel(mixed_in, dx_in, gains_in, qkv_in, od_in, gu_in, mixed, dx, ag, gq, gk, gv, go, mg, gg, gu_out, gd, gains, qkv, od, gu, sems):
    f32 = jnp.float32
    pairs = ((gu_in, gu), (od_in, od), (qkv_in, qkv), (gains_in, gains), (mixed_in, mixed), (dx_in, dx))
    loads = start([pltpu.make_async_copy(src, dst, sems.at[n]) for n, (src, dst) in enumerate(pairs)])
    for load in loads[:4]:
        load.wait()
    gg[...] = gu[:FFB, :].astype(f32)
    gu_out[...] = gu[FFB:, :].astype(f32)
    go[...] = od[:256, :].astype(f32).T
    gd[...] = od[256:, :].astype(f32)
    for n, dst in enumerate((gq, gk, gv)):
        dst[...] = qkv[n * 256 : n * 256 + 256, :].astype(f32).T
    ag[...] = gains[0:1, :]
    mg[...] = gains[1:2, :]
    for load in loads[4:]:
        load.wait()


def finish(mixed, dx, gains, qkv, od, gu):
    f32, bf = jnp.float32, jnp.bfloat16
    outs = (
        ((ROWS, D), bf), ((ROWS, D), f32), ((1, D), f32), ((ROWS, 256), f32), ((ROWS, 256), f32), ((ROWS, 256), f32),
        ((ROWS, 256), f32), ((1, D), f32), ((FFB, 128), f32), ((FFB, 128), f32), ((FFB, 128), f32),
    )
    held = (((2, D), f32), ((QKV, 128), bf), ((OD, 128), bf), ((GU, 128), bf))
    return pl.pallas_call(
        finish_kernel,
        name="finish",
        out_shape=tuple(jax.ShapeDtypeStruct(*s) for s in outs),
        in_specs=[ANY] * 6,
        out_specs=(VMEM,) * 11,
        scratch_shapes=[pltpu.VMEM(*s) for s in held] + [pltpu.SemaphoreType.DMA((6,))],
        compiler_params=pltpu.CompilerParams(vmem_limit_bytes=60 << 20),
    )(mixed, dx, gains, qkv, od, gu)


def shards(
    tokens,
    lengths,
    attn_gain,
    query_weight,
    key_weight,
    value_weight,
    out_weight,
    mlp_gain,
    gate_weight,
    up_weight,
    down_weight,
    cotangent,
):
    half_rates = THETA ** (-(np.arange(64, dtype=np.float32) * np.float32(2.0 / HEAD_DIM)))
    rates = jnp.asarray(np.concatenate([half_rates, half_rates])[None].astype(np.float32))
    n1, w, q, k, v, p, table, h1, dh1, do, m, od_part, gain_part, gu = front(
        tokens, cotangent, lengths, attn_gain[None], mlp_gain[None], rates, query_weight, key_weight, value_weight, out_weight,
        gate_weight.T, up_weight.T, down_weight.T,
    )
    mixed, dx, gains, qkv, od_grad = back(do, n1, w, q, k, v, p, table, m, od_part, tokens, h1, dh1, attn_gain[None], gain_part)
    mixed, dx, ag, gq, gk, gv, go, mg, gg, gu, gd = finish(mixed, dx, gains, qkv, od_grad, gu)
    return (mixed, dx, ag[0], gq, gk, gv, go, mg[0], gg.T, gu.T, gd.T)


def solution(mesh):
    return jax.shard_map(
        shards,
        mesh=mesh,
        in_specs=(
            P(("dp", "tensor"), None),
            P("dp", None),
            P(),
            P("dp", "tensor"),
            P("dp", "tensor"),
            P("dp", "tensor"),
            P("dp", "tensor"),
            P(),
            P("dp", "tensor"),
            P("dp", "tensor"),
            P("dp", "tensor"),
            P(("dp", "tensor"), None),
        ),
        out_specs=(
            P(("dp", "tensor"), None),
            P(("dp", "tensor"), None),
            P(),
            P("dp", "tensor"),
            P("dp", "tensor"),
            P("dp", "tensor"),
            P("dp", "tensor"),
            P(),
            P("dp", "tensor"),
            P("dp", "tensor"),
            P("dp", "tensor"),
        ),
        check_vma=False,
    )
```
